32 devices in a mesh: ctx: 4 (over y, x), tile: 8 (over z, core).
Axes of the slice: x: 2, y: 2, z: 4, core: 2. Of those that a mesh axis runs over, the one named last changes fastest.
Arguments:
- syndrome_bits: int32 [8, 2, 32, 256], P(None, None, 'ctx', 'tile'), may hold values from 0 to 1
- region_assign: int32 [16, 128], P('ctx', 'tile'), may hold values from 0 to 127
- state_in: bfloat16 [32, 256, 512], P('ctx', 'tile'), may hold values from -3 to 3
- bit_to_candidate: float32 [2, 512], replicated, may hold values from -5 to 5
- bit_to_gate: float32 [2, 512], replicated, may hold values from -5 to 5
- conv_weight: bfloat16 [9, 512, 512], replicated, may hold values from -0.09375 to 0.09375
- gate_weight: bfloat16 [512, 512], replicated, may hold values from -0.25 to 0.25
- gate_bias: float32 [512], replicated, may hold values from -4 to 1
- pool_weight: bfloat16 [512, 1024], replicated, may hold values from -0.25 to 0.25
- region_embed: bfloat16 [512, 1024], P('ctx'), may hold values from -6 to 6
- attn_norm_gain: float32 [1024], replicated, may hold values from 0.1 to 1.9
- query_weight: bfloat16 [1024, 1024], replicated
- key_weight: bfloat16 [1024, 1024], replicated
- value_weight: bfloat16 [1024, 1024], replicated, may hold values from -0.1875 to 0.1875
- out_weight: bfloat16 [1024, 1024], replicated, may hold values from -0.1875 to 0.1875
- mlp_norm_gain: float32 [1024], replicated, may hold values from 0.1 to 1.9
- mlp_up: bfloat16 [1024, 2048], replicated, may hold values from -0.1875 to 0.1875
- mlp_down: bfloat16 [2048, 1024], replicated, may hold values from -0.125 to 0.125
- return_weight: bfloat16 [1024, 512], replicated, may hold values from -0.1875 to 0.1875
Outputs:
- state_out: bfloat16 [32, 256, 512], P('ctx', 'tile')
- context_out: bfloat16 [512, 1024], P('ctx')
The draws below stay inside these ranges and needn't reach their ends.
All inputs are finite; a program needn't handle non-finite values.
Results may differ from the reference program's by a relative error of at most 0.02.
Values may be sent and summed in bfloat16 or wider, within the bound.
No kernel may reach another device: no remote copies, remote signals or barrier semaphores. Data moves between devices by JAX's collectives and lax.ppermute only.
A program may use at most 128 MiB of HBM per device.

```python
import math
import jax
import jax.numpy as jnp
from jax import lax

C = 512
E = 1024
HEADS = 8
HDIM = 128
MLP = 2048
ROUNDS = 8
PR = 8
REG_DEV = 128
NR = 32
NC = 256
REGIONS = 512


def shared_query(key):
    return jax.random.normal(jax.random.fold_in(key, 11), (E, E), jnp.float32) * E ** (-0.5)


def draw_query_weight(key, part):
    return shared_query(key).astype(jnp.bfloat16)


def draw_key_weight(key, part):
    fresh = jax.random.normal(jax.random.fold_in(key, 13), (E, E), jnp.float32) * E ** (-0.5)
    return fresh.astype(jnp.bfloat16)


def with_ends(values, rng, smallest, top_value):
    spot = [jax.random.randint(jax.random.fold_in(rng, axis), (), 0, length) for axis, length in enumerate(values.shape)]
    longest = values.shape.index(max(values.shape))
    next_to = spot[:longest] + [(spot[longest] + 1) % values.shape[longest]] + spot[longest + 1:]
    return values.at[tuple(spot)].set(smallest).at[tuple(next_to)].set(top_value)


def levels(stream_key, extent, split, least, top_value):
    def one(position, shards_of):
        draws = jax.random.uniform(jax.random.fold_in(jax.random.fold_in(stream_key, 6), position), (shards_of,), jnp.float32, least / len(split), top_value / len(split))
        return jnp.repeat(jnp.exp(draws), extent[position] // shards_of).reshape((-1,) + (1,) * (len(extent) - position - 1))

    level = one(*split[0])
    for cut in split[1:]:
        level = level * one(*cut)
    return level


def noise(key, shape, spread, most, pieces=(), held_as=jnp.bfloat16):
    drawn = jax.random.normal(key, shape, jnp.float32) * spread
    if len(pieces) > 0:
        drawn = levels(key, shape, pieces, -0.22, 0.18) * drawn
    return jnp.clip(drawn, min=-most, max=most).astype(held_as)


def setup_inputs(seed: int = 0) -> dict:
    key_of = jax.random.split(jax.random.key(seed), 20)
    syndrome_bits = with_ends(jax.random.randint(key_of[0], (ROUNDS, 2, NR, NC), 0, 2), jax.random.fold_in(key_of[0], 1), 0, 1).astype(jnp.int32)
    region_assign = with_ends(jax.random.randint(key_of[1], (NR // 2, NC // 2), 0, REG_DEV), jax.random.fold_in(key_of[1], 1), 0, REG_DEV - 1).astype(jnp.int32)
    state_in = noise(key_of[2], (NR, NC, C), 0.5, 3.0, ((0, 4), (1, 8)))
    bit_to_candidate = noise(key_of[3], (2, C), 1.0, 5.0, (), jnp.float32)
    bit_to_gate = noise(key_of[4], (2, C), 1.0, 5.0, (), jnp.float32)
    conv_weight = noise(key_of[5], (9, C, C), (9 * C) ** -0.5, 0.09375)
    gate_weight = noise(key_of[6], (C, C), C ** -0.5, 0.25)
    gate_bias = jnp.clip(jax.random.uniform(key_of[7], (C,), jnp.float32, -4.0, 1.0), -4.0, 1.0)
    pool_weight = noise(key_of[8], (C, E), C ** -0.5, 0.25)
    region_embed = noise(key_of[9], (REGIONS, E), 1.0, 6.0, ((0, 4),))
    attn_norm_gain = jnp.clip(1.0 + 0.18 * jax.random.normal(key_of[10], (E,), jnp.float32), 0.1, 1.9)
    query_weight = draw_query_weight(jax.random.fold_in(key_of[19], 71), 0)
    key_weight = draw_key_weight(jax.random.fold_in(key_of[19], 71), 0)
    value_weight = noise(key_of[13], (E, E), E ** -0.5, 0.1875)
    out_weight = noise(key_of[14], (E, E), E ** -0.5, 0.1875)
    mlp_norm_gain = jnp.clip(1.0 + 0.18 * jax.random.normal(key_of[15], (E,), jnp.float32), 0.1, 1.9)
    mlp_up = noise(key_of[16], (E, MLP), E ** -0.5, 0.1875)
    mlp_down = noise(key_of[17], (MLP, E), MLP ** -0.5, 0.125)
    return_weight = noise(key_of[18], (E, C), E ** -0.5, 0.1875)
    return dict(syndrome_bits=syndrome_bits, region_assign=region_assign, state_in=state_in, bit_to_candidate=bit_to_candidate, bit_to_gate=bit_to_gate, conv_weight=conv_weight, gate_weight=gate_weight, gate_bias=gate_bias, pool_weight=pool_weight, region_embed=region_embed, attn_norm_gain=attn_norm_gain, query_weight=query_weight, key_weight=key_weight, value_weight=value_weight, out_weight=out_weight, mlp_norm_gain=mlp_norm_gain, mlp_up=mlp_up, mlp_down=mlp_down, return_weight=return_weight)


def product(left, right):
    return jnp.dot(left.astype(jnp.float32), right.astype(jnp.float32), precision=lax.Precision.HIGHEST)

def rms_norm(values, gain):
    return values * lax.rsqrt(lax.optimization_barrier(jnp.mean(values * values, axis=-1, keepdims=True)) + 1e-05) * gain

def advance(state, syndrome_now, conv_weight, gate_weight, gate_bias, bit_to_candidate, bit_to_gate):
    patch_rows, patch_cols, channels = state.shape
    rounded = state.astype(jnp.bfloat16)
    padded = jnp.pad(rounded, ((1, 1), (1, 1), (0, 0)))
    columns = jnp.concatenate([padded[offset_row:offset_row + patch_rows, offset_col:offset_col + patch_cols] for offset_row in range(3) for offset_col in range(3)], axis=-1)
    syndrome_flags = syndrome_now.astype(jnp.float32)
    drive_cand = syndrome_flags[0][..., None] * bit_to_candidate[0] + syndrome_flags[1][..., None] * bit_to_candidate[1]
    drive_gate = syndrome_flags[0][..., None] * bit_to_gate[0] + syndrome_flags[1][..., None] * bit_to_gate[1]
    candidate = product(columns.reshape(patch_rows * patch_cols, 9 * channels), conv_weight.reshape(9 * channels, channels)).reshape(patch_rows, patch_cols, channels) + drive_cand
    update_gate = jax.nn.sigmoid(product(rounded.reshape(patch_rows * patch_cols, channels), gate_weight).reshape(patch_rows, patch_cols, channels) + drive_gate + gate_bias)
    return state + update_gate * (jnp.tanh(candidate) - state)

def reference(syndrome_bits, region_assign, state_in, bit_to_candidate, bit_to_gate, conv_weight, gate_weight, gate_bias, pool_weight, region_embed, attn_norm_gain, query_weight, key_weight, value_weight, out_weight, mlp_norm_gain, mlp_up, mlp_down, return_weight):
    state = state_in.astype(jnp.float32)
    patch_rows, patch_cols, channels = state.shape
    context_out = None
    for round_index in range(ROUNDS):
        if round_index == ROUNDS // 2:
            pooled = state.reshape(patch_rows // 2, 2, patch_cols // 2, 2, channels).mean(axis=(1, 3)).astype(jnp.bfloat16)
            projected = product(pooled.reshape(-1, channels), pool_weight)
            band = (jnp.arange(patch_rows // 2, dtype=jnp.int32) // (PR // 2))[:, None]
            token_index = (band * REG_DEV + region_assign).astype(jnp.int32).reshape(-1)
            tokens = region_embed.astype(jnp.float32) + jax.ops.segment_sum(projected, token_index, num_segments=REGIONS)
            token_count = tokens.shape[0]
            normed = rms_norm(tokens, attn_norm_gain).astype(jnp.bfloat16)
            queries = product(normed, query_weight).astype(jnp.bfloat16)
            key_rows = product(normed, key_weight).astype(jnp.bfloat16)
            value_rows = product(normed, value_weight).astype(jnp.bfloat16)
            query_heads = queries.astype(jnp.float32).reshape(token_count, HEADS, HDIM).transpose(1, 0, 2)
            key_heads = key_rows.astype(jnp.float32).reshape(token_count, HEADS, HDIM).transpose(1, 0, 2)
            value_heads = value_rows.astype(jnp.float32).reshape(token_count, HEADS, HDIM).transpose(1, 0, 2)
            scores = jnp.einsum('hqd,hkd->hqk', query_heads, key_heads, precision=lax.Precision.HIGHEST) / math.sqrt(HDIM)
            running_max = lax.optimization_barrier(jnp.max(scores, axis=-1, keepdims=True))
            weights = jnp.exp(scores - running_max)
            denominator = lax.optimization_barrier(jnp.sum(weights, axis=-1))
            weights_low = lax.optimization_barrier(weights.astype(jnp.bfloat16)).astype(jnp.float32)
            weighted = jnp.einsum('hqk,hkd->hqd', weights_low, value_heads, precision=lax.Precision.HIGHEST) / denominator[..., None]
            attention = weighted.transpose(1, 0, 2).reshape(token_count, HEADS * HDIM).astype(jnp.bfloat16)
            attended = tokens + product(attention, out_weight)
            hidden = jax.nn.gelu(product(rms_norm(attended, mlp_norm_gain).astype(jnp.bfloat16), mlp_up)).astype(jnp.bfloat16)
            context_out = (attended + product(hidden, mlp_down)).astype(jnp.bfloat16)
            returned = product(context_out, return_weight)
            share_back = returned[token_index].reshape(patch_rows // 2, patch_cols // 2, channels)
            state = (state.reshape(patch_rows // 2, 2, patch_cols // 2, 2, channels) + share_back[:, None, :, None, :]).reshape(patch_rows, patch_cols, channels)
        state = advance(state, syndrome_bits[round_index], conv_weight, gate_weight, gate_bias, bit_to_candidate, bit_to_gate)
    return (state.astype(jnp.bfloat16), context_out)
```

```python
import math

import jax
import jax.numpy as jnp
from jax import lax
from jax.sharding import PartitionSpec as P

HEADS = 8
HDIM = 128
ROUNDS = 8
HALF = ROUNDS // 2
F32 = jnp.float32
BF16 = jnp.bfloat16


def shifted(value, axis, step):
    size = lax.axis_size(axis)
    pairs = [(i, i + step) for i in range(size) if 0 <= i + step < size]
    return lax.ppermute(value, axis, pairs)


def with_halo(value, width):
    for axis, dim in (("tile", 1), ("ctx", 0)):
        length = value.shape[dim]
        last = lax.slice_in_dim(value, length - width, length, axis=dim)
        first = lax.slice_in_dim(value, 0, width, axis=dim)
        before = shifted(last, axis, 1)
        after = shifted(first, axis, -1)
        value = jnp.concatenate([before, value, after], axis=dim)
    return value


def matmul(left, right):
    return jnp.dot(left, right, preferred_element_type=F32)


def select(member, values):
    high = values.astype(BF16)
    low = (values - high.astype(F32)).astype(BF16)
    return matmul(member, high) + matmul(member, low)


def rms_norm(values, gain):
    return values * lax.rsqrt(jnp.mean(values * values, axis=-1, keepdims=True) + 1e-05) * gain


def rounds(state, flags, inside, first_round, conv_flat, gate_weight, gate_bias, bit_to_candidate, bit_to_gate):
    for step in range(HALF):
        t = first_round + step
        rounded = jnp.where(inside[..., None], state, 0.0).astype(BF16)
        rows, cols, channels = state.shape
        rows, cols = rows - 2, cols - 2
        columns = jnp.concatenate(
            [rounded[a : a + rows, b : b + cols] for a in range(3) for b in range(3)], axis=-1
        )
        flags, inside, state = flags[1:-1, 1:-1], inside[1:-1, 1:-1], state[1:-1, 1:-1]
        bit0, bit1 = flags[..., 2 * t, None], flags[..., 2 * t + 1, None]
        candidate = (
            matmul(columns.reshape(rows * cols, 9 * channels), conv_flat).reshape(rows, cols, channels)
            + bit0 * bit_to_candidate[0]
            + bit1 * bit_to_candidate[1]
        )
        gate = (
            matmul(rounded[1:-1, 1:-1].reshape(rows * cols, channels), gate_weight).reshape(rows, cols, channels)
            + bit0 * bit_to_gate[0]
            + bit1 * bit_to_gate[1]
            + gate_bias
        )
        state = state + jax.nn.sigmoid(gate) * (jnp.tanh(candidate) - state)
    return state


def local(
    syndrome_bits, region_assign, state_in, bit_to_candidate, bit_to_gate, conv_weight, gate_weight, gate_bias,
    pool_weight, region_embed, attn_norm_gain, query_weight, key_weight, value_weight, out_weight, mlp_norm_gain,
    mlp_up, mlp_down, return_weight,
):
    patch_rows, patch_cols, channels = state_in.shape
    band_tokens = region_embed.shape[0]
    bands, tiles = lax.axis_size("ctx"), lax.axis_size("tile")
    g, tile = lax.axis_index("ctx"), lax.axis_index("tile")
    width = HALF
    conv_flat = conv_weight.reshape(9 * channels, channels)
    round_weights = (conv_flat, gate_weight, gate_bias, bit_to_candidate, bit_to_gate)

    bits = syndrome_bits.transpose(2, 3, 0, 1).reshape(patch_rows, patch_cols, 2 * ROUNDS).astype(BF16)
    assign_cells = jnp.repeat(jnp.repeat(region_assign, 2, axis=0), 2, axis=1).astype(BF16)[..., None]
    spare = jnp.zeros((patch_rows, patch_cols, 128 - 2 * ROUNDS - 1), BF16)
    extended = with_halo(jnp.concatenate([state_in, bits, assign_cells, spare], axis=-1), width)
    embed_all = lax.all_gather(region_embed, "ctx", axis=0, tiled=True)
    band_assign = lax.all_gather(region_assign.reshape(1, -1), "tile", axis=0, tiled=True)

    flags = extended[..., channels : channels + 2 * ROUNDS].astype(F32)
    assign_ext = extended[::2, ::2, channels + 2 * ROUNDS].astype(jnp.int32)
    row = jnp.arange(patch_rows + 2 * width)[:, None] + g * patch_rows - width
    col = jnp.arange(patch_cols + 2 * width)[None, :] + tile * patch_cols - width
    inside = (row >= 0) & (row < bands * patch_rows) & (col >= 0) & (col < tiles * patch_cols)

    state = rounds(extended[..., :channels].astype(F32), flags, inside, 0, *round_weights)

    outer = with_halo(state.astype(BF16), width).astype(F32)
    outer = lax.dynamic_update_slice(outer, state, (width, width, 0))

    pooled = state.reshape(patch_rows // 2, 2, patch_cols // 2, 2, channels).mean(axis=(1, 3)).astype(BF16)
    pooled = pooled.reshape(-1, channels)
    spread = lax.all_to_all(jnp.broadcast_to(pooled[None], (tiles,) + pooled.shape), "tile", 0, 0)
    member = (band_assign.reshape(1, -1) == jnp.arange(band_tokens, dtype=jnp.int32)[:, None]).astype(BF16)
    sums = matmul(member, spread.reshape(-1, channels)).astype(BF16)
    sums_all = lax.all_gather(sums, "ctx", axis=0, tiled=True)

    tokens_all = embed_all.astype(F32) + matmul(sums_all, pool_weight)
    normed_all = rms_norm(tokens_all, attn_norm_gain).astype(BF16)
    keys = matmul(normed_all, key_weight).astype(BF16)
    values = matmul(normed_all, value_weight).astype(BF16)

    half_width = width // 2
    above = (g - 1) * band_tokens + assign_ext[:half_width].reshape(-1)
    below = (g + 1) * band_tokens + assign_ext[-half_width:].reshape(-1)
    own = g * band_tokens + jnp.arange(band_tokens, dtype=jnp.int32)
    chosen = jnp.concatenate([own, above, below])
    pick = (chosen[:, None] == jnp.arange(bands * band_tokens, dtype=jnp.int32)).astype(BF16)
    tokens = select(pick, tokens_all)
    normed = matmul(pick, normed_all).astype(BF16)
    queries = matmul(normed, query_weight).astype(BF16)
    count = tokens.shape[0]
    scores = jnp.einsum(
        "qhd,khd->hqk", queries.reshape(count, HEADS, HDIM), keys.reshape(-1, HEADS, HDIM), preferred_element_type=F32
    ) * (1.0 / math.sqrt(HDIM))
    weights = jnp.exp(scores - jnp.max(scores, axis=-1, keepdims=True))
    denominator = jnp.sum(weights, axis=-1)
    weighted = jnp.einsum(
        "hqk,khd->hqd", weights.astype(BF16), values.reshape(-1, HEADS, HDIM), preferred_element_type=F32
    ) / denominator[..., None]
    attention = weighted.transpose(1, 0, 2).reshape(count, HEADS * HDIM).astype(BF16)
    attended = tokens + matmul(attention, out_weight)
    hidden = jax.nn.gelu(matmul(rms_norm(attended, mlp_norm_gain).astype(BF16), mlp_up)).astype(BF16)
    context = (attended + matmul(hidden, mlp_down)).astype(BF16)
    returned = matmul(context, return_weight)

    middle = assign_ext[half_width:-half_width].reshape(-1)
    back = (middle[:, None] == jnp.arange(band_tokens, dtype=jnp.int32)).astype(BF16)
    share_middle = select(back, returned[:band_tokens])
    share_above, share_below = jnp.split(returned[band_tokens:], 2)
    share = jnp.concatenate([share_above, share_middle, share_below]).reshape(assign_ext.shape + (channels,))
    block_rows, block_cols = assign_ext.shape
    state = (
        outer.reshape(block_rows, 2, block_cols, 2, channels) + share[:, None, :, None, :]
    ).reshape(outer.shape)
    state = rounds(state, flags, inside, HALF, *round_weights)
    return (state.astype(BF16), context[:band_tokens])


def solution(mesh):
    return jax.shard_map(
        local,
        mesh=mesh,
        in_specs=(
            P(None, None, "ctx", "tile"),
            P("ctx", "tile"),
            P("ctx", "tile", None),
            P(), P(), P(), P(), P(), P(),
            P("ctx", None),
            P(), P(), P(), P(), P(), P(), P(), P(), P(),
        ),
        out_specs=(P("ctx", "tile", None), P("ctx", None)),
        check_vma=False,
    )
```

```python
import functools
import math

import jax
import jax.numpy as jnp
from jax import lax
from jax.experimental import pallas as pl
from jax.experimental.pallas import tpu as pltpu
from jax.sharding import PartitionSpec as P

HEADS = 8
HDIM = 128
ROUNDS = 8
HALF = ROUNDS // 2
LANES = 128
F32 = jnp.float32
BF16 = jnp.bfloat16

REGION_LANE, LOW_LANE, ONE_LANE = 2 * ROUNDS, 32, 64


def shifted(value, axis, step):
    size = lax.axis_size(axis)
    pairs = [(i, i + step) for i in range(size) if 0 <= i + step < size]
    return lax.ppermute(value, axis, pairs)


def to_all(pieces, axis):
    return lax.all_to_all(pieces, axis, 0, 0)


def matmul(left, right):
    return jnp.dot(left, right, preferred_element_type=F32)


def two_parts(values):
    high = values.astype(BF16)
    return high, (values - high.astype(F32)).astype(BF16)


def select(member, values):
    high, low = two_parts(values)
    return matmul(member, high) + matmul(member, low)


def rms_norm(values, gain):
    return values * lax.rsqrt(jnp.mean(values * values, axis=-1, keepdims=True) + 1e-05) * gain


def row_halo(top, bottom):
    return shifted(bottom, "ctx", 1), shifted(top, "ctx", -1)


def col_halo(above, value, below):
    width = HALF
    left = jnp.concatenate([part[:, :width] for part in (above, value, below)])
    right = jnp.concatenate([part[:, -width:] for part in (above, value, below)])
    return shifted(right, "tile", 1), shifted(left, "tile", -1)


def flat(value):
    return value.reshape(-1, value.shape[-1])


def rounds_kernel(first_round, cols, *refs):
    last = first_round > 0
    center, above, below, left, right, flags, inside, conv, gate_weight, bit_weight, extra = refs[:11]
    outs, (state, taps, bits) = refs[11:-3], refs[-3:]
    width, span = HALF, cols + 2 * HALF
    groups, count = state.shape[:2]
    rows, channels = count // span, groups * LANES

    def get(at):
        return jnp.concatenate([state[j, at] for j in range(groups)], axis=1)

    def put(at, values):
        for j in range(groups):
            state[j, at] = values[:, j * LANES : (j + 1) * LANES]

    for part, first in ((above, 0), (center, width), (below, rows - width)):
        for r in range(part.shape[0] // cols):
            put(pl.ds((first + r) * span + width, cols), part[r * cols : (r + 1) * cols].astype(F32))
    for part, first in ((left, 0), (right, width + cols)):
        values = part[...].astype(F32)
        for r in range(rows):
            put(pl.ds(r * span + first, width), values[r * width : (r + 1) * width])
    if last:
        blocks = span // 2
        for r in range(rows):
            share = extra[r // 2 * blocks : (r // 2 + 1) * blocks]
            for c in range(2):
                at = pl.ds(r * span + c, blocks, stride=2)
                put(at, get(at) + share)

    def keep(slot, first, values):
        size = values.shape[0]
        mask = inside[first : first + size]
        values = jnp.concatenate([values[:, c : c + LANES] * mask for c in range(0, channels, LANES)], axis=1)
        for b in range(3):
            moved = values if b == 1 else pltpu.roll(values, 1 if b == 0 else size - 1, 0)
            taps[slot, first : first + size, b * channels : (b + 1) * channels] = moved.astype(BF16)

    for first in range(0, rows, rows // 2):
        keep(0, first * span, get(pl.ds(first * span, rows // 2 * span)))

    lane = lax.broadcasted_iota(jnp.int32, (1, LANES), 1)
    for step in range(HALF):
        t = first_round + step
        slot = step % 2
        now = (lane == 2 * t) | (lane == 2 * t + 1) | (lane == LOW_LANE + 2 * t) | (lane == LOW_LANE + 2 * t + 1)
        now = now | (lane >= ONE_LANE)
        bits[...] = flags[...] * jnp.where(now, 1.0, 0.0).astype(BF16)
        total = rows - 2 * (step + 1)
        cut = (total // 4 + total // 2 % 2) * 2
        for begin, part_rows in ((step + 1, cut), (step + 1 + cut, total - cut)):
            first, size = begin * span, part_rows * span
            columns = jnp.concatenate(
                [taps[slot, first + a * span : first + a * span + size] for a in (-1, 0, 1)], axis=1
            )
            flag = bits[first : first + size]
            rounded = taps[slot, first : first + size, channels : 2 * channels]
            candidate = matmul(columns, conv[...]) + matmul(flag, bit_weight[:, :channels])
            gate = matmul(rounded, gate_weight[...]) + matmul(flag, bit_weight[:, channels:])
            before = get(pl.ds(first, size))
            after = before + (0.5 * jnp.tanh(0.5 * gate) + 0.5) * (jnp.tanh(candidate) - before)
            put(pl.ds(first, size), after)
            if step < HALF - 1:
                keep(1 - slot, first, after)

    own = rows - 2 * width
    if last:
        for r in range(own):
            values = get(pl.ds((width + r) * span + width, cols))
            outs[0][r * cols : (r + 1) * cols] = values.astype(BF16)
        return
    exact, top, bottom, spread = outs
    for r in range(own):
        values = get(pl.ds((width + r) * span + width, cols))
        exact[r * cols : (r + 1) * cols] = values
        half = (top, bottom)[r // width]
        half[r % width * cols : (r % width + 1) * cols] = values.astype(BF16)
    block_cols = cols // 2
    block_count = own // 2 * block_cols
    piece = block_count + extra.shape[0]
    pooled = []
    for r in range(0, own, 2):
        parts = [
            get(pl.ds((width + r + a) * span + width + b, block_cols, stride=2)) for a in range(2) for b in range(2)
        ]
        pooled.append((sum(parts[1:], parts[0]) * 0.25).astype(BF16))
    pooled = jnp.concatenate(pooled + [extra[...]], axis=0)
    for p in range(spread.shape[0] // piece):
        spread[p * piece : (p + 1) * piece] = pooled


def rounds(first_round, cols, operands, out_shapes):
    center, flags = operands[0], operands[5]
    count, channels = flags.shape[0], center.shape[1]
    cell_rounds = HALF * center.shape[0] * 3 // 2
    return pl.pallas_call(
        functools.partial(rounds_kernel, first_round, cols),
        out_shape=out_shapes,
        scratch_shapes=[
            pltpu.VMEM((channels // LANES, count, LANES), F32),
            pltpu.VMEM((2, count, 3 * channels), BF16),
            pltpu.VMEM((count, LANES), BF16),
        ],
        compiler_params=pltpu.CompilerParams(vmem_limit_bytes=40 * 2**20),
        cost_estimate=pl.CostEstimate(
            flops=20 * cell_rounds * channels * channels, bytes_accessed=12 * 2**20, transcendentals=0
        ),
        name="rounds",
    )(*operands)


def sums_kernel(tiles, block_count, band_tokens, spread, out):
    piece = spread.shape[0] // tiles
    token = lax.broadcasted_iota(jnp.int32, (band_tokens, block_count), 0).astype(F32)
    total = None
    for p in range(tiles):
        region = spread[p * piece + block_count : (p + 1) * piece].astype(F32)[:1, :block_count]
        member = jnp.where(token == region, 1.0, 0.0).astype(BF16)
        part = matmul(member, spread[p * piece : p * piece + block_count])
        total = part if total is None else total + part
    total = total.astype(BF16)
    for band in range(out.shape[0] // band_tokens):
        out[band * band_tokens : (band + 1) * band_tokens] = total


def local(
    syndrome_bits, region_assign, state_in, bit_to_candidate, bit_to_gate, conv_weight, gate_weight, gate_bias,
    pool_weight, region_embed, attn_norm_gain, query_weight, key_weight, value_weight, out_weight, mlp_norm_gain,
    mlp_up, mlp_down, return_weight,
):
    rows, cols, channels = state_in.shape
    band_tokens = region_embed.shape[0]
    bands, tiles = lax.axis_size("ctx"), lax.axis_size("tile")
    g, tile = lax.axis_index("ctx"), lax.axis_index("tile")
    width = HALF
    conv_flat = conv_weight.reshape(9 * channels, channels)

    by_bit = jnp.concatenate([bit_to_candidate, bit_to_gate], axis=1)
    bit_high, bit_low = two_parts(jnp.tile(by_bit, (ROUNDS, 1)))
    bias_high, bias_low = two_parts(jnp.concatenate([jnp.zeros_like(gate_bias), gate_bias])[None])
    gap = lambda count: jnp.zeros((count, 2 * channels), BF16)
    bit_weight = jnp.concatenate(
        [
            bit_high, gap(LOW_LANE - 2 * ROUNDS), bit_low, gap(ONE_LANE - LOW_LANE - 2 * ROUNDS),
            bias_high, bias_low, gap(LANES - ONE_LANE - 2),
        ]
    )

    above, below = row_halo(state_in[:width], state_in[-width:])
    left, right = col_halo(above, state_in, below)

    bits = syndrome_bits.transpose(2, 3, 0, 1).reshape(rows, cols, 2 * ROUNDS).astype(BF16)
    region = jnp.repeat(jnp.repeat(region_assign, 2, axis=0), 2, axis=1).astype(BF16)[..., None]
    fill = lambda count, value: jnp.full((rows, cols, count), value, BF16)
    flags = jnp.concatenate(
        [
            bits, region, fill(LOW_LANE - 2 * ROUNDS - 1, 0), bits, fill(ONE_LANE - LOW_LANE - 2 * ROUNDS, 0),
            fill(2, 1), fill(LANES - ONE_LANE - 2, 0),
        ],
        axis=-1,
    )
    flags_above, flags_below = row_halo(flags[:width], flags[-width:])
    flags_left, flags_right = col_halo(flags_above, flags, flags_below)
    flags = jnp.concatenate(
        [flags_left, jnp.concatenate([flags_above, flags, flags_below]), flags_right], axis=1
    )
    region_ext = flags[::2, ::2, REGION_LANE].astype(jnp.int32)
    row = jnp.arange(rows + 2 * width)[:, None] + g * rows - width
    col = jnp.arange(cols + 2 * width)[None, :] + tile * cols - width
    inside = (row >= 0) & (row < bands * rows) & (col >= 0) & (col < tiles * cols)
    inside = jnp.broadcast_to(inside.astype(F32).reshape(-1, 1), (inside.size, LANES))
    block_count = region_assign.size
    note = jnp.pad(region_assign.reshape(1, -1).astype(BF16), ((0, 15), (0, channels - block_count)))

    shape = lambda count, dtype: jax.ShapeDtypeStruct((count, channels), dtype)
    common = (flat(flags), inside, conv_flat, gate_weight, bit_weight)
    exact, top, bottom, spread = rounds(
        0,
        cols,
        (flat(state_in), flat(above), flat(below), flat(left), flat(right)) + common + (note,),
        [
            shape(rows * cols, F32), shape(width * cols, BF16), shape(width * cols, BF16),
            shape(tiles * (block_count + 16), BF16),
        ],
    )

    embed, _ = lax.optimization_barrier((region_embed, left))
    embed_all = to_all(jnp.broadcast_to(embed[None], (bands,) + embed.shape), "ctx").reshape(-1, embed.shape[1])

    spread = flat(to_all(spread.reshape(tiles, -1, channels), "tile"))
    grid_of = lambda value: value.reshape(-1, cols, channels)
    above, below = row_halo(grid_of(top), grid_of(bottom))
    sums = pl.pallas_call(
        functools.partial(sums_kernel, tiles, block_count, band_tokens),
        out_shape=shape(bands * band_tokens, BF16),
        name="sums",
    )(spread)
    sums_all = flat(to_all(sums.reshape(bands, band_tokens, channels), "ctx"))
    left, right = col_halo(above, jnp.concatenate([grid_of(top), grid_of(bottom)]), below)

    tokens_all = embed_all.astype(F32) + matmul(sums_all, pool_weight)
    normed_all = rms_norm(tokens_all, attn_norm_gain).astype(BF16)
    keys = matmul(normed_all, key_weight).astype(BF16)
    values = matmul(normed_all, value_weight).astype(BF16)

    half_width = width // 2
    first = (g - 1) * band_tokens + region_ext[:half_width].reshape(-1)
    second = (g + 1) * band_tokens + region_ext[-half_width:].reshape(-1)
    own = g * band_tokens + jnp.arange(band_tokens, dtype=jnp.int32)
    chosen = jnp.concatenate([own, first, second])
    pick = (chosen[:, None] == jnp.arange(bands * band_tokens, dtype=jnp.int32)).astype(BF16)
    tokens = select(pick, tokens_all)
    normed = matmul(pick, normed_all).astype(BF16)
    queries = matmul(normed, query_weight).astype(BF16)
    count = tokens.shape[0]
    scores = jnp.einsum(
        "qhd,khd->hqk", queries.reshape(count, HEADS, HDIM), keys.reshape(-1, HEADS, HDIM), preferred_element_type=F32
    ) * (1.0 / math.sqrt(HDIM))
    weights = jnp.exp(scores - jnp.max(scores, axis=-1, keepdims=True))
    denominator = jnp.sum(weights, axis=-1)
    weighted = jnp.einsum(
        "hqk,khd->hqd", weights.astype(BF16), values.reshape(-1, HEADS, HDIM), preferred_element_type=F32
    ) / denominator[..., None]
    attention = weighted.transpose(1, 0, 2).reshape(count, HEADS * HDIM).astype(BF16)
    attended = tokens + matmul(attention, out_weight)
    hidden = jax.nn.gelu(matmul(rms_norm(attended, mlp_norm_gain).astype(BF16), mlp_up)).astype(BF16)
    context = (attended + matmul(hidden, mlp_down)).astype(BF16)
    returned = matmul(context, return_weight)

    middle = region_ext[half_width:-half_width].reshape(-1)
    back = (middle[:, None] == jnp.arange(band_tokens, dtype=jnp.int32)).astype(BF16)
    share_middle = select(back, returned[:band_tokens])
    share_above, share_below = jnp.split(returned[band_tokens:], 2)
    share = jnp.concatenate([share_above, share_middle, share_below])
    (state,) = rounds(
        HALF,
        cols,
        (exact, flat(above), flat(below), flat(left), flat(right)) + common + (share,),
        [shape(rows * cols, BF16)],
    )
    return (state.reshape(rows, cols, channels), context[:band_tokens])


def solution(mesh):
    return jax.shard_map(
        local,
        mesh=mesh,
        in_specs=(
            P(None, None, "ctx", "tile"),
            P("ctx", "tile"),
            P("ctx", "tile", None),
            P(), P(), P(), P(), P(), P(),
            P("ctx", None),
            P(), P(), P(), P(), P(), P(), P(), P(), P(),
        ),
        out_specs=(P("ctx", "tile", None), P("ctx", None)),
        check_vma=False,
    )
```

```python
import functools
import math

import jax
import jax.numpy as jnp
from jax import lax
from jax.experimental import pallas as pl
from jax.experimental.pallas import tpu as pltpu
from jax.sharding import PartitionSpec as P

HEADS = 8
HDIM = 128
ROUNDS = 8
HALF = ROUNDS // 2
LANES = 128
F32 = jnp.float32
BF16 = jnp.bfloat16
MIB = 2**20

REGION_LANE, LOW_LANE, ONE_LANE = 2 * ROUNDS, 32, 64


def shifted(value, axis, step):
    size = lax.axis_size(axis)
    pairs = [(i, i + step) for i in range(size) if 0 <= i + step < size]
    return lax.ppermute(value, axis, pairs)


def matmul(left, right):
    return jnp.dot(left, right, preferred_element_type=F32)


def matmul_nt(left, right):
    return lax.dot_general(left, right, (((1,), (1,)), ((), ())), preferred_element_type=F32)


def two_parts(values):
    high = values.astype(BF16)
    return high, (values - high.astype(F32)).astype(BF16)


def select(member, values):
    high, low = two_parts(values)
    return matmul(member, high) + matmul(member, low)


def rms_norm(values, gain):
    return values * lax.rsqrt(jnp.mean(values * values, axis=-1, keepdims=True) + 1e-05) * gain


def iota(shape, dim):
    return lax.broadcasted_iota(jnp.int32, shape, dim)


def one_hot(condition):
    return jnp.where(condition, 1.0, 0.0).astype(BF16)


def call(kernel, name, operands, outs, scratch=(), in_hbm=(), scalars=(), grant=8, flops=0, moved=MIB):
    def spec(index):
        if index in in_hbm:
            return pl.BlockSpec(memory_space=pltpu.HBM)
        return pl.BlockSpec(memory_space=pltpu.SMEM if index in scalars else pltpu.VMEM)

    return pl.pallas_call(
        kernel,
        out_shape=outs,
        in_specs=[spec(index) for index in range(len(operands))],
        out_specs=[pl.BlockSpec(memory_space=pltpu.VMEM)] * len(outs),
        scratch_shapes=scratch,
        compiler_params=pltpu.CompilerParams(vmem_limit_bytes=grant * MIB),
        cost_estimate=pl.CostEstimate(flops=flops, bytes_accessed=moved, transcendentals=0),
        name=name,
    )(*operands)


def array(count, lanes, dtype):
    return jax.ShapeDtypeStruct((count, lanes), dtype)


def message_kernel(syndrome, region, state, top, bottom):
    planes, rows, cols = syndrome.shape
    channels = state.shape[1]
    bits = syndrome[...].reshape(planes * rows, cols).astype(F32).astype(BF16)
    column_bits = matmul_nt(one_hot(iota((cols, cols), 0) == iota((cols, cols), 1)), bits).astype(BF16)
    block_rows, block_cols = region.shape
    regions = jnp.concatenate([region[...].astype(F32), jnp.zeros((8 - block_rows, block_cols), F32)])
    spread = one_hot(iota((cols, block_cols), 0) // 2 == iota((cols, block_cols), 1))
    column_region = matmul_nt(spread, regions.astype(BF16)).astype(BF16)
    plane, lane = iota((planes * rows, LANES), 0), iota((planes * rows, LANES), 1)
    ones = jnp.where((iota((cols, LANES), 1) == ONE_LANE) | (iota((cols, LANES), 1) == ONE_LANE + 1), 1.0, 0.0)
    for r in range(rows):
        place = one_hot((plane == lane * rows + r) | (plane == (lane - LOW_LANE) * rows + r))
        region_place = one_hot((iota((8, LANES), 0) == r // 2) & (iota((8, LANES), 1) == REGION_LANE))
        flags = matmul(column_bits, place) + matmul(column_region, region_place) + ones
        half = (top, bottom)[r // (rows // 2)]
        at = pl.ds(r % (rows // 2) * cols, cols)
        half[at, :channels] = state[r * cols : (r + 1) * cols]
        half[at, channels:] = flags.astype(BF16)


def edges_kernel(cols, *refs):
    parts, (first, last) = refs[:-2], refs[-2:]
    firsts, lasts = [], []
    for part in parts:
        values = part[...].astype(F32)
        for at in range(0, part.shape[0], cols):
            firsts.append(values[at : at + HALF])
            lasts.append(values[at + cols - HALF : at + cols])
    first[...] = jnp.concatenate(firsts).astype(BF16)
    last[...] = jnp.concatenate(lasts).astype(BF16)


def fetch(sources, targets, sems):
    copies = [pltpu.make_async_copy(*pair, sems.at[i]) for i, pair in enumerate(zip(sources, targets))]
    for copy in copies:
        copy.start()
    return copies


def prepare_kernel(candidate_bits, gate_bits, bias, embed, conv_hbm, gate_hbm, bit_weight, spread, conv, gate, sems):
    copies = fetch((conv_hbm, gate_hbm), (conv, gate), sems)
    by_bit = jnp.concatenate([candidate_bits[...], gate_bits[...]], axis=1)
    bias = jnp.concatenate([jnp.zeros_like(bias), bias[...]], axis=1)
    lane = iota((LANES, 1), 0)
    weight = jnp.zeros(bit_weight.shape, F32)
    for part in range(2):
        begin = (0, LOW_LANE)[part]
        for bit in range(2):
            row = two_parts(by_bit[bit : bit + 1])[part].astype(F32)
            here = (lane >= begin) & (lane < begin + 2 * ROUNDS) & (lane % 2 == bit)
            weight = jnp.where(here, row, weight)
        weight = jnp.where(lane == ONE_LANE + part, two_parts(bias)[part].astype(F32), weight)
    bit_weight[...] = weight.astype(BF16)
    for at in range(0, spread.shape[0], embed.shape[0]):
        spread[at : at + embed.shape[0]] = embed[...]
    for copy in copies:
        copy.wait()


class Patch:
    def __init__(self, cols, state, taps, bits, mask):
        self.cols, self.span, self.width = cols, cols + 2 * HALF, HALF
        self.state, self.taps, self.bits, self.mask = state, taps, bits, mask
        self.groups, self.count = state.shape[:2]
        self.rows, self.channels = self.count // self.span, self.groups * LANES

    def get(self, at):
        return jnp.concatenate([self.state[j, at] for j in range(self.groups)], axis=1)

    def put(self, at, values):
        for j in range(self.groups):
            self.state[j, at] = values[:, j * LANES : (j + 1) * LANES]

    def fill(self, parts, left, right, put):
        r = 0
        for part in parts:
            for at in range(0, part.shape[0], self.cols):
                put(pl.ds(r * self.span + self.width, self.cols), part[at : at + self.cols].astype(F32))
                r += 1
        for part, first in ((left, 0), (right, self.width + self.cols)):
            values = part[...].astype(F32)
            for r in range(self.rows):
                put(pl.ds(r * self.span + first, self.width), values[r * self.width : (r + 1) * self.width])

    def keep(self, slot, first, values):
        size = values.shape[0]
        mask = self.mask[first : first + size]
        values = jnp.concatenate([values[:, c : c + LANES] * mask for c in range(0, self.channels, LANES)], axis=1)
        for b in range(3):
            moved = values if b == 1 else pltpu.roll(values, 1 if b == 0 else size - 1, 0)
            self.taps[slot, first : first + size, b * self.channels : (b + 1) * self.channels] = moved.astype(BF16)

    def advance(self, first_round, flags, conv, gate_weight, bit_weight):
        span, channels, rows = self.span, self.channels, self.rows
        for first in range(0, rows, rows // 2):
            self.keep(0, first * span, self.get(pl.ds(first * span, rows // 2 * span)))
        lane = iota((1, LANES), 1)
        for step in range(HALF):
            t, slot = first_round + step, step % 2
            now = (lane == 2 * t) | (lane == 2 * t + 1) | (lane == LOW_LANE + 2 * t) | (lane == LOW_LANE + 2 * t + 1)
            self.bits[...] = flags[...] * one_hot(now | (lane >= ONE_LANE))
            total = rows - 2 * (step + 1)
            cut = (total // 4 + total // 2 % 2) * 2
            for begin, part_rows in ((step + 1, cut), (step + 1 + cut, total - cut)):
                first, size = begin * span, part_rows * span
                columns = jnp.concatenate(
                    [self.taps[slot, first + a * span : first + a * span + size] for a in (-1, 0, 1)], axis=1
                )
                flag = self.bits[first : first + size]
                rounded = self.taps[slot, first : first + size, channels : 2 * channels]
                candidate = matmul(columns, conv[...]) + matmul(flag, bit_weight[:, :channels])
                gate = matmul(rounded, gate_weight[...]) + matmul(flag, bit_weight[:, channels:])
                before = self.get(pl.ds(first, size))
                after = before + (0.5 * jnp.tanh(0.5 * gate) + 0.5) * (jnp.tanh(candidate) - before)
                self.put(pl.ds(first, size), after)
                if step < HALF - 1:
                    self.keep(1 - slot, first, after)

    def own(self, r):
        return self.get(pl.ds((self.width + r) * self.span + self.width, self.cols))


def patch_scratch(rows, cols, channels):
    count = (rows + 2 * HALF) * (cols + 2 * HALF)
    return [
        pltpu.VMEM((channels // LANES, count, LANES), F32),
        pltpu.VMEM((2, count, 3 * channels), BF16),
        pltpu.VMEM((count, LANES), BF16),
        pltpu.VMEM((count, LANES), F32),
    ]


def mask_of(flags):
    return matmul(flags, one_hot(iota((LANES, LANES), 0) == ONE_LANE))


def first_kernel(
    cols, above, top, bottom, below, left, right, region, bit_weight, conv, gate_weight,
    exact, new_top, new_bottom, partial, flags, state, taps, bits, mask, flags_wide,
):
    patch = Patch(cols, state, taps, bits, mask)
    channels = patch.channels

    def put(at, values):
        patch.put(at, values[:, :channels])
        flags_wide[at] = values[:, channels:]

    patch.fill((above, top, bottom, below), left, right, put)
    flags[...] = flags_wide[...].astype(BF16)
    mask[...] = mask_of(flags[...])
    patch.advance(0, flags, conv, gate_weight, bit_weight)

    own = patch.rows - 2 * patch.width
    for r in range(own):
        values = patch.own(r)
        exact[r * cols : (r + 1) * cols] = values
        half = (new_top, new_bottom)[r // (own // 2)]
        half[r % (own // 2) * cols : (r % (own // 2) + 1) * cols] = values.astype(BF16)
    block_cols = cols // 2
    total = jnp.zeros(partial.shape, F32)
    for r in range(0, own, 2):
        begin = (patch.width + r) * patch.span + patch.width
        parts = [
            patch.get(pl.ds(begin + a * patch.span + b, block_cols, stride=2)) for a in range(2) for b in range(2)
        ]
        pooled = (sum(parts[1:], parts[0]) * 0.25).astype(BF16)
        member = one_hot(iota((partial.shape[0], block_cols), 0) == region[r // 2 : r // 2 + 1])
        total = total + matmul(member, pooled)
    partial[...] = total.astype(BF16)


def chunk_kernel(tiles, pieces, out):
    values = pieces[...].astype(F32)
    chunk = values.shape[0] // tiles
    total = values[:chunk]
    for p in range(1, tiles):
        total = total + values[p * chunk : (p + 1) * chunk]
    total = total.astype(BF16)
    for p in range(out.shape[0] // chunk):
        out[p * chunk : (p + 1) * chunk] = total


def second_kernel(
    cols, bands, band_index, exact, above, below, left, right, flags, sums, embed, attn_gain, mlp_gain, bit_weight,
    conv, gate_weight, pool_weight, key_weight, value_weight, query_weight, out_hbm, up_hbm, down_hbm, return_hbm,
    state_out, context_out,
    state, taps, bits, mask, out_weight, up_weight, down_weight, return_weight,
    tokens_all, normed_all, keys, values, member, tokens, normed, attention, hidden, context, sems,
):
    copies = fetch(
        (out_hbm, up_hbm, down_hbm, return_hbm), (out_weight, up_weight, down_weight, return_weight), sems
    )
    patch = Patch(cols, state, taps, bits, mask)
    patch.fill((above, exact, below), left, right, patch.put)
    mask[...] = mask_of(flags[...])
    region = matmul(flags[...], one_hot(iota((LANES, LANES), 0) == REGION_LANE))
    member[...] = jnp.where(region == iota(region.shape, 1).astype(F32), 1.0, 0.0)

    band_tokens = sums.shape[0] // bands
    for band in range(bands):
        at = pl.ds(band * band_tokens, band_tokens)
        total = embed[at].astype(F32) + matmul(sums[at], pool_weight[...])
        tokens_all[at] = total
        normed_all[at] = rms_norm(total, attn_gain[...]).astype(BF16)

    g = band_index[0]
    own = pl.ds(pl.multiple_of(g * band_tokens, band_tokens), band_tokens)
    tokens[:band_tokens] = tokens_all[own]
    normed[:band_tokens] = normed_all[own]
    blocks = patch.span // 2
    room = (blocks + 7) // 8 * 8
    block_rows = patch.width // 2
    side = room * block_rows
    for number, (band, row) in enumerate(
        ((jnp.maximum(g - 1, 0), 0), (jnp.minimum(g + 1, bands - 1), patch.rows - patch.width))
    ):
        pick = jnp.concatenate(
            [member[pl.ds((row + 2 * r) * patch.span, room, stride=2)] for r in range(block_rows)]
        ).astype(BF16)
        at = pl.ds(pl.multiple_of(band * band_tokens, band_tokens), band_tokens)
        into = pl.ds(band_tokens + number * side, side)
        tokens[into] = select(pick, tokens_all[at])
        normed[into] = matmul(pick, normed_all[at]).astype(BF16)

    keys[...] = matmul(normed_all[...], key_weight[...]).astype(BF16)
    values[...] = matmul(normed_all[...], value_weight[...]).astype(BF16)
    queries = matmul(normed[...], query_weight[...]).astype(BF16)
    for head in range(HEADS):
        at = slice(head * HDIM, (head + 1) * HDIM)
        scores = matmul_nt(queries[:, at], keys[:, at]) * (1.0 / math.sqrt(HDIM))
        weights = jnp.exp(scores - jnp.max(scores, axis=-1, keepdims=True))
        denominator = jnp.sum(weights, axis=-1, keepdims=True)
        attention[:, at] = (matmul(weights.astype(BF16), values[:, at]) / denominator).astype(BF16)
    copies[0].wait()
    attended = tokens[...] + matmul(attention[...], out_weight[...])
    tokens[...] = attended
    normed[...] = rms_norm(attended, mlp_gain[...]).astype(BF16)
    copies[1].wait()
    part = 512
    for at in range(0, up_weight.shape[1], part):
        hidden[:, at : at + part] = jax.nn.gelu(matmul(normed[...], up_weight[:, at : at + part])).astype(BF16)
    copies[2].wait()
    context[...] = (tokens[...] + matmul(hidden[...], down_weight[...])).astype(BF16)
    context_out[...] = context[:band_tokens]
    copies[3].wait()
    returned = matmul(context[...], return_weight[...])

    first, last = patch.width * patch.span, (patch.rows - patch.width) * patch.span
    middle = pl.ds(first, last - first)
    patch.put(middle, patch.get(middle) + select(member[first:last].astype(BF16), returned[:band_tokens]))
    for number, row in enumerate((0, patch.rows - patch.width)):
        for r in range(patch.width):
            start = band_tokens + number * side + r // 2 * room
            share = returned[start : start + blocks]
            for c in range(2):
                at = pl.ds((row + r) * patch.span + c, blocks, stride=2)
                patch.put(at, patch.get(at) + share)

    patch.advance(HALF, flags, conv, gate_weight, bit_weight)
    for r in range(patch.rows - 2 * patch.width):
        state_out[r * cols : (r + 1) * cols] = patch.own(r).astype(BF16)


def local(
    syndrome_bits, region_assign, state_in, bit_to_candidate, bit_to_gate, conv_weight, gate_weight, gate_bias,
    pool_weight, region_embed, attn_norm_gain, query_weight, key_weight, value_weight, out_weight, mlp_norm_gain,
    mlp_up, mlp_down, return_weight,
):
    rows, cols, channels = state_in.shape
    band_tokens, embed_width = region_embed.shape
    bands, tiles = lax.axis_size("ctx"), lax.axis_size("tile")
    conv = conv_weight.reshape(9 * channels, channels)
    half = HALF * cols

    wide = channels + LANES
    top, bottom = call(
        message_kernel,
        "message",
        (syndrome_bits.reshape(2 * ROUNDS, rows, cols), region_assign, state_in.reshape(rows * cols, channels)),
        [array(half, wide, BF16)] * 2,
    )

    def row_halo(top, bottom):
        return shifted(bottom, "ctx", 1), shifted(top, "ctx", -1)

    def col_halo(above, top, bottom, below):
        first, last = call(
            functools.partial(edges_kernel, cols),
            "edges",
            (above, top, bottom, below),
            [array((rows + 2 * HALF) * HALF, top.shape[1], BF16)] * 2,
        )
        return shifted(last, "tile", 1), shifted(first, "tile", -1)

    above, below = row_halo(top, bottom)
    conv_late, _ = lax.optimization_barrier((conv, top))
    bit_weight, embed, conv_near, gate_near = call(
        prepare_kernel,
        "prepare",
        (bit_to_candidate, bit_to_gate, gate_bias[None], region_embed, conv_late, gate_weight),
        [
            array(LANES, 2 * channels, BF16), array(bands * band_tokens, embed_width, BF16),
            array(*conv.shape, BF16), array(*gate_weight.shape, BF16),
        ],
        [pltpu.SemaphoreType.DMA((2,))],
        in_hbm=(4, 5),
        moved=16 * MIB,
    )
    above, below, embed, conv_near = lax.optimization_barrier((above, below, embed, conv_near))
    left, right = col_halo(above, top, bottom, below)
    embed = lax.all_to_all(embed.reshape(bands, band_tokens, -1), "ctx", 0, 0).reshape(-1, embed_width)

    count = (rows + 2 * HALF) * (cols + 2 * HALF)
    flops = 15 * rows * cols * HALF * 2 * channels * channels
    exact, top, bottom, partial, flags = call(
        functools.partial(first_kernel, cols),
        "rounds",
        (above, top, bottom, below, left, right, region_assign, bit_weight, conv_near, gate_near),
        [
            array(rows * cols, channels, F32), array(half, channels, BF16), array(half, channels, BF16),
            array(band_tokens, channels, BF16), array(count, LANES, BF16),
        ],
        patch_scratch(rows, cols, channels) + [pltpu.VMEM((count, LANES), F32)],
        grant=24,
        flops=flops,
    )

    above, below = row_halo(top, bottom)
    partial, embed = lax.optimization_barrier((partial, embed))
    pieces = lax.all_to_all(partial.reshape(tiles, -1, channels), "tile", 0, 0)
    (chunks,) = call(
        functools.partial(chunk_kernel, tiles),
        "chunk",
        (pieces.reshape(band_tokens, channels),),
        [array(bands * band_tokens, channels, BF16)],
    )
    sums = lax.all_to_all(chunks.reshape(bands * tiles, -1, channels), ("ctx", "tile"), 0, 0)
    above, below, _ = lax.optimization_barrier((above, below, chunks))
    left, right = col_halo(above, top, bottom, below)
    late = (out_weight, mlp_up, mlp_down, return_weight)
    blocks = (cols + 2 * HALF) // 2
    layer_rows = band_tokens + HALF * ((blocks + 7) // 8 * 8)
    all_tokens = bands * band_tokens
    state, context = call(
        functools.partial(second_kernel, cols, bands),
        "context",
        (
            lax.axis_index("ctx").reshape(1), exact, above, below, left, right, flags,
            sums.reshape(all_tokens, channels), embed, attn_norm_gain[None], mlp_norm_gain[None], bit_weight,
            conv, gate_weight, pool_weight, key_weight, value_weight, query_weight, *late,
        ),
        [array(rows * cols, channels, BF16), array(band_tokens, embed_width, BF16)],
        patch_scratch(rows, cols, channels)
        + [pltpu.VMEM(weight.shape, BF16) for weight in late]
        + [
            pltpu.VMEM((all_tokens, embed_width), F32), pltpu.VMEM((all_tokens, embed_width), BF16),
            pltpu.VMEM((all_tokens, embed_width), BF16), pltpu.VMEM((all_tokens, embed_width), BF16),
            pltpu.VMEM((count, LANES), F32),
            pltpu.VMEM((layer_rows, embed_width), F32), pltpu.VMEM((layer_rows, embed_width), BF16),
            pltpu.VMEM((layer_rows, embed_width), BF16), pltpu.VMEM((layer_rows, mlp_up.shape[1]), BF16),
            pltpu.VMEM((layer_rows, embed_width), BF16), pltpu.SemaphoreType.DMA((len(late),)),
        ],
        in_hbm=range(18, 22),
        scalars=(0,),
        grant=28 + all_tokens // 64,
        flops=2 * flops,
    )
    return (state.reshape(rows, cols, channels), context)


def solution(mesh):
    return jax.shard_map(
        local,
        mesh=mesh,
        in_specs=(
            P(None, None, "ctx", "tile"),
            P("ctx", "tile"),
            P("ctx", "tile", None),
            P(), P(), P(), P(), P(), P(),
            P("ctx", None),
            P(), P(), P(), P(), P(), P(), P(), P(), P(),
        ),
        out_specs=(P("ctx", "tile", None), P("ctx", None)),
        check_vma=False,
    )
```

```python
import functools
import math

import jax
import jax.numpy as jnp
from jax import lax
from jax.experimental import pallas as pl
from jax.experimental.pallas import tpu as pltpu
from jax.sharding import PartitionSpec as P

HEADS = 8
HDIM = 128
ROUNDS = 8
HALF = ROUNDS // 2
LANES = 128
F32 = jnp.float32
BF16 = jnp.bfloat16
MIB = 2**20

REGION_LANE, LOW_LANE, ONE_LANE = 2 * ROUNDS, 32, 64


def shifted(value, down, right):
    bands, tiles = lax.axis_size("ctx"), lax.axis_size("tile")
    pairs = [
        (i * tiles + j, (i + down) * tiles + j + right)
        for i in range(bands)
        for j in range(tiles)
        if 0 <= i + down < bands and 0 <= j + right < tiles
    ]
    return lax.ppermute(value, ("ctx", "tile"), pairs)


def exchange(sides):
    top, bottom, first, last, top_first, top_last, bottom_first, bottom_last = sides
    return (
        shifted(bottom, 1, 0),
        shifted(top, -1, 0),
        shifted(last, 0, 1),
        shifted(first, 0, -1),
        shifted(bottom_last, 1, 1),
        shifted(bottom_first, 1, -1),
        shifted(top_last, -1, 1),
        shifted(top_first, -1, -1),
    )


def matmul(left, right):
    return jnp.dot(left, right, preferred_element_type=F32)


def matmul_nt(left, right):
    return lax.dot_general(left, right, (((1,), (1,)), ((), ())), preferred_element_type=F32)


def two_parts(values):
    high = values.astype(BF16)
    return high, (values - high.astype(F32)).astype(BF16)


def select(member, values):
    high, low = two_parts(values)
    return matmul(member, high) + matmul(member, low)


def rms_norm(values, gain):
    return values * lax.rsqrt(jnp.mean(values * values, axis=-1, keepdims=True) + 1e-05) * gain


def iota(shape, dim):
    return lax.broadcasted_iota(jnp.int32, shape, dim)


def one_hot(condition):
    return jnp.where(condition, 1.0, 0.0).astype(BF16)


def call(kernel, name, operands, outs, scratch=(), in_hbm=(), scalars=(), grant=60, flops=0, moved=MIB):
    def spec(index):
        if index in in_hbm:
            return pl.BlockSpec(memory_space=pltpu.HBM)
        return pl.BlockSpec(memory_space=pltpu.SMEM if index in scalars else pltpu.VMEM)

    return pl.pallas_call(
        kernel,
        out_shape=outs,
        in_specs=[spec(index) for index in range(len(operands))],
        out_specs=[pl.BlockSpec(memory_space=pltpu.VMEM)] * len(outs),
        scratch_shapes=scratch,
        compiler_params=pltpu.CompilerParams(vmem_limit_bytes=grant * MIB),
        cost_estimate=pl.CostEstimate(flops=flops, bytes_accessed=moved, transcendentals=0),
        name=name,
    )(*operands)


def array(count, lanes, dtype):
    return jax.ShapeDtypeStruct((count, lanes), dtype)


def side_arrays(half, lanes):
    edge = HALF * HALF
    return [array(count, lanes, BF16) for count in (half, half, 2 * edge, 2 * edge, edge, edge, edge, edge)]


def write_sides(sides, rows, cols):
    top, bottom, first, last, *corners = sides
    edges = []
    for r, values in enumerate(rows):
        half = (top, bottom)[r // HALF]
        half[r % HALF * cols : (r % HALF + 1) * cols] = values.astype(BF16)
    for begin in (0, cols - HALF):
        edges.append(jnp.concatenate([values[begin : begin + HALF] for values in rows]).astype(BF16))
    first[...], last[...] = edges
    edge = HALF * HALF
    for at, corner in enumerate(corners):
        corner[...] = edges[at % 2][at // 2 * edge : (at // 2 + 1) * edge]


def message_kernel(syndrome, region, state, *sides):
    planes, rows, cols = syndrome.shape
    bits = syndrome[...].reshape(planes * rows, cols).astype(F32).astype(BF16)
    column_bits = matmul_nt(one_hot(iota((cols, cols), 0) == iota((cols, cols), 1)), bits).astype(BF16)
    block_rows, block_cols = region.shape
    regions = jnp.concatenate([region[...].astype(F32), jnp.zeros((8 - block_rows, block_cols), F32)])
    spread = one_hot(iota((cols, block_cols), 0) // 2 == iota((cols, block_cols), 1))
    column_region = matmul_nt(spread, regions.astype(BF16)).astype(BF16)
    plane, lane = iota((planes * rows, LANES), 0), iota((planes * rows, LANES), 1)
    ones = jnp.where((iota((cols, LANES), 1) == ONE_LANE) | (iota((cols, LANES), 1) == ONE_LANE + 1), 1.0, 0.0)
    cells = []
    for r in range(rows):
        place = one_hot((plane == lane * rows + r) | (plane == (lane - LOW_LANE) * rows + r))
        region_place = one_hot((iota((8, LANES), 0) == r // 2) & (iota((8, LANES), 1) == REGION_LANE))
        flags = matmul(column_bits, place) + matmul(column_region, region_place) + ones
        cells.append(jnp.concatenate([state[r * cols : (r + 1) * cols].astype(F32), flags], axis=1))
    write_sides(sides, cells, cols)


def fetch(sources, targets, sems):
    copies = [pltpu.make_async_copy(*pair, sems.at[i]) for i, pair in enumerate(zip(sources, targets))]
    for copy in copies:
        copy.start()
    return copies


def prepare_kernel(candidate_bits, gate_bits, bias, embed, bit_weight, spread):
    by_bit = jnp.concatenate([candidate_bits[...], gate_bits[...]], axis=1)
    bias = jnp.concatenate([jnp.zeros_like(bias), bias[...]], axis=1)
    lane = iota((LANES, 1), 0)
    weight = jnp.zeros(bit_weight.shape, F32)
    for part in range(2):
        begin = (0, LOW_LANE)[part]
        for bit in range(2):
            row = two_parts(by_bit[bit : bit + 1])[part].astype(F32)
            here = (lane >= begin) & (lane < begin + 2 * ROUNDS) & (lane % 2 == bit)
            weight = jnp.where(here, row, weight)
        weight = jnp.where(lane == ONE_LANE + part, two_parts(bias)[part].astype(F32), weight)
    bit_weight[...] = weight.astype(BF16)
    for at in range(0, spread.shape[0], embed.shape[0]):
        spread[at : at + embed.shape[0]] = embed[...]


class Patch:
    def __init__(self, cols, state, taps, bits, mask):
        self.cols, self.span, self.width = cols, cols + 2 * HALF, HALF
        self.state, self.taps, self.bits, self.mask = state, taps, bits, mask
        self.groups, self.count = state.shape[:2]
        self.rows, self.channels = self.count // self.span, self.groups * LANES

    def get(self, at):
        return jnp.concatenate([self.state[j, at] for j in range(self.groups)], axis=1)

    def put(self, at, values):
        for j in range(self.groups):
            self.state[j, at] = values[:, j * LANES : (j + 1) * LANES]

    def fill(self, parts, halo, put):
        above, below, left, right, above_left, above_right, below_left, below_right = halo
        parts = (above, *parts, below)
        r = 0
        for part in parts:
            for at in range(0, part.shape[0], self.cols):
                put(pl.ds(r * self.span + self.width, self.cols), part[at : at + self.cols].astype(F32))
                r += 1
        for parts, first in (
            ((above_left, left, below_left), 0),
            ((above_right, right, below_right), self.width + self.cols),
        ):
            values = jnp.concatenate([part[...].astype(F32) for part in parts])
            for r in range(self.rows):
                put(pl.ds(r * self.span + first, self.width), values[r * self.width : (r + 1) * self.width])

    def keep(self, slot, first, values):
        size = values.shape[0]
        mask = self.mask[first : first + size]
        values = jnp.concatenate([values[:, c : c + LANES] * mask for c in range(0, self.channels, LANES)], axis=1)
        for b in range(3):
            moved = values if b == 1 else pltpu.roll(values, 1 if b == 0 else size - 1, 0)
            self.taps[slot, first : first + size, b * self.channels : (b + 1) * self.channels] = moved.astype(BF16)

    def advance(self, first_round, flags, conv, gate_weight, bit_weight):
        span, channels, rows = self.span, self.channels, self.rows
        for first in range(0, rows, rows // 2):
            self.keep(0, first * span, self.get(pl.ds(first * span, rows // 2 * span)))
        lane = iota((1, LANES), 1)
        for step in range(HALF):
            t, slot = first_round + step, step % 2
            now = (lane == 2 * t) | (lane == 2 * t + 1) | (lane == LOW_LANE + 2 * t) | (lane == LOW_LANE + 2 * t + 1)
            self.bits[...] = flags[...] * one_hot(now | (lane >= ONE_LANE))
            total = rows - 2 * (step + 1)
            cut = (total // 4 + total // 2 % 2) * 2
            for begin, part_rows in ((step + 1, cut), (step + 1 + cut, total - cut)):
                first, size = begin * span, part_rows * span
                columns = jnp.concatenate(
                    [self.taps[slot, first + a * span : first + a * span + size] for a in (-1, 0, 1)], axis=1
                )
                flag = self.bits[first : first + size]
                rounded = self.taps[slot, first : first + size, channels : 2 * channels]
                candidate = matmul(columns, conv[...]) + matmul(flag, bit_weight[:, :channels])
                gate = matmul(rounded, gate_weight[...]) + matmul(flag, bit_weight[:, channels:])
                before = self.get(pl.ds(first, size))
                after = before + (0.5 * jnp.tanh(0.5 * gate) + 0.5) * (jnp.tanh(candidate) - before)
                self.put(pl.ds(first, size), after)
                if step < HALF - 1:
                    self.keep(1 - slot, first, after)

    def own(self, r):
        return self.get(pl.ds((self.width + r) * self.span + self.width, self.cols))


def patch_scratch(rows, cols, channels):
    count = (rows + 2 * HALF) * (cols + 2 * HALF)
    return [
        pltpu.VMEM((channels // LANES, count, LANES), F32),
        pltpu.VMEM((2, count, 3 * channels), BF16),
        pltpu.VMEM((count, LANES), BF16),
        pltpu.VMEM((count, LANES), F32),
    ]


def mask_of(flags):
    return matmul(flags, one_hot(iota((LANES, LANES), 0) == ONE_LANE))


def first_kernel(cols, top, bottom, *refs):
    halo, (region, bit_weight, conv_hbm, gate_hbm) = refs[:8], refs[8:12]
    (exact, partial, flags), sides = refs[12:15], refs[15:23]
    state, taps, bits, mask, flags_wide, conv, gate_weight, sems = refs[23:]
    copies = fetch((conv_hbm, gate_hbm), (conv, gate_weight), sems)
    patch = Patch(cols, state, taps, bits, mask)
    channels = patch.channels

    def put(at, values):
        patch.put(at, values[:, :channels])
        flags_wide[at] = values[:, channels:]

    patch.fill((top, bottom), halo, put)
    flags[...] = flags_wide[...].astype(BF16)
    mask[...] = mask_of(flags[...])
    for copy in copies:
        copy.wait()
    patch.advance(0, flags, conv, gate_weight, bit_weight)

    own = patch.rows - 2 * patch.width
    cells = [patch.own(r) for r in range(own)]
    for r in range(own):
        exact[r * cols : (r + 1) * cols] = cells[r]
    write_sides(sides, cells, cols)
    block_cols = cols // 2
    total = jnp.zeros(partial.shape, F32)
    for r in range(0, own, 2):
        begin = (patch.width + r) * patch.span + patch.width
        parts = [
            patch.get(pl.ds(begin + a * patch.span + b, block_cols, stride=2)) for a in range(2) for b in range(2)
        ]
        pooled = (sum(parts[1:], parts[0]) * 0.25).astype(BF16)
        member = one_hot(iota((partial.shape[0], block_cols), 0) == region[r // 2 : r // 2 + 1])
        total = total + matmul(member, pooled)
    partial[...] = total.astype(BF16)


def chunk_kernel(tiles, pieces, out):
    values = pieces[...].astype(F32)
    chunk = values.shape[0] // tiles
    total = values[:chunk]
    for p in range(1, tiles):
        total = total + values[p * chunk : (p + 1) * chunk]
    total = total.astype(BF16)
    for p in range(out.shape[0] // chunk):
        out[p * chunk : (p + 1) * chunk] = total


def second_kernel(
    cols, bands, band_index, exact, above, below, left, right, above_left, above_right, below_left, below_right,
    flags, sums, embed, attn_gain, mlp_gain, bit_weight,
    pool_hbm, key_hbm, value_hbm, query_hbm, out_hbm, up_hbm, down_hbm, return_hbm, conv_hbm, gate_hbm,
    state_out, context_out,
    state, taps, bits, mask, pool_weight, key_weight, value_weight, query_weight, out_weight, up_weight,
    down_weight, return_weight, conv, gate_weight,
    tokens_all, normed_all, keys, values, member, tokens, normed, attention, hidden, context, sems,
):
    copies = fetch(
        (pool_hbm, key_hbm, value_hbm, query_hbm, out_hbm, up_hbm, down_hbm, return_hbm, conv_hbm, gate_hbm),
        (pool_weight, key_weight, value_weight, query_weight, out_weight, up_weight, down_weight, return_weight,
         conv, gate_weight),
        sems,
    )
    patch = Patch(cols, state, taps, bits, mask)
    halo = (above, below, left, right, above_left, above_right, below_left, below_right)
    patch.fill((exact,), halo, patch.put)
    mask[...] = mask_of(flags[...])
    region = matmul(flags[...], one_hot(iota((LANES, LANES), 0) == REGION_LANE))
    member[...] = jnp.where(region == iota(region.shape, 1).astype(F32), 1.0, 0.0)

    band_tokens = sums.shape[0] // bands
    copies[0].wait()
    for band in range(bands):
        at = pl.ds(band * band_tokens, band_tokens)
        total = embed[at].astype(F32) + matmul(sums[at], pool_weight[...])
        tokens_all[at] = total
        normed_all[at] = rms_norm(total, attn_gain[...]).astype(BF16)

    g = band_index[0]
    own = pl.ds(pl.multiple_of(g * band_tokens, band_tokens), band_tokens)
    tokens[:band_tokens] = tokens_all[own]
    normed[:band_tokens] = normed_all[own]
    blocks = patch.span // 2
    room = (blocks + 7) // 8 * 8
    block_rows = patch.width // 2
    side = room * block_rows
    for number, (band, row) in enumerate(
        ((jnp.maximum(g - 1, 0), 0), (jnp.minimum(g + 1, bands - 1), patch.rows - patch.width))
    ):
        pick = jnp.concatenate(
            [member[pl.ds((row + 2 * r) * patch.span, room, stride=2)] for r in range(block_rows)]
        ).astype(BF16)
        at = pl.ds(pl.multiple_of(band * band_tokens, band_tokens), band_tokens)
        into = pl.ds(band_tokens + number * side, side)
        tokens[into] = select(pick, tokens_all[at])
        normed[into] = matmul(pick, normed_all[at]).astype(BF16)

    copies[1].wait()
    keys[...] = matmul(normed_all[...], key_weight[...]).astype(BF16)
    copies[2].wait()
    values[...] = matmul(normed_all[...], value_weight[...]).astype(BF16)
    copies[3].wait()
    queries = matmul(normed[...], query_weight[...]).astype(BF16)
    for head in range(HEADS):
        at = slice(head * HDIM, (head + 1) * HDIM)
        scores = matmul_nt(queries[:, at], keys[:, at]) * (1.0 / math.sqrt(HDIM))
        weights = jnp.exp(scores - jnp.max(scores, axis=-1, keepdims=True))
        denominator = jnp.sum(weights, axis=-1, keepdims=True)
        attention[:, at] = (matmul(weights.astype(BF16), values[:, at]) / denominator).astype(BF16)
    copies[4].wait()
    attended = tokens[...] + matmul(attention[...], out_weight[...])
    tokens[...] = attended
    normed[...] = rms_norm(attended, mlp_gain[...]).astype(BF16)
    copies[5].wait()
    part = 512
    for at in range(0, up_weight.shape[1], part):
        hidden[:, at : at + part] = jax.nn.gelu(matmul(normed[...], up_weight[:, at : at + part])).astype(BF16)
    copies[6].wait()
    context[...] = (tokens[...] + matmul(hidden[...], down_weight[...])).astype(BF16)
    context_out[...] = context[:band_tokens]
    copies[7].wait()
    returned = matmul(context[...], return_weight[...])

    first, last = patch.width * patch.span, (patch.rows - patch.width) * patch.span
    middle = pl.ds(first, last - first)
    patch.put(middle, patch.get(middle) + select(member[first:last].astype(BF16), returned[:band_tokens]))
    for number, row in enumerate((0, patch.rows - patch.width)):
        for r in range(patch.width):
            start = band_tokens + number * side + r // 2 * room
            share = returned[start : start + blocks]
            for c in range(2):
                at = pl.ds((row + r) * patch.span + c, blocks, stride=2)
                patch.put(at, patch.get(at) + share)

    copies[8].wait()
    copies[9].wait()
    patch.advance(HALF, flags, conv, gate_weight, bit_weight)
    for r in range(patch.rows - 2 * patch.width):
        state_out[r * cols : (r + 1) * cols] = patch.own(r).astype(BF16)


def local(
    syndrome_bits, region_assign, state_in, bit_to_candidate, bit_to_gate, conv_weight, gate_weight, gate_bias,
    pool_weight, region_embed, attn_norm_gain, query_weight, key_weight, value_weight, out_weight, mlp_norm_gain,
    mlp_up, mlp_down, return_weight,
):
    rows, cols, channels = state_in.shape
    band_tokens, embed_width = region_embed.shape
    bands, tiles = lax.axis_size("ctx"), lax.axis_size("tile")
    conv = conv_weight.reshape(9 * channels, channels)
    half = HALF * cols

    sides = call(
        message_kernel,
        "message",
        (syndrome_bits.reshape(2 * ROUNDS, rows, cols), region_assign, state_in.reshape(rows * cols, channels)),
        side_arrays(half, channels + LANES),
    )
    halo = exchange(sides)
    embed, _ = lax.optimization_barrier((region_embed, sides[0]))
    bit_weight, embed = call(
        prepare_kernel,
        "prepare",
        (bit_to_candidate, bit_to_gate, gate_bias[None], embed),
        [array(LANES, 2 * channels, BF16), array(bands * band_tokens, embed_width, BF16)],
        moved=8 * MIB,
    )
    embed, *rows_halo = lax.optimization_barrier((embed, *halo[:2]))
    halo = (*rows_halo, *halo[2:])
    embed = lax.all_to_all(embed.reshape(bands, band_tokens, -1), "ctx", 0, 0).reshape(-1, embed_width)

    count = (rows + 2 * HALF) * (cols + 2 * HALF)
    flops = 15 * rows * cols * HALF * 2 * channels * channels
    exact, partial, flags, *new_sides = call(
        functools.partial(first_kernel, cols),
        "rounds",
        (*sides[:2], *halo, region_assign, bit_weight, conv, gate_weight),
        [array(rows * cols, channels, F32), array(band_tokens, channels, BF16), array(count, LANES, BF16)]
        + side_arrays(half, channels),
        patch_scratch(rows, cols, channels)
        + [
            pltpu.VMEM((count, LANES), F32), pltpu.VMEM(conv.shape, BF16), pltpu.VMEM(gate_weight.shape, BF16),
            pltpu.SemaphoreType.DMA((2,)),
        ],
        in_hbm=(12, 13),
        flops=flops,
    )

    partial, embed = lax.optimization_barrier((partial, embed))
    pieces = lax.all_to_all(partial.reshape(tiles, -1, channels), "tile", 0, 0)
    (chunks,) = call(
        functools.partial(chunk_kernel, tiles),
        "chunk",
        (pieces.reshape(band_tokens, channels),),
        [array(bands * band_tokens, channels, BF16)],
        grant=8,
    )
    sums = lax.all_to_all(chunks.reshape(bands * tiles, -1, channels), ("ctx", "tile"), 0, 0)
    halo = exchange(new_sides)

    layer = (
        pool_weight, key_weight, value_weight, query_weight, out_weight, mlp_up, mlp_down, return_weight, conv,
        gate_weight,
    )
    blocks = (cols + 2 * HALF) // 2
    layer_rows = band_tokens + HALF * ((blocks + 7) // 8 * 8)
    all_tokens = bands * band_tokens
    state, context = call(
        functools.partial(second_kernel, cols, bands),
        "context",
        (
            lax.axis_index("ctx").reshape(1), exact, *halo, flags, sums.reshape(all_tokens, channels), embed,
            attn_norm_gain[None], mlp_norm_gain[None], bit_weight, *layer,
        ),
        [array(rows * cols, channels, BF16), array(band_tokens, embed_width, BF16)],
        patch_scratch(rows, cols, channels)
        + [pltpu.VMEM(weight.shape, BF16) for weight in layer]
        + [
            pltpu.VMEM((all_tokens, embed_width), F32), pltpu.VMEM((all_tokens, embed_width), BF16),
            pltpu.VMEM((all_tokens, embed_width), BF16), pltpu.VMEM((all_tokens, embed_width), BF16),
            pltpu.VMEM((count, LANES), F32),
            pltpu.VMEM((layer_rows, embed_width), F32), pltpu.VMEM((layer_rows, embed_width), BF16),
            pltpu.VMEM((layer_rows, embed_width), BF16), pltpu.VMEM((layer_rows, mlp_up.shape[1]), BF16),
            pltpu.VMEM((layer_rows, embed_width), BF16), pltpu.SemaphoreType.DMA((len(layer),)),
        ],
        in_hbm=range(16, 16 + len(layer)),
        scalars=(0,),
        flops=2 * flops,
    )
    return (state.reshape(rows, cols, channels), context)


def solution(mesh):
    return jax.shard_map(
        local,
        mesh=mesh,
        in_specs=(
            P(None, None, "ctx", "tile"),
            P("ctx", "tile"),
            P("ctx", "tile", None),
            P(), P(), P(), P(), P(), P(),
            P("ctx", None),
            P(), P(), P(), P(), P(), P(), P(), P(), P(),
        ),
        out_specs=(P("ctx", "tile", None), P("ctx", None)),
        check_vma=False,
    )
```

```python
import functools
import math

import jax
import jax.numpy as jnp
from jax import lax
from jax.experimental import pallas as pl
from jax.experimental.pallas import tpu as pltpu
from jax.sharding import PartitionSpec as P

HEADS = 8
HDIM = 128
ROUNDS = 8
HALF = ROUNDS // 2
LANES = 128
F32 = jnp.float32
BF16 = jnp.bfloat16
MIB = 2**20

REGION_LANE, LOW_LANE, ONE_LANE = 2 * ROUNDS, 32, 64


def shifted(value, axis, step):
    size = lax.axis_size(axis)
    pairs = [(i, i + step) for i in range(size) if 0 <= i + step < size]
    return lax.ppermute(value, axis, pairs)


def row_halo(top, bottom):
    return shifted(bottom, "ctx", 1), shifted(top, "ctx", -1)


def col_halo(cols, above, top, bottom, below):
    rows = 4 * top.shape[0] // cols
    first, last = call(
        functools.partial(edges_kernel, cols),
        "edges",
        (above, top, bottom, below),
        [array(rows * HALF, top.shape[1], BF16)] * 2,
        grant=8,
    )
    return shifted(last, "tile", 1), shifted(first, "tile", -1)


def matmul(left, right):
    return jnp.dot(left, right, preferred_element_type=F32)


def matmul_nt(left, right):
    return lax.dot_general(left, right, (((1,), (1,)), ((), ())), preferred_element_type=F32)


def two_parts(values):
    high = values.astype(BF16)
    return high, (values - high.astype(F32)).astype(BF16)


def select(member, values):
    high, low = two_parts(values)
    return matmul(member, high) + matmul(member, low)


def rms_norm(values, gain):
    return values * lax.rsqrt(jnp.mean(values * values, axis=-1, keepdims=True) + 1e-05) * gain


def iota(shape, dim):
    return lax.broadcasted_iota(jnp.int32, shape, dim)


def one_hot(condition):
    return jnp.where(condition, 1.0, 0.0).astype(BF16)


def call(kernel, name, operands, outs, scratch=(), in_hbm=(), scalars=(), grant=60, flops=0, moved=MIB):
    def spec(index):
        if index in in_hbm:
            return pl.BlockSpec(memory_space=pltpu.HBM)
        return pl.BlockSpec(memory_space=pltpu.SMEM if index in scalars else pltpu.VMEM)

    return pl.pallas_call(
        kernel,
        out_shape=outs,
        in_specs=[spec(index) for index in range(len(operands))],
        out_specs=[pl.BlockSpec(memory_space=pltpu.VMEM)] * len(outs),
        scratch_shapes=scratch,
        compiler_params=pltpu.CompilerParams(vmem_limit_bytes=grant * MIB),
        cost_estimate=pl.CostEstimate(flops=flops, bytes_accessed=moved, transcendentals=0),
        name=name,
    )(*operands)


def array(count, lanes, dtype):
    return jax.ShapeDtypeStruct((count, lanes), dtype)


def edges_kernel(cols, *refs):
    parts, (first, last) = refs[:-2], refs[-2:]
    firsts, lasts = [], []
    for part in parts:
        values = part[...].astype(F32)
        for at in range(0, part.shape[0], cols):
            firsts.append(values[at : at + HALF])
            lasts.append(values[at + cols - HALF : at + cols])
    first[...] = jnp.concatenate(firsts).astype(BF16)
    last[...] = jnp.concatenate(lasts).astype(BF16)


def write_halves(top, bottom, r, values):
    half, count = (top, bottom)[r // HALF], values.shape[0]
    half[r % HALF * count : (r % HALF + 1) * count] = values.astype(BF16)


def message_kernel(syndrome, region, state, top, bottom):
    planes, rows, cols = syndrome.shape
    bits = syndrome[...].reshape(planes * rows, cols).astype(F32).astype(BF16)
    column_bits = matmul_nt(one_hot(iota((cols, cols), 0) == iota((cols, cols), 1)), bits).astype(BF16)
    block_rows, block_cols = region.shape
    regions = jnp.concatenate([region[...].astype(F32), jnp.zeros((8 - block_rows, block_cols), F32)])
    spread = one_hot(iota((cols, block_cols), 0) // 2 == iota((cols, block_cols), 1))
    column_region = matmul_nt(spread, regions.astype(BF16)).astype(BF16)
    plane, lane = iota((planes * rows, LANES), 0), iota((planes * rows, LANES), 1)
    ones = jnp.where((iota((cols, LANES), 1) == ONE_LANE) | (iota((cols, LANES), 1) == ONE_LANE + 1), 1.0, 0.0)
    for r in range(rows):
        place = one_hot((plane == lane * rows + r) | (plane == (lane - LOW_LANE) * rows + r))
        region_place = one_hot((iota((8, LANES), 0) == r // 2) & (iota((8, LANES), 1) == REGION_LANE))
        flags = matmul(column_bits, place) + matmul(column_region, region_place) + ones
        cells = jnp.concatenate([state[r * cols : (r + 1) * cols], flags.astype(BF16)], axis=1)
        write_halves(top, bottom, r, cells)


def fetch(sources, targets, sems):
    copies = [pltpu.make_async_copy(*pair, sems.at[i]) for i, pair in enumerate(zip(sources, targets))]
    for copy in copies:
        copy.start()
    return copies


def prepare_kernel(candidate_bits, gate_bits, bias, embed, bit_weight, spread):
    by_bit = jnp.concatenate([candidate_bits[...], gate_bits[...]], axis=1)
    bias = jnp.concatenate([jnp.zeros_like(bias), bias[...]], axis=1)
    lane = iota((LANES, 1), 0)
    weight = jnp.zeros(bit_weight.shape, F32)
    for part in range(2):
        begin = (0, LOW_LANE)[part]
        for bit in range(2):
            row = two_parts(by_bit[bit : bit + 1])[part].astype(F32)
            here = (lane >= begin) & (lane < begin + 2 * ROUNDS) & (lane % 2 == bit)
            weight = jnp.where(here, row, weight)
        weight = jnp.where(lane == ONE_LANE + part, two_parts(bias)[part].astype(F32), weight)
    bit_weight[...] = weight.astype(BF16)
    for at in range(0, spread.shape[0], embed.shape[0]):
        spread[at : at + embed.shape[0]] = embed[...]


class Patch:
    def __init__(self, cols, state, taps, bits, mask):
        self.cols, self.span, self.width = cols, cols + 2 * HALF, HALF
        self.state, self.taps, self.bits, self.mask = state, taps, bits, mask
        self.groups, self.count = state.shape[:2]
        self.rows, self.channels = self.count // self.span, self.groups * LANES

    def get(self, at):
        return jnp.concatenate([self.state[j, at] for j in range(self.groups)], axis=1)

    def put(self, at, values):
        for j in range(self.groups):
            self.state[j, at] = values[:, j * LANES : (j + 1) * LANES]

    def fill(self, parts, halo, put):
        above, below, left, right = halo
        parts = (above, *parts, below)
        r = 0
        for part in parts:
            for at in range(0, part.shape[0], self.cols):
                put(pl.ds(r * self.span + self.width, self.cols), part[at : at + self.cols].astype(F32))
                r += 1
        for part, first in ((left, 0), (right, self.width + self.cols)):
            values = part[...].astype(F32)
            for r in range(self.rows):
                put(pl.ds(r * self.span + first, self.width), values[r * self.width : (r + 1) * self.width])

    def keep(self, slot, first, values):
        size = values.shape[0]
        mask = self.mask[first : first + size]
        values = jnp.concatenate([values[:, c : c + LANES] * mask for c in range(0, self.channels, LANES)], axis=1)
        for b in range(3):
            moved = values if b == 1 else pltpu.roll(values, 1 if b == 0 else size - 1, 0)
            self.taps[slot, first : first + size, b * self.channels : (b + 1) * self.channels] = moved.astype(BF16)

    def begin(self):
        part = self.count // 2
        for first in range(0, self.count, part):
            self.keep(0, first, self.get(pl.ds(first, part)))

    def advance(self, first_round, flags, conv, gate_weight, bit_weight):
        span, channels, rows = self.span, self.channels, self.rows
        lane = iota((1, LANES), 1)
        for step in range(HALF):
            t, slot = first_round + step, step % 2
            now = (lane == 2 * t) | (lane == 2 * t + 1) | (lane == LOW_LANE + 2 * t) | (lane == LOW_LANE + 2 * t + 1)
            self.bits[...] = flags[...] * one_hot(now | (lane >= ONE_LANE))
            total = rows - 2 * (step + 1)
            for begin, part_rows in ((step + 1, total),):
                first, size = begin * span, part_rows * span
                columns = jnp.concatenate(
                    [self.taps[slot, first + a * span : first + a * span + size] for a in (-1, 0, 1)], axis=1
                )
                flag = self.bits[first : first + size]
                rounded = self.taps[slot, first : first + size, channels : 2 * channels]
                candidate = matmul(columns, conv[...]) + matmul(flag, bit_weight[:, :channels])
                gate = matmul(rounded, gate_weight[...]) + matmul(flag, bit_weight[:, channels:])
                before = self.get(pl.ds(first, size))
                after = before + (0.5 * jnp.tanh(0.5 * gate) + 0.5) * (jnp.tanh(candidate) - before)
                self.put(pl.ds(first, size), after)
                if step < HALF - 1:
                    self.keep(1 - slot, first, after)

    def own(self, r):
        return self.get(pl.ds((self.width + r) * self.span + self.width, self.cols))


def patch_scratch(rows, cols, channels):
    count = (rows + 2 * HALF) * (cols + 2 * HALF)
    return [
        pltpu.VMEM((channels // LANES, count, LANES), F32),
        pltpu.VMEM((2, count, 3 * channels), BF16),
        pltpu.VMEM((count, LANES), BF16),
        pltpu.VMEM((count, LANES), F32),
    ]


def mask_of(flags):
    return matmul(flags, one_hot(iota((LANES, LANES), 0) == ONE_LANE))


def first_kernel(cols, top, bottom, *refs):
    halo, (region, bit_weight, conv_hbm, gate_hbm) = refs[:4], refs[4:8]
    exact, partial, flags, new_top, new_bottom = refs[8:13]
    state, taps, bits, mask, flags_wide, conv, gate_weight, sems = refs[13:]
    copies = fetch((conv_hbm, gate_hbm), (conv, gate_weight), sems)
    patch = Patch(cols, state, taps, bits, mask)
    channels = patch.channels

    def put(at, values):
        patch.put(at, values[:, :channels])
        flags_wide[at] = values[:, channels:]

    patch.fill((top, bottom), halo, put)
    flags[...] = flags_wide[...].astype(BF16)
    mask[...] = mask_of(flags[...])
    patch.begin()
    for copy in copies:
        copy.wait()
    patch.advance(0, flags, conv, gate_weight, bit_weight)

    own = patch.rows - 2 * patch.width
    for r in range(own):
        values = patch.own(r)
        exact[r * cols : (r + 1) * cols] = values
        write_halves(new_top, new_bottom, r, values)
    block_cols = cols // 2
    total = jnp.zeros(partial.shape, F32)
    for r in range(0, own, 2):
        begin = (patch.width + r) * patch.span + patch.width
        parts = [
            patch.get(pl.ds(begin + a * patch.span + b, block_cols, stride=2)) for a in range(2) for b in range(2)
        ]
        pooled = (sum(parts[1:], parts[0]) * 0.25).astype(BF16)
        member = one_hot(iota((partial.shape[0], block_cols), 0) == region[r // 2 : r // 2 + 1])
        total = total + matmul(member, pooled)
    partial[...] = total.astype(BF16)


def chunk_kernel(tiles, pieces, out):
    values = pieces[...].astype(F32)
    chunk = values.shape[0] // tiles
    total = values[:chunk]
    for p in range(1, tiles):
        total = total + values[p * chunk : (p + 1) * chunk]
    total = total.astype(BF16)
    for p in range(out.shape[0] // chunk):
        out[p * chunk : (p + 1) * chunk] = total


def second_kernel(
    cols, bands, band_index, exact, above, below, left, right, flags, sums, embed, attn_gain, mlp_gain, bit_weight,
    pool_hbm, key_hbm, value_hbm, query_hbm, out_hbm, up_hbm, down_hbm, return_hbm, conv_hbm, gate_hbm,
    state_out, context_out,
    state, taps, bits, mask, pool_weight, key_weight, value_weight, query_weight, out_weight, up_weight,
    down_weight, return_weight, conv, gate_weight,
    tokens_all, normed_all, keys, values, member, tokens, normed, attention, hidden, context, sems,
):
    copies = fetch(
        (pool_hbm, key_hbm, value_hbm, query_hbm, out_hbm, up_hbm, down_hbm, return_hbm, conv_hbm, gate_hbm),
        (pool_weight, key_weight, value_weight, query_weight, out_weight, up_weight, down_weight, return_weight,
         conv, gate_weight),
        sems,
    )
    patch = Patch(cols, state, taps, bits, mask)
    patch.fill((exact,), (above, below, left, right), patch.put)
    mask[...] = mask_of(flags[...])
    region = matmul(flags[...], one_hot(iota((LANES, LANES), 0) == REGION_LANE))
    member[...] = jnp.where(region == iota(region.shape, 1).astype(F32), 1.0, 0.0)

    band_tokens = sums.shape[0] // bands
    copies[0].wait()
    for band in range(bands):
        at = pl.ds(band * band_tokens, band_tokens)
        total = embed[at].astype(F32) + matmul(sums[at], pool_weight[...])
        tokens_all[at] = total
        normed_all[at] = rms_norm(total, attn_gain[...]).astype(BF16)

    g = band_index[0]
    own = pl.ds(pl.multiple_of(g * band_tokens, band_tokens), band_tokens)
    tokens[:band_tokens] = tokens_all[own]
    normed[:band_tokens] = normed_all[own]
    blocks = patch.span // 2
    room = (blocks + 7) // 8 * 8
    block_rows = patch.width // 2
    side = room * block_rows
    for number, (band, row) in enumerate(
        ((jnp.maximum(g - 1, 0), 0), (jnp.minimum(g + 1, bands - 1), patch.rows - patch.width))
    ):
        pick = jnp.concatenate(
            [member[pl.ds((row + 2 * r) * patch.span, room, stride=2)] for r in range(block_rows)]
        ).astype(BF16)
        at = pl.ds(pl.multiple_of(band * band_tokens, band_tokens), band_tokens)
        into = pl.ds(band_tokens + number * side, side)
        tokens[into] = select(pick, tokens_all[at])
        normed[into] = matmul(pick, normed_all[at]).astype(BF16)

    copies[1].wait()
    keys[...] = matmul(normed_all[...], key_weight[...]).astype(BF16)
    copies[2].wait()
    values[...] = matmul(normed_all[...], value_weight[...]).astype(BF16)
    copies[3].wait()
    queries = matmul(normed[...], query_weight[...]).astype(BF16)
    for head in range(HEADS):
        at = slice(head * HDIM, (head + 1) * HDIM)
        scores = matmul_nt(queries[:, at], keys[:, at]) * (1.0 / math.sqrt(HDIM))
        weights = jnp.exp(scores - jnp.max(scores, axis=-1, keepdims=True))
        denominator = jnp.sum(weights, axis=-1, keepdims=True)
        attention[:, at] = (matmul(weights.astype(BF16), values[:, at]) / denominator).astype(BF16)
    copies[4].wait()
    attended = tokens[...] + matmul(attention[...], out_weight[...])
    tokens[...] = attended
    normed[...] = rms_norm(attended, mlp_gain[...]).astype(BF16)
    copies[5].wait()
    part = 512
    for at in range(0, up_weight.shape[1], part):
        hidden[:, at : at + part] = jax.nn.gelu(matmul(normed[...], up_weight[:, at : at + part])).astype(BF16)
    copies[6].wait()
    context[...] = (tokens[...] + matmul(hidden[...], down_weight[...])).astype(BF16)
    context_out[...] = context[:band_tokens]
    copies[7].wait()
    returned = matmul(context[...], return_weight[...])

    first, last = patch.width * patch.span, (patch.rows - patch.width) * patch.span
    middle = pl.ds(first, last - first)
    patch.put(middle, patch.get(middle) + select(member[first:last].astype(BF16), returned[:band_tokens]))
    for number, row in enumerate((0, patch.rows - patch.width)):
        for r in range(patch.width):
            start = band_tokens + number * side + r // 2 * room
            share = returned[start : start + blocks]
            for c in range(2):
                at = pl.ds((row + r) * patch.span + c, blocks, stride=2)
                patch.put(at, patch.get(at) + share)

    copies[8].wait()
    copies[9].wait()
    patch.begin()
    patch.advance(HALF, flags, conv, gate_weight, bit_weight)
    for r in range(patch.rows - 2 * patch.width):
        state_out[r * cols : (r + 1) * cols] = patch.own(r).astype(BF16)


def local(
    syndrome_bits, region_assign, state_in, bit_to_candidate, bit_to_gate, conv_weight, gate_weight, gate_bias,
    pool_weight, region_embed, attn_norm_gain, query_weight, key_weight, value_weight, out_weight, mlp_norm_gain,
    mlp_up, mlp_down, return_weight,
):
    rows, cols, channels = state_in.shape
    band_tokens, embed_width = region_embed.shape
    bands, tiles = lax.axis_size("ctx"), lax.axis_size("tile")
    conv = conv_weight.reshape(9 * channels, channels)
    half = HALF * cols

    top, bottom = call(
        message_kernel,
        "message",
        (syndrome_bits.reshape(2 * ROUNDS, rows, cols), region_assign, state_in.reshape(rows * cols, channels)),
        [array(half, channels + LANES, BF16)] * 2,
    )
    above, below = row_halo(top, bottom)
    embed, _ = lax.optimization_barrier((region_embed, top))
    bit_weight, embed = call(
        prepare_kernel,
        "prepare",
        (bit_to_candidate, bit_to_gate, gate_bias[None], embed),
        [array(LANES, 2 * channels, BF16), array(bands * band_tokens, embed_width, BF16)],
        moved=8 * MIB,
    )
    embed, bit_weight, above, below = lax.optimization_barrier((embed, bit_weight, above, below))
    left, right = col_halo(cols, above, top, bottom, below)
    embed = lax.all_to_all(embed.reshape(bands, band_tokens, -1), "ctx", 0, 0).reshape(-1, embed_width)

    count = (rows + 2 * HALF) * (cols + 2 * HALF)
    flops = 15 * rows * cols * HALF * 2 * channels * channels
    exact, partial, flags, top, bottom = call(
        functools.partial(first_kernel, cols),
        "rounds",
        (top, bottom, above, below, left, right, region_assign, bit_weight, conv, gate_weight),
        [array(rows * cols, channels, F32), array(band_tokens, channels, BF16), array(count, LANES, BF16)]
        + [array(half, channels, BF16)] * 2,
        patch_scratch(rows, cols, channels)
        + [
            pltpu.VMEM((count, LANES), F32), pltpu.VMEM(conv.shape, BF16), pltpu.VMEM(gate_weight.shape, BF16),
            pltpu.SemaphoreType.DMA((2,)),
        ],
        in_hbm=(8, 9),
        flops=flops,
    )

    partial, embed = lax.optimization_barrier((partial, embed))
    pieces = lax.all_to_all(partial.reshape(tiles, -1, channels), "tile", 0, 0)
    above, below = row_halo(top, bottom)
    pieces, above, below = lax.optimization_barrier((pieces, above, below))
    (chunks,) = call(
        functools.partial(chunk_kernel, tiles),
        "chunk",
        (pieces.reshape(band_tokens, channels),),
        [array(bands * band_tokens, channels, BF16)],
        grant=8,
    )
    sums = lax.all_to_all(chunks.reshape(bands * tiles, -1, channels), ("ctx", "tile"), 0, 0)
    above, below, _ = lax.optimization_barrier((above, below, chunks))
    left, right = col_halo(cols, above, top, bottom, below)

    layer = (
        pool_weight, key_weight, value_weight, query_weight, out_weight, mlp_up, mlp_down, return_weight, conv,
        gate_weight,
    )
    blocks = (cols + 2 * HALF) // 2
    layer_rows = band_tokens + HALF * ((blocks + 7) // 8 * 8)
    all_tokens = bands * band_tokens
    state, context = call(
        functools.partial(second_kernel, cols, bands),
        "context",
        (
            lax.axis_index("ctx").reshape(1), exact, above, below, left, right, flags,
            sums.reshape(all_tokens, channels), embed, attn_norm_gain[None], mlp_norm_gain[None], bit_weight, *layer,
        ),
        [array(rows * cols, channels, BF16), array(band_tokens, embed_width, BF16)],
        patch_scratch(rows, cols, channels)
        + [pltpu.VMEM(weight.shape, BF16) for weight in layer]
        + [
            pltpu.VMEM((all_tokens, embed_width), F32), pltpu.VMEM((all_tokens, embed_width), BF16),
            pltpu.VMEM((all_tokens, embed_width), BF16), pltpu.VMEM((all_tokens, embed_width), BF16),
            pltpu.VMEM((count, LANES), F32),
            pltpu.VMEM((layer_rows, embed_width), F32), pltpu.VMEM((layer_rows, embed_width), BF16),
            pltpu.VMEM((layer_rows, embed_width), BF16), pltpu.VMEM((layer_rows, mlp_up.shape[1]), BF16),
            pltpu.VMEM((layer_rows, embed_width), BF16), pltpu.SemaphoreType.DMA((len(layer),)),
        ],
        in_hbm=range(12, 12 + len(layer)),
        scalars=(0,),
        flops=2 * flops,
    )
    return (state.reshape(rows, cols, channels), context)


def solution(mesh):
    return jax.shard_map(
        local,
        mesh=mesh,
        in_specs=(
            P(None, None, "ctx", "tile"),
            P("ctx", "tile"),
            P("ctx", "tile", None),
            P(), P(), P(), P(), P(), P(),
            P("ctx", None),
            P(), P(), P(), P(), P(), P(), P(), P(), P(),
        ),
        out_specs=(P("ctx", "tile", None), P("ctx", None)),
        check_vma=False,
    )
```

```python
import functools
import math

import jax
import jax.numpy as jnp
from jax import lax
from jax.experimental import pallas as pl
from jax.experimental.pallas import tpu as pltpu
from jax.sharding import PartitionSpec as P

HEADS = 8
HDIM = 128
ROUNDS = 8
HALF = ROUNDS // 2
LANES = 128
F32 = jnp.float32
BF16 = jnp.bfloat16
MIB = 2**20

TILE = ("chip", "core")

REGION_LANE, LOW_LANE, ONE_LANE = 2 * ROUNDS, 32, 64


def shifted(value, axis, step):
    size = math.prod(lax.axis_size(name) for name in axis)
    pairs = [(i, i + step) for i in range(size) if 0 <= i + step < size]
    return lax.ppermute(value, axis, pairs)


def row_halo(top, bottom):
    return shifted(bottom, ("ctx",), 1), shifted(top, ("ctx",), -1)


def col_halo(cols, above, first, last, below):
    count, lanes = first.shape
    first, last = call(
        functools.partial(edges_kernel, cols),
        "edges",
        (above, first, last, below),
        [array(2 * count, lanes, BF16)] * 2,
        grant=8,
    )
    return shifted(last, TILE, 1), shifted(first, TILE, -1)


def matmul(left, right):
    return jnp.dot(left, right, preferred_element_type=F32)


def matmul_nt(left, right):
    return lax.dot_general(left, right, (((1,), (1,)), ((), ())), preferred_element_type=F32)


def two_parts(values):
    high = values.astype(BF16)
    return high, (values - high.astype(F32)).astype(BF16)


def select(member, values):
    high, low = two_parts(values)
    return matmul(member, high) + matmul(member, low)


def rms_norm(values, gain):
    return values * lax.rsqrt(jnp.mean(values * values, axis=-1, keepdims=True) + 1e-05) * gain


def iota(shape, dim):
    return lax.broadcasted_iota(jnp.int32, shape, dim)


def one_hot(condition):
    return jnp.where(condition, 1.0, 0.0).astype(BF16)


def call(kernel, name, operands, outs, scratch=(), in_hbm=(), scalars=(), grant=60, flops=0, moved=MIB):
    def spec(index):
        if index in in_hbm:
            return pl.BlockSpec(memory_space=pltpu.HBM)
        return pl.BlockSpec(memory_space=pltpu.SMEM if index in scalars else pltpu.VMEM)

    return pl.pallas_call(
        kernel,
        out_shape=outs,
        in_specs=[spec(index) for index in range(len(operands))],
        out_specs=[pl.BlockSpec(memory_space=pltpu.VMEM)] * len(outs),
        scratch_shapes=scratch,
        compiler_params=pltpu.CompilerParams(vmem_limit_bytes=grant * MIB),
        cost_estimate=pl.CostEstimate(flops=flops, bytes_accessed=moved, transcendentals=0),
        name=name,
    )(*operands)


def array(count, lanes, dtype):
    return jax.ShapeDtypeStruct((count, lanes), dtype)


def first_columns(part, cols, begin):
    values = part[...].astype(F32)
    return [values[at + begin : at + begin + HALF] for at in range(0, part.shape[0], cols)]


def edges_kernel(cols, above, own_first, own_last, below, first, last):
    for own, begin, out in ((own_first, 0, first), (own_last, cols - HALF, last)):
        parts = first_columns(above, cols, begin) + [own[...].astype(F32)] + first_columns(below, cols, begin)
        out[...] = jnp.concatenate(parts).astype(BF16)


def patch_outputs(half, lanes):
    return [array(half, lanes, BF16)] * 2 + [array(2 * HALF * HALF, lanes, BF16)] * 2


def write_patch(outs, rows):
    top, bottom, first, last = outs
    cols = rows[0].shape[0]
    for r, values in enumerate(rows):
        half = (top, bottom)[r // HALF]
        half[r % HALF * cols : (r % HALF + 1) * cols] = values.astype(BF16)
    first[...] = jnp.concatenate([values[:HALF] for values in rows]).astype(BF16)
    last[...] = jnp.concatenate([values[cols - HALF :] for values in rows]).astype(BF16)


def message_kernel(syndrome, region, state, *outs):
    planes, rows, cols = syndrome.shape
    bits = syndrome[...].reshape(planes * rows, cols).astype(F32).astype(BF16)
    column_bits = matmul_nt(one_hot(iota((cols, cols), 0) == iota((cols, cols), 1)), bits).astype(BF16)
    block_rows, block_cols = region.shape
    regions = jnp.concatenate([region[...].astype(F32), jnp.zeros((8 - block_rows, block_cols), F32)])
    spread = one_hot(iota((cols, block_cols), 0) // 2 == iota((cols, block_cols), 1))
    column_region = matmul_nt(spread, regions.astype(BF16)).astype(BF16)
    plane, lane = iota((planes * rows, LANES), 0), iota((planes * rows, LANES), 1)
    ones = jnp.where((iota((cols, LANES), 1) == ONE_LANE) | (iota((cols, LANES), 1) == ONE_LANE + 1), 1.0, 0.0)
    cells = []
    for r in range(rows):
        place = one_hot((plane == lane * rows + r) | (plane == (lane - LOW_LANE) * rows + r))
        region_place = one_hot((iota((8, LANES), 0) == r // 2) & (iota((8, LANES), 1) == REGION_LANE))
        flags = matmul(column_bits, place) + matmul(column_region, region_place) + ones
        cells.append(jnp.concatenate([state[r * cols : (r + 1) * cols].astype(F32), flags], axis=1))
    write_patch(outs, cells)


def fetch(sources, targets, sems):
    copies = [pltpu.make_async_copy(*pair, sems.at[i]) for i, pair in enumerate(zip(sources, targets))]
    for copy in copies:
        copy.start()
    return copies


def prepare_kernel(candidate_bits, gate_bits, bias, embed, bit_weight, spread):
    by_bit = jnp.concatenate([candidate_bits[...], gate_bits[...]], axis=1)
    bias = jnp.concatenate([jnp.zeros_like(bias), bias[...]], axis=1)
    lane = iota((LANES, 1), 0)
    weight = jnp.zeros(bit_weight.shape, F32)
    for part in range(2):
        begin = (0, LOW_LANE)[part]
        for bit in range(2):
            row = two_parts(by_bit[bit : bit + 1])[part].astype(F32)
            here = (lane >= begin) & (lane < begin + 2 * ROUNDS) & (lane % 2 == bit)
            weight = jnp.where(here, row, weight)
        weight = jnp.where(lane == ONE_LANE + part, two_parts(bias)[part].astype(F32), weight)
    bit_weight[...] = weight.astype(BF16)
    for at in range(0, spread.shape[0], embed.shape[0]):
        spread[at : at + embed.shape[0]] = embed[...]


class Patch:
    def __init__(self, cols, state, taps, bits, mask):
        self.cols, self.span, self.width = cols, cols + 2 * HALF, HALF
        self.state, self.taps, self.bits, self.mask = state, taps, bits, mask
        self.groups, self.count = state.shape[:2]
        self.rows, self.channels = self.count // self.span, self.groups * LANES

    def get(self, at):
        return jnp.concatenate([self.state[j, at] for j in range(self.groups)], axis=1)

    def put(self, at, values):
        for j in range(self.groups):
            self.state[j, at] = values[:, j * LANES : (j + 1) * LANES]

    def fill(self, parts, halo, put):
        above, below, left, right = halo
        parts = (above, *parts, below)
        r = 0
        for part in parts:
            for at in range(0, part.shape[0], self.cols):
                put(pl.ds(r * self.span + self.width, self.cols), part[at : at + self.cols].astype(F32))
                r += 1
        for part, first in ((left, 0), (right, self.width + self.cols)):
            values = part[...].astype(F32)
            for r in range(self.rows):
                put(pl.ds(r * self.span + first, self.width), values[r * self.width : (r + 1) * self.width])

    def keep(self, slot, first, values):
        size = values.shape[0]
        mask = self.mask[first : first + size]
        values = jnp.concatenate([values[:, c : c + LANES] * mask for c in range(0, self.channels, LANES)], axis=1)
        for b in range(3):
            moved = values if b == 1 else pltpu.roll(values, 1 if b == 0 else size - 1, 0)
            self.taps[slot, first : first + size, b * self.channels : (b + 1) * self.channels] = moved.astype(BF16)

    def begin(self):
        part = self.count // 2
        for first in range(0, self.count, part):
            self.keep(0, first, self.get(pl.ds(first, part)))

    def advance(self, first_round, flags, conv, gate_weight, bit_weight, waits):
        span, channels, rows = self.span, self.channels, self.rows
        lane = iota((1, LANES), 1)
        for step in range(HALF):
            t, slot = first_round + step, step % 2
            now = (lane == 2 * t) | (lane == 2 * t + 1) | (lane == LOW_LANE + 2 * t) | (lane == LOW_LANE + 2 * t + 1)
            self.bits[...] = flags[...] * one_hot(now | (lane >= ONE_LANE))
            total = rows - 2 * (step + 1)
            for begin, part_rows in ((step + 1, total),):
                first, size = begin * span, part_rows * span
                parts = [self.taps[slot, first + a * span : first + a * span + size] for a in (-1, 0, 1)]
                flag = self.bits[first : first + size]
                rounded = self.taps[slot, first : first + size, channels : 2 * channels]
                candidate = matmul(flag, bit_weight[:, :channels])
                if step == 0:
                    third = conv.shape[0] // 3
                    for a in range(3):
                        waits[a].wait()
                        candidate = candidate + matmul(parts[a], conv[a * third : (a + 1) * third])
                    waits[3].wait()
                else:
                    candidate = candidate + matmul(jnp.concatenate(parts, axis=1), conv[...])
                gate = matmul(rounded, gate_weight[...]) + matmul(flag, bit_weight[:, channels:])
                before = self.get(pl.ds(first, size))
                after = before + (0.5 * jnp.tanh(0.5 * gate) + 0.5) * (jnp.tanh(candidate) - before)
                self.put(pl.ds(first, size), after)
                if step < HALF - 1:
                    self.keep(1 - slot, first, after)

    def own(self, r):
        return self.get(pl.ds((self.width + r) * self.span + self.width, self.cols))


def patch_scratch(rows, cols, channels):
    count = (rows + 2 * HALF) * (cols + 2 * HALF)
    return [
        pltpu.VMEM((channels // LANES, count, LANES), F32),
        pltpu.VMEM((2, count, 3 * channels), BF16),
        pltpu.VMEM((count, LANES), BF16),
        pltpu.VMEM((count, LANES), F32),
    ]


def mask_of(flags):
    return matmul(flags, one_hot(iota((LANES, LANES), 0) == ONE_LANE))


def thirds(ref):
    size = ref.shape[0] // 3
    return [ref.at[a * size : (a + 1) * size] for a in range(3)]


def first_kernel(cols, tiles, top, bottom, *refs):
    halo, (region, bit_weight, conv_hbm, gate_hbm) = refs[:4], refs[4:8]
    (exact, partial, flags), new_patch = refs[8:11], refs[11:15]
    state, taps, bits, mask, flags_wide, conv, gate_weight, sems = refs[15:]
    copies = fetch((*thirds(conv_hbm), gate_hbm), (*thirds(conv), gate_weight), sems)
    patch = Patch(cols, state, taps, bits, mask)
    channels = patch.channels

    def put(at, values):
        patch.put(at, values[:, :channels])
        flags_wide[at] = values[:, channels:]

    patch.fill((top, bottom), halo, put)
    flags[...] = flags_wide[...].astype(BF16)
    mask[...] = mask_of(flags[...])
    patch.begin()
    patch.advance(0, flags, conv, gate_weight, bit_weight, copies)

    own = patch.rows - 2 * patch.width
    cells = [patch.own(r) for r in range(own)]
    for r in range(own):
        exact[r * cols : (r + 1) * cols] = cells[r]
    write_patch(new_patch, cells)
    block_cols = cols // 2
    total = jnp.zeros(partial.shape, F32)
    for r in range(0, own, 2):
        begin = (patch.width + r) * patch.span + patch.width
        parts = [
            patch.get(pl.ds(begin + a * patch.span + b, block_cols, stride=2)) for a in range(2) for b in range(2)
        ]
        pooled = (sum(parts[1:], parts[0]) * 0.25).astype(BF16)
        member = one_hot(iota((partial.shape[0], block_cols), 0) == region[r // 2 : r // 2 + 1])
        total = total + matmul(member, pooled)
    chunk = total.shape[0] // tiles
    for tile in range(tiles):
        at = (tile % 2 * (tiles // 2) + tile // 2) * chunk
        partial[tile * chunk : (tile + 1) * chunk] = total[at : at + chunk].astype(BF16)


def chunk_kernel(tiles, pieces, out):
    values = pieces[...].astype(F32)
    chunk = values.shape[0] // tiles
    total = values[:chunk]
    for p in range(1, tiles):
        total = total + values[p * chunk : (p + 1) * chunk]
    total = total.astype(BF16)
    for p in range(out.shape[0] // chunk):
        out[p * chunk : (p + 1) * chunk] = total


def second_kernel(cols, bands, place, sums, other_sums, attn_gain, mlp_gain, *refs):
    sources, (state_out, context_out) = refs[:18], refs[18:20]
    state, taps, bits, mask, tokens_all, normed_all, keys, values, member, tokens, normed, attention = refs[20:32]
    hidden, context, sems = refs[32:35]
    targets = refs[35:]
    embed, flags, exact, above, below, left, right, bit_weight = targets[1:9]
    pool_weight, key_weight, value_weight, query_weight = targets[0], *targets[9:12]
    out_weight, up_weight, down_weight, return_weight, gate_weight, conv = targets[12:]
    copies = fetch((*sources[:-1], *thirds(sources[-1])), (*targets[:-1], *thirds(conv)), sems)
    patch = Patch(cols, state, taps, bits, mask)
    own_half = place[1]

    half_tokens = sums.shape[0] // bands
    band_tokens = 2 * half_tokens
    copies[0].wait()
    copies[1].wait()
    for band in range(bands):
        for half in range(2):
            at = pl.ds(band * half_tokens, half_tokens)
            part = jnp.where(own_half == half, sums[at].astype(F32), other_sums[at].astype(F32)).astype(BF16)
            at = pl.ds(band * band_tokens + half * half_tokens, half_tokens)
            total = embed[at].astype(F32) + matmul(part, pool_weight[...])
            tokens_all[at] = total
            normed_all[at] = rms_norm(total, attn_gain[...]).astype(BF16)

    copies[2].wait()
    mask[...] = mask_of(flags[...])
    region = matmul(flags[...], one_hot(iota((LANES, LANES), 0) == REGION_LANE))
    member[...] = jnp.where(region == iota(region.shape, 1).astype(F32), 1.0, 0.0)

    g = place[0]
    own = pl.ds(pl.multiple_of(g * band_tokens, band_tokens), band_tokens)
    tokens[:band_tokens] = tokens_all[own]
    normed[:band_tokens] = normed_all[own]
    blocks = patch.span // 2
    room = (blocks + 7) // 8 * 8
    block_rows = patch.width // 2
    side = room * block_rows
    for number, (band, row) in enumerate(
        ((jnp.maximum(g - 1, 0), 0), (jnp.minimum(g + 1, bands - 1), patch.rows - patch.width))
    ):
        pick = jnp.concatenate(
            [member[pl.ds((row + 2 * r) * patch.span, room, stride=2)] for r in range(block_rows)]
        ).astype(BF16)
        at = pl.ds(pl.multiple_of(band * band_tokens, band_tokens), band_tokens)
        into = pl.ds(band_tokens + number * side, side)
        tokens[into] = select(pick, tokens_all[at])
        normed[into] = matmul(pick, normed_all[at]).astype(BF16)

    copies[9].wait()
    keys[...] = matmul(normed_all[...], key_weight[...]).astype(BF16)
    copies[10].wait()
    values[...] = matmul(normed_all[...], value_weight[...]).astype(BF16)
    copies[11].wait()
    queries = matmul(normed[...], query_weight[...]).astype(BF16)
    for head in range(HEADS):
        at = slice(head * HDIM, (head + 1) * HDIM)
        scores = matmul_nt(queries[:, at], keys[:, at]) * (1.0 / math.sqrt(HDIM))
        weights = jnp.exp(scores - jnp.max(scores, axis=-1, keepdims=True))
        denominator = jnp.sum(weights, axis=-1, keepdims=True)
        attention[:, at] = (matmul(weights.astype(BF16), values[:, at]) / denominator).astype(BF16)
    copies[12].wait()
    attended = tokens[...] + matmul(attention[...], out_weight[...])
    tokens[...] = attended
    normed[...] = rms_norm(attended, mlp_gain[...]).astype(BF16)
    copies[13].wait()
    part = 512
    for at in range(0, up_weight.shape[1], part):
        hidden[:, at : at + part] = jax.nn.gelu(matmul(normed[...], up_weight[:, at : at + part])).astype(BF16)
    copies[14].wait()
    context[...] = (tokens[...] + matmul(hidden[...], down_weight[...])).astype(BF16)
    context_out[...] = context[:band_tokens]
    copies[15].wait()
    returned = matmul(context[...], return_weight[...])

    for copy in copies[3:9]:
        copy.wait()
    patch.fill((exact,), (above, below, left, right), patch.put)
    first, last = patch.width * patch.span, (patch.rows - patch.width) * patch.span
    middle = pl.ds(first, last - first)
    patch.put(middle, patch.get(middle) + select(member[first:last].astype(BF16), returned[:band_tokens]))
    for number, row in enumerate((0, patch.rows - patch.width)):
        for r in range(patch.width):
            start = band_tokens + number * side + r // 2 * room
            share = returned[start : start + blocks]
            for c in range(2):
                at = pl.ds((row + r) * patch.span + c, blocks, stride=2)
                patch.put(at, patch.get(at) + share)

    patch.begin()
    patch.advance(HALF, flags, conv, gate_weight, bit_weight, (*copies[17:], copies[16]))
    for r in range(patch.rows - 2 * patch.width):
        state_out[r * cols : (r + 1) * cols] = patch.own(r).astype(BF16)


def local(
    syndrome_bits, region_assign, state_in, bit_to_candidate, bit_to_gate, conv_weight, gate_weight, gate_bias,
    pool_weight, region_embed, attn_norm_gain, query_weight, key_weight, value_weight, out_weight, mlp_norm_gain,
    mlp_up, mlp_down, return_weight,
):
    rows, cols, channels = state_in.shape
    band_tokens, embed_width = region_embed.shape
    bands, tiles = lax.axis_size("ctx"), math.prod(lax.axis_size(name) for name in TILE)
    conv = conv_weight.reshape(9 * channels, channels)
    half = HALF * cols

    top, bottom, first, last = call(
        message_kernel,
        "message",
        (syndrome_bits.reshape(2 * ROUNDS, rows, cols), region_assign, state_in.reshape(rows * cols, channels)),
        patch_outputs(half, channels + LANES),
    )
    above, below = row_halo(top, bottom)
    embed, _ = lax.optimization_barrier((region_embed, top))
    bit_weight, embed = call(
        prepare_kernel,
        "prepare",
        (bit_to_candidate, bit_to_gate, gate_bias[None], embed),
        [array(LANES, 2 * channels, BF16), array(bands * band_tokens, embed_width, BF16)],
        moved=8 * MIB,
    )
    embed, bit_weight, above, below = lax.optimization_barrier((embed, bit_weight, above, below))
    left, right = col_halo(cols, above, first, last, below)
    embed = lax.all_to_all(embed.reshape(bands, band_tokens, -1), "ctx", 0, 0).reshape(-1, embed_width)

    count = (rows + 2 * HALF) * (cols + 2 * HALF)
    flops = 15 * rows * cols * HALF * 2 * channels * channels
    exact, partial, flags, top, bottom, first, last = call(
        functools.partial(first_kernel, cols, tiles),
        "rounds",
        (top, bottom, above, below, left, right, region_assign, bit_weight, conv, gate_weight),
        [array(rows * cols, channels, F32), array(band_tokens, channels, BF16), array(count, LANES, BF16)]
        + patch_outputs(half, channels),
        patch_scratch(rows, cols, channels)
        + [
            pltpu.VMEM((count, LANES), F32), pltpu.VMEM(conv.shape, BF16), pltpu.VMEM(gate_weight.shape, BF16),
            pltpu.SemaphoreType.DMA((4,)),
        ],
        in_hbm=(8, 9),
        flops=flops,
    )

    partial, embed = lax.optimization_barrier((partial, embed))
    pieces = lax.all_to_all(partial.reshape(tiles, -1, channels), TILE, 0, 0)
    above, below = row_halo(top, bottom)
    pieces, above, below = lax.optimization_barrier((pieces, above, below))
    (chunks,) = call(
        functools.partial(chunk_kernel, tiles),
        "chunk",
        (pieces.reshape(band_tokens, channels),),
        [array(bands * band_tokens // 2, channels, BF16)],
        grant=8,
    )
    sums = lax.all_to_all(chunks.reshape(bands * tiles // 2, -1, channels), ("ctx", "chip"), 0, 0)
    sums = sums.reshape(-1, channels)
    other_sums = lax.ppermute(sums, "core", [(0, 1), (1, 0)])
    above, below, _ = lax.optimization_barrier((above, below, chunks))
    left, right = col_halo(cols, above, first, last, below)

    fetched = (
        pool_weight, embed, flags, exact, above, below, left, right, bit_weight, key_weight, value_weight, query_weight,
        out_weight, mlp_up, mlp_down, return_weight, gate_weight, conv,
    )
    blocks = (cols + 2 * HALF) // 2
    layer_rows = band_tokens + HALF * ((blocks + 7) // 8 * 8)
    all_tokens = bands * band_tokens
    place = jnp.stack([lax.axis_index("ctx"), lax.axis_index("core")]).astype(jnp.int32)
    state, context = call(
        functools.partial(second_kernel, cols, bands),
        "context",
        (place, sums, other_sums, attn_norm_gain[None], mlp_norm_gain[None], *fetched),
        [array(rows * cols, channels, BF16), array(band_tokens, embed_width, BF16)],
        patch_scratch(rows, cols, channels)
        + [
            pltpu.VMEM((all_tokens, embed_width), F32), pltpu.VMEM((all_tokens, embed_width), BF16),
            pltpu.VMEM((all_tokens, embed_width), BF16), pltpu.VMEM((all_tokens, embed_width), BF16),
            pltpu.VMEM((count, LANES), F32),
            pltpu.VMEM((layer_rows, embed_width), F32), pltpu.VMEM((layer_rows, embed_width), BF16),
            pltpu.VMEM((layer_rows, embed_width), BF16), pltpu.VMEM((layer_rows, mlp_up.shape[1]), BF16),
            pltpu.VMEM((layer_rows, embed_width), BF16), pltpu.SemaphoreType.DMA((len(fetched) + 2,)),
        ]
        + [pltpu.VMEM(value.shape, value.dtype) for value in fetched],
        in_hbm=range(5, 5 + len(fetched)),
        scalars=(0,),
        flops=2 * flops,
    )
    return (state.reshape(rows, cols, channels), context)


def solution(mesh):
    bands, tiles = mesh.devices.shape
    split = jax.sharding.Mesh(mesh.devices.reshape(bands, tiles // 2, 2), ("ctx", *TILE))
    return jax.shard_map(
        local,
        mesh=split,
        in_specs=(
            P(None, None, "ctx", TILE),
            P("ctx", TILE),
            P("ctx", TILE, None),
            P(), P(), P(), P(), P(), P(),
            P("ctx", None),
            P(), P(), P(), P(), P(), P(), P(), P(), P(),
        ),
        out_specs=(P("ctx", TILE, None), P("ctx", None)),
        check_vma=False,
    )
```

```python
import functools
import math

import jax
import jax.numpy as jnp
from jax import lax
from jax.experimental import pallas as pl
from jax.experimental.pallas import tpu as pltpu
from jax.sharding import PartitionSpec as P

HEADS = 8
HDIM = 128
ROUNDS = 8
HALF = ROUNDS // 2
LANES = 128
F32 = jnp.float32
BF16 = jnp.bfloat16
MIB = 2**20

TILE = ("chip", "core")

REGION_LANE, LOW_LANE, ONE_LANE = 2 * ROUNDS, 32, 64


def shifted(value, axis, step):
    size = math.prod(lax.axis_size(name) for name in axis)
    pairs = [(i, i + step) for i in range(size) if 0 <= i + step < size]
    return lax.ppermute(value, axis, pairs)


def row_halo(top, bottom):
    return shifted(bottom, ("ctx",), 1), shifted(top, ("ctx",), -1)


def col_halo(cols, above, first, last, below):
    count, lanes = first.shape
    first, last = call(
        functools.partial(edges_kernel, cols),
        "edges",
        (above, first, last, below),
        [array(2 * count, lanes, BF16)] * 2,
        grant=8,
    )
    return shifted(last, TILE, 1), shifted(first, TILE, -1)


def matmul(left, right):
    return jnp.dot(left, right, preferred_element_type=F32)


def matmul_nt(left, right):
    return lax.dot_general(left, right, (((1,), (1,)), ((), ())), preferred_element_type=F32)


def two_parts(values):
    high = values.astype(BF16)
    return high, (values - high.astype(F32)).astype(BF16)


def select(member, values):
    high, low = two_parts(values)
    return matmul(member, high) + matmul(member, low)


def rms_norm(values, gain):
    return values * lax.rsqrt(jnp.mean(values * values, axis=-1, keepdims=True) + 1e-05) * gain


def iota(shape, dim):
    return lax.broadcasted_iota(jnp.int32, shape, dim)


def one_hot(condition):
    return jnp.where(condition, 1.0, 0.0).astype(BF16)


def call(kernel, name, operands, outs, scratch=(), in_hbm=(), scalars=(), grant=60, flops=0, moved=MIB):
    def spec(index):
        if index in in_hbm:
            return pl.BlockSpec(memory_space=pltpu.HBM)
        return pl.BlockSpec(memory_space=pltpu.SMEM if index in scalars else pltpu.VMEM)

    return pl.pallas_call(
        kernel,
        out_shape=outs,
        in_specs=[spec(index) for index in range(len(operands))],
        out_specs=[pl.BlockSpec(memory_space=pltpu.VMEM)] * len(outs),
        scratch_shapes=scratch,
        compiler_params=pltpu.CompilerParams(vmem_limit_bytes=grant * MIB),
        cost_estimate=pl.CostEstimate(flops=flops, bytes_accessed=moved, transcendentals=0),
        name=name,
    )(*operands)


def array(count, lanes, dtype):
    return jax.ShapeDtypeStruct((count, lanes), dtype)


def first_columns(part, cols, begin):
    values = part[...].astype(F32)
    return [values[at + begin : at + begin + HALF] for at in range(0, part.shape[0], cols)]


def edges_kernel(cols, above, own_first, own_last, below, first, last):
    for own, begin, out in ((own_first, 0, first), (own_last, cols - HALF, last)):
        parts = first_columns(above, cols, begin) + [own[...].astype(F32)] + first_columns(below, cols, begin)
        out[...] = jnp.concatenate(parts).astype(BF16)


def rows_kernel(top, bottom, left, right, up, down):
    sides = left[...].astype(F32), right[...].astype(F32)
    cols = top.shape[0] // HALF
    for number, (part, out) in enumerate(((top, up), (bottom, down))):
        values, cells = part[...].astype(F32), []
        for r in range(HALF):
            at = (number * HALF + r) * HALF
            before, after = (side[at : at + HALF] for side in sides)
            cells += [before, values[r * cols : (r + 1) * cols], after]
        out[...] = jnp.concatenate(cells).astype(BF16)


def patch_outputs(half, lanes):
    return [array(half, lanes, BF16)] * 2 + [array(2 * HALF * HALF, lanes, BF16)] * 2


def write_patch(outs, rows):
    top, bottom, first, last = outs
    cols = rows[0].shape[0]
    for r, values in enumerate(rows):
        half = (top, bottom)[r // HALF]
        half[r % HALF * cols : (r % HALF + 1) * cols] = values.astype(BF16)
    first[...] = jnp.concatenate([values[:HALF] for values in rows]).astype(BF16)
    last[...] = jnp.concatenate([values[cols - HALF :] for values in rows]).astype(BF16)


def message_kernel(syndrome, region, state, *outs):
    planes, rows, cols = syndrome.shape
    bits = syndrome[...].reshape(planes * rows, cols).astype(F32).astype(BF16)
    column_bits = matmul_nt(one_hot(iota((cols, cols), 0) == iota((cols, cols), 1)), bits).astype(BF16)
    block_rows, block_cols = region.shape
    regions = jnp.concatenate([region[...].astype(F32), jnp.zeros((8 - block_rows, block_cols), F32)])
    spread = one_hot(iota((cols, block_cols), 0) // 2 == iota((cols, block_cols), 1))
    column_region = matmul_nt(spread, regions.astype(BF16)).astype(BF16)
    plane, lane = iota((planes * rows, LANES), 0), iota((planes * rows, LANES), 1)
    ones = jnp.where((iota((cols, LANES), 1) == ONE_LANE) | (iota((cols, LANES), 1) == ONE_LANE + 1), 1.0, 0.0)
    cells = []
    for r in range(rows):
        place = one_hot((plane == lane * rows + r) | (plane == (lane - LOW_LANE) * rows + r))
        region_place = one_hot((iota((8, LANES), 0) == r // 2) & (iota((8, LANES), 1) == REGION_LANE))
        flags = matmul(column_bits, place) + matmul(column_region, region_place) + ones
        cells.append(jnp.concatenate([state[r * cols : (r + 1) * cols].astype(F32), flags], axis=1))
    write_patch(outs, cells)


def fetch(sources, targets, sems):
    return [pltpu.make_async_copy(*pair, sems.at[i]) for i, pair in enumerate(zip(sources, targets))]


def prepare_kernel(candidate_bits, gate_bits, bias, embed, bit_weight, spread):
    by_bit = jnp.concatenate([candidate_bits[...], gate_bits[...]], axis=1)
    bias = jnp.concatenate([jnp.zeros_like(bias), bias[...]], axis=1)
    lane = iota((LANES, 1), 0)
    weight = jnp.zeros(bit_weight.shape, F32)
    for part in range(2):
        begin = (0, LOW_LANE)[part]
        for bit in range(2):
            row = two_parts(by_bit[bit : bit + 1])[part].astype(F32)
            here = (lane >= begin) & (lane < begin + 2 * ROUNDS) & (lane % 2 == bit)
            weight = jnp.where(here, row, weight)
        weight = jnp.where(lane == ONE_LANE + part, two_parts(bias)[part].astype(F32), weight)
    bit_weight[...] = weight.astype(BF16)
    for at in range(0, spread.shape[0], embed.shape[0]):
        spread[at : at + embed.shape[0]] = embed[...]


class Patch:
    def __init__(self, cols, state, taps, bits, mask):
        self.cols, self.span, self.width = cols, cols + 2 * HALF, HALF
        self.state, self.taps, self.bits, self.mask = state, taps, bits, mask
        self.groups, self.count = state.shape[:2]
        self.rows, self.channels = self.count // self.span, self.groups * LANES

    def get(self, at):
        return jnp.concatenate([self.state[j, at] for j in range(self.groups)], axis=1)

    def put(self, at, values):
        for j in range(self.groups):
            self.state[j, at] = values[:, j * LANES : (j + 1) * LANES]

    def fill(self, parts, halo, put):
        above, below, left, right = halo
        r = 0
        for part, part_rows in (
            (above, self.width), *((part, part.shape[0] // self.cols) for part in parts), (below, self.width)
        ):
            length = part.shape[0] // part_rows
            for at in range(0, part.shape[0], length):
                put(pl.ds(r * self.span + (self.span - length) // 2, length), part[at : at + length].astype(F32))
                r += 1
        for part, first in ((left, 0), (right, self.width + self.cols)):
            values = part[...].astype(F32)
            side_rows = values.shape[0] // self.width
            for r in range(side_rows):
                at = (r + (self.rows - side_rows) // 2) * self.span + first
                put(pl.ds(at, self.width), values[r * self.width : (r + 1) * self.width])

    def keep(self, slot, first, values):
        size = values.shape[0]
        mask = self.mask[first : first + size]
        values = jnp.concatenate([values[:, c : c + LANES] * mask for c in range(0, self.channels, LANES)], axis=1)
        for b in range(3):
            moved = values if b == 1 else pltpu.roll(values, 1 if b == 0 else size - 1, 0)
            self.taps[slot, first : first + size, b * self.channels : (b + 1) * self.channels] = moved.astype(BF16)

    def begin(self):
        part = self.count // 2
        for first in range(0, self.count, part):
            self.keep(0, first, self.get(pl.ds(first, part)))

    def advance(self, first_round, flags, conv, gate_weight, bit_weight, waits):
        span, channels, rows = self.span, self.channels, self.rows
        lane = iota((1, LANES), 1)
        for step in range(HALF):
            t, slot = first_round + step, step % 2
            now = (lane == 2 * t) | (lane == 2 * t + 1) | (lane == LOW_LANE + 2 * t) | (lane == LOW_LANE + 2 * t + 1)
            self.bits[...] = flags[...] * one_hot(now | (lane >= ONE_LANE))
            total = rows - 2 * (step + 1)
            for begin, part_rows in ((step + 1, total),):
                first, size = begin * span, part_rows * span
                parts = [self.taps[slot, first + a * span : first + a * span + size] for a in (-1, 0, 1)]
                flag = self.bits[first : first + size]
                rounded = self.taps[slot, first : first + size, channels : 2 * channels]
                candidate = matmul(flag, bit_weight[:, :channels])
                if step == 0:
                    third = conv.shape[0] // 3
                    for a in range(3):
                        waits[a].wait()
                        candidate = candidate + matmul(parts[a], conv[a * third : (a + 1) * third])
                    waits[3].wait()
                else:
                    candidate = candidate + matmul(jnp.concatenate(parts, axis=1), conv[...])
                gate = matmul(rounded, gate_weight[...]) + matmul(flag, bit_weight[:, channels:])
                before = self.get(pl.ds(first, size))
                after = before + (0.5 * jnp.tanh(0.5 * gate) + 0.5) * (jnp.tanh(candidate) - before)
                self.put(pl.ds(first, size), after)
                if step < HALF - 1:
                    self.keep(1 - slot, first, after)

    def own(self, r):
        return self.get(pl.ds((self.width + r) * self.span + self.width, self.cols))


def patch_scratch(rows, cols, channels):
    count = (rows + 2 * HALF) * (cols + 2 * HALF)
    return [
        pltpu.VMEM((channels // LANES, count, LANES), F32),
        pltpu.VMEM((2, count, 3 * channels), BF16),
        pltpu.VMEM((count, LANES), BF16),
        pltpu.VMEM((count, LANES), F32),
    ]


def mask_of(flags):
    return matmul(flags, one_hot(iota((LANES, LANES), 0) == ONE_LANE))


def thirds(ref):
    size = ref.shape[0] // 3
    return [ref.at[a * size : (a + 1) * size] for a in range(3)]


def first_kernel(cols, tiles, top, bottom, *refs):
    halo, (region, bit_weight, conv_hbm, gate_hbm) = refs[:4], refs[4:8]
    (exact, partial, flags), new_patch = refs[8:11], refs[11:15]
    state, taps, bits, mask, flags_wide, conv, gate_weight, sems = refs[15:]
    copies = fetch((*thirds(conv_hbm), gate_hbm), (*thirds(conv), gate_weight), sems)
    for copy in copies:
        copy.start()
    patch = Patch(cols, state, taps, bits, mask)
    channels = patch.channels

    def put(at, values):
        patch.put(at, values[:, :channels])
        flags_wide[at] = values[:, channels:]

    patch.fill((top, bottom), halo, put)
    flags[...] = flags_wide[...].astype(BF16)
    mask[...] = mask_of(flags[...])
    patch.begin()
    patch.advance(0, flags, conv, gate_weight, bit_weight, copies)

    own = patch.rows - 2 * patch.width
    cells = [patch.own(r) for r in range(own)]
    for r in range(own):
        exact[r * cols : (r + 1) * cols] = cells[r]
    write_patch(new_patch, cells)
    block_cols = cols // 2
    total = jnp.zeros(partial.shape, F32)
    for r in range(0, own, 2):
        begin = (patch.width + r) * patch.span + patch.width
        parts = [
            patch.get(pl.ds(begin + a * patch.span + b, block_cols, stride=2)) for a in range(2) for b in range(2)
        ]
        pooled = (sum(parts[1:], parts[0]) * 0.25).astype(BF16)
        member = one_hot(iota((partial.shape[0], block_cols), 0) == region[r // 2 : r // 2 + 1])
        total = total + matmul(member, pooled)
    chunk = total.shape[0] // tiles
    for tile in range(tiles):
        at = (tile % 2 * (tiles // 2) + tile // 2) * chunk
        partial[tile * chunk : (tile + 1) * chunk] = total[at : at + chunk].astype(BF16)


def chunk_kernel(tiles, pieces, out):
    values = pieces[...].astype(F32)
    chunk = values.shape[0] // tiles
    total = values[:chunk]
    for p in range(1, tiles):
        total = total + values[p * chunk : (p + 1) * chunk]
    total = total.astype(BF16)
    for p in range(out.shape[0] // chunk):
        out[p * chunk : (p + 1) * chunk] = total


def second_kernel(cols, bands, place, sums, other_sums, attn_gain, mlp_gain, *refs):
    sources, (state_out, context_out) = refs[:18], refs[18:20]
    state, taps, bits, mask, tokens_all, normed_all, keys, values, member, tokens, normed, attention = refs[20:32]
    hidden, context, sems = refs[32:35]
    targets = refs[35:]
    embed, flags, exact, above, below, left, right, bit_weight = targets[1:9]
    pool_weight, key_weight, value_weight, query_weight = targets[0], *targets[9:12]
    out_weight, up_weight, down_weight, return_weight, gate_weight, conv = targets[12:]
    copies = fetch((*sources[:-1], *thirds(sources[-1])), (*targets[:-1], *thirds(conv)), sems)
    patch = Patch(cols, state, taps, bits, mask)
    own_half = place[1]

    def start(*numbers):
        for number in numbers:
            copies[number].start()

    start(0, 1, 2, 9)

    half_tokens = sums.shape[0] // bands
    band_tokens = 2 * half_tokens
    copies[0].wait()
    copies[1].wait()
    start(10, 11)
    for band in range(bands):
        for half in range(2):
            at = pl.ds(band * half_tokens, half_tokens)
            part = jnp.where(own_half == half, sums[at].astype(F32), other_sums[at].astype(F32)).astype(BF16)
            at = pl.ds(band * band_tokens + half * half_tokens, half_tokens)
            total = embed[at].astype(F32) + matmul(part, pool_weight[...])
            tokens_all[at] = total
            normed_all[at] = rms_norm(total, attn_gain[...]).astype(BF16)

    copies[2].wait()
    mask[...] = mask_of(flags[...])
    region = matmul(flags[...], one_hot(iota((LANES, LANES), 0) == REGION_LANE))
    member[...] = jnp.where(region == iota(region.shape, 1).astype(F32), 1.0, 0.0)

    g = place[0]
    own = pl.ds(pl.multiple_of(g * band_tokens, band_tokens), band_tokens)
    tokens[:band_tokens] = tokens_all[own]
    normed[:band_tokens] = normed_all[own]
    blocks = patch.span // 2
    room = (blocks + 7) // 8 * 8
    block_rows = patch.width // 2
    side = room * block_rows
    for number, (band, row) in enumerate(
        ((jnp.maximum(g - 1, 0), 0), (jnp.minimum(g + 1, bands - 1), patch.rows - patch.width))
    ):
        pick = jnp.concatenate(
            [member[pl.ds((row + 2 * r) * patch.span, room, stride=2)] for r in range(block_rows)]
        ).astype(BF16)
        at = pl.ds(pl.multiple_of(band * band_tokens, band_tokens), band_tokens)
        into = pl.ds(band_tokens + number * side, side)
        tokens[into] = select(pick, tokens_all[at])
        normed[into] = matmul(pick, normed_all[at]).astype(BF16)

    copies[9].wait()
    start(12, 13)
    keys[...] = matmul(normed_all[...], key_weight[...]).astype(BF16)
    copies[10].wait()
    start(14, 15)
    values[...] = matmul(normed_all[...], value_weight[...]).astype(BF16)
    copies[11].wait()
    start(*range(3, 9))
    queries = matmul(normed[...], query_weight[...]).astype(BF16)
    for head in range(HEADS):
        at = slice(head * HDIM, (head + 1) * HDIM)
        scores = matmul_nt(queries[:, at], keys[:, at]) * (1.0 / math.sqrt(HDIM))
        weights = jnp.exp(scores - jnp.max(scores, axis=-1, keepdims=True))
        denominator = jnp.sum(weights, axis=-1, keepdims=True)
        attention[:, at] = (matmul(weights.astype(BF16), values[:, at]) / denominator).astype(BF16)
    copies[12].wait()
    start(*range(16, len(copies)))
    attended = tokens[...] + matmul(attention[...], out_weight[...])
    tokens[...] = attended
    normed[...] = rms_norm(attended, mlp_gain[...]).astype(BF16)
    copies[13].wait()
    part = 512
    for at in range(0, up_weight.shape[1], part):
        hidden[:, at : at + part] = jax.nn.gelu(matmul(normed[...], up_weight[:, at : at + part])).astype(BF16)
    copies[14].wait()
    context[...] = (tokens[...] + matmul(hidden[...], down_weight[...])).astype(BF16)
    context_out[...] = context[:band_tokens]
    copies[15].wait()
    returned = matmul(context[...], return_weight[...])

    for copy in copies[3:9]:
        copy.wait()
    patch.fill((exact,), (above, below, left, right), patch.put)
    first, last = patch.width * patch.span, (patch.rows - patch.width) * patch.span
    middle = pl.ds(first, last - first)
    patch.put(middle, patch.get(middle) + select(member[first:last].astype(BF16), returned[:band_tokens]))
    for number, row in enumerate((0, patch.rows - patch.width)):
        for r in range(patch.width):
            start = band_tokens + number * side + r // 2 * room
            share = returned[start : start + blocks]
            for c in range(2):
                at = pl.ds((row + r) * patch.span + c, blocks, stride=2)
                patch.put(at, patch.get(at) + share)

    patch.begin()
    patch.advance(HALF, flags, conv, gate_weight, bit_weight, (*copies[17:], copies[16]))
    for r in range(patch.rows - 2 * patch.width):
        state_out[r * cols : (r + 1) * cols] = patch.own(r).astype(BF16)


def local(
    syndrome_bits, region_assign, state_in, bit_to_candidate, bit_to_gate, conv_weight, gate_weight, gate_bias,
    pool_weight, region_embed, attn_norm_gain, query_weight, key_weight, value_weight, out_weight, mlp_norm_gain,
    mlp_up, mlp_down, return_weight,
):
    rows, cols, channels = state_in.shape
    band_tokens, embed_width = region_embed.shape
    bands, tiles = lax.axis_size("ctx"), math.prod(lax.axis_size(name) for name in TILE)
    conv = conv_weight.reshape(9 * channels, channels)
    half = HALF * cols

    top, bottom, first, last = call(
        message_kernel,
        "message",
        (syndrome_bits.reshape(2 * ROUNDS, rows, cols), region_assign, state_in.reshape(rows * cols, channels)),
        patch_outputs(half, channels + LANES),
        grant=8,
    )
    above, below = row_halo(top, bottom)
    embed, _ = lax.optimization_barrier((region_embed, top))
    bit_weight, embed = call(
        prepare_kernel,
        "prepare",
        (bit_to_candidate, bit_to_gate, gate_bias[None], embed),
        [array(LANES, 2 * channels, BF16), array(bands * band_tokens, embed_width, BF16)],
        moved=8 * MIB,
    )
    embed, bit_weight, above, below = lax.optimization_barrier((embed, bit_weight, above, below))
    left, right = col_halo(cols, above, first, last, below)
    embed = lax.all_to_all(embed.reshape(bands, band_tokens, -1), "ctx", 0, 0).reshape(-1, embed_width)

    count = (rows + 2 * HALF) * (cols + 2 * HALF)
    flops = 15 * rows * cols * HALF * 2 * channels * channels
    exact, partial, flags, top, bottom, first, last = call(
        functools.partial(first_kernel, cols, tiles),
        "rounds",
        (top, bottom, above, below, left, right, region_assign, bit_weight, conv, gate_weight),
        [array(rows * cols, channels, F32), array(band_tokens, channels, BF16), array(count, LANES, BF16)]
        + patch_outputs(half, channels),
        patch_scratch(rows, cols, channels)
        + [
            pltpu.VMEM((count, LANES), F32), pltpu.VMEM(conv.shape, BF16), pltpu.VMEM(gate_weight.shape, BF16),
            pltpu.SemaphoreType.DMA((4,)),
        ],
        in_hbm=(8, 9),
        flops=flops,
    )

    partial, embed = lax.optimization_barrier((partial, embed))
    pieces = lax.all_to_all(partial.reshape(tiles, -1, channels), TILE, 0, 0)
    left, right = shifted(last, TILE, 1), shifted(first, TILE, -1)
    up, down = call(
        rows_kernel,
        "rows",
        (top, bottom, left, right),
        [array(HALF * (cols + 2 * HALF), channels, BF16)] * 2,
        grant=8,
    )
    pieces, up, down = lax.optimization_barrier((pieces, up, down))
    (chunks,) = call(
        functools.partial(chunk_kernel, tiles),
        "chunk",
        (pieces.reshape(band_tokens, channels),),
        [array(bands * band_tokens // 2, channels, BF16)],
        grant=8,
    )
    sums = lax.all_to_all(chunks.reshape(bands * tiles // 2, -1, channels), ("ctx", "chip"), 0, 0)
    up, down, _ = lax.optimization_barrier((up, down, chunks))
    above, below = row_halo(up, down)
    sums, above, below = lax.optimization_barrier((sums.reshape(-1, channels), above, below))
    other_sums = lax.ppermute(sums, "core", [(0, 1), (1, 0)])

    fetched = (
        pool_weight, embed, flags, exact, above, below, left, right, bit_weight, key_weight, value_weight, query_weight,
        out_weight, mlp_up, mlp_down, return_weight, gate_weight, conv,
    )
    blocks = (cols + 2 * HALF) // 2
    layer_rows = band_tokens + HALF * ((blocks + 7) // 8 * 8)
    all_tokens = bands * band_tokens
    place = jnp.stack([lax.axis_index("ctx"), lax.axis_index("core")]).astype(jnp.int32)
    state, context = call(
        functools.partial(second_kernel, cols, bands),
        "context",
        (place, sums, other_sums, attn_norm_gain[None], mlp_norm_gain[None], *fetched),
        [array(rows * cols, channels, BF16), array(band_tokens, embed_width, BF16)],
        patch_scratch(rows, cols, channels)
        + [
            pltpu.VMEM((all_tokens, embed_width), F32), pltpu.VMEM((all_tokens, embed_width), BF16),
            pltpu.VMEM((all_tokens, embed_width), BF16), pltpu.VMEM((all_tokens, embed_width), BF16),
            pltpu.VMEM((count, LANES), F32),
            pltpu.VMEM((layer_rows, embed_width), F32), pltpu.VMEM((layer_rows, embed_width), BF16),
            pltpu.VMEM((layer_rows, embed_width), BF16), pltpu.VMEM((layer_rows, mlp_up.shape[1]), BF16),
            pltpu.VMEM((layer_rows, embed_width), BF16), pltpu.SemaphoreType.DMA((len(fetched) + 2,)),
        ]
        + [pltpu.VMEM(value.shape, value.dtype) for value in fetched],
        in_hbm=range(5, 5 + len(fetched)),
        scalars=(0,),
        flops=2 * flops,
    )
    return (state.reshape(rows, cols, channels), context)


def solution(mesh):
    bands, tiles = mesh.devices.shape
    split = jax.sharding.Mesh(mesh.devices.reshape(bands, tiles // 2, 2), ("ctx", *TILE))
    return jax.shard_map(
        local,
        mesh=split,
        in_specs=(
            P(None, None, "ctx", TILE),
            P("ctx", TILE),
            P("ctx", TILE, None),
            P(), P(), P(), P(), P(), P(),
            P("ctx", None),
            P(), P(), P(), P(), P(), P(), P(), P(), P(),
        ),
        out_specs=(P("ctx", TILE, None), P("ctx", None)),
        check_vma=False,
    )
```

```python
import functools
import math

import jax
import jax.numpy as jnp
from jax import lax
from jax.experimental import pallas as pl
from jax.experimental.pallas import tpu as pltpu
from jax.sharding import PartitionSpec as P

HEADS = 8
HDIM = 128
ROUNDS = 8
HALF = ROUNDS // 2
LANES = 128
F32 = jnp.float32
BF16 = jnp.bfloat16
MIB = 2**20

TILE = ("chip", "core")

REGION_LANE, LOW_LANE, ONE_LANE = 2 * ROUNDS, 32, 64


def shifted(value, axis, step):
    size = math.prod(lax.axis_size(name) for name in axis)
    pairs = [(i, i + step) for i in range(size) if 0 <= i + step < size]
    return lax.ppermute(value, axis, pairs)


def row_halo(top, bottom):
    return shifted(bottom, ("ctx",), 1), shifted(top, ("ctx",), -1)


def col_halo(cols, above, first, last, below):
    count, lanes = first.shape
    first, last = call(
        functools.partial(edges_kernel, cols),
        "edges",
        (above, first, last, below),
        [array(2 * count, lanes, BF16)] * 2,
        grant=8,
    )
    return shifted(last, TILE, 1), shifted(first, TILE, -1)


def matmul(left, right):
    return jnp.dot(left, right, preferred_element_type=F32)


def matmul_nt(left, right):
    return lax.dot_general(left, right, (((1,), (1,)), ((), ())), preferred_element_type=F32)


def two_parts(values):
    high = values.astype(BF16)
    return high, (values - high.astype(F32)).astype(BF16)


def select(member, values):
    high, low = two_parts(values)
    return matmul(member, high) + matmul(member, low)


def rms_norm(values, gain):
    return values * lax.rsqrt(jnp.mean(values * values, axis=-1, keepdims=True) + 1e-05) * gain


def iota(shape, dim):
    return lax.broadcasted_iota(jnp.int32, shape, dim)


def one_hot(condition):
    return jnp.where(condition, 1.0, 0.0).astype(BF16)


def call(kernel, name, operands, outs, scratch=(), in_hbm=(), scalars=(), grant=60, flops=0, moved=MIB):
    def spec(index):
        if index in in_hbm:
            return pl.BlockSpec(memory_space=pltpu.HBM)
        return pl.BlockSpec(memory_space=pltpu.SMEM if index in scalars else pltpu.VMEM)

    return pl.pallas_call(
        kernel,
        out_shape=outs,
        in_specs=[spec(index) for index in range(len(operands))],
        out_specs=[pl.BlockSpec(memory_space=pltpu.VMEM)] * len(outs),
        scratch_shapes=scratch,
        compiler_params=pltpu.CompilerParams(vmem_limit_bytes=grant * MIB),
        cost_estimate=pl.CostEstimate(flops=flops, bytes_accessed=moved, transcendentals=0),
        name=name,
    )(*operands)


def array(count, lanes, dtype):
    return jax.ShapeDtypeStruct((count, lanes), dtype)


def first_columns(part, cols, begin):
    values = part[...].astype(F32)
    return [values[at + begin : at + begin + HALF] for at in range(0, part.shape[0], cols)]


def edges_kernel(cols, above, own_first, own_last, below, first, last):
    for own, begin, out in ((own_first, 0, first), (own_last, cols - HALF, last)):
        parts = first_columns(above, cols, begin) + [own[...].astype(F32)] + first_columns(below, cols, begin)
        out[...] = jnp.concatenate(parts).astype(BF16)


def rows_kernel(top, bottom, left, right, up, down):
    sides = left[...].astype(F32), right[...].astype(F32)
    cols = top.shape[0] // HALF
    for number, (part, out) in enumerate(((top, up), (bottom, down))):
        values, cells = part[...].astype(F32), []
        for r in range(HALF):
            at = (number * HALF + r) * HALF
            before, after = (side[at : at + HALF] for side in sides)
            cells += [before, values[r * cols : (r + 1) * cols], after]
        out[...] = jnp.concatenate(cells).astype(BF16)


def patch_outputs(half, lanes):
    return [array(half, lanes, BF16)] * 2 + [array(2 * HALF * HALF, lanes, BF16)] * 2


def write_patch(outs, rows):
    top, bottom, first, last = outs
    cols = rows[0].shape[0]
    for r, values in enumerate(rows):
        half = (top, bottom)[r // HALF]
        half[r % HALF * cols : (r % HALF + 1) * cols] = values.astype(BF16)
    first[...] = jnp.concatenate([values[:HALF] for values in rows]).astype(BF16)
    last[...] = jnp.concatenate([values[cols - HALF :] for values in rows]).astype(BF16)


def message_kernel(syndrome, region, state, *outs):
    planes, rows, cols = syndrome.shape
    bits = syndrome[...].reshape(planes * rows, cols).astype(F32).astype(BF16)
    column_bits = matmul_nt(one_hot(iota((cols, cols), 0) == iota((cols, cols), 1)), bits).astype(BF16)
    block_rows, block_cols = region.shape
    regions = jnp.concatenate([region[...].astype(F32), jnp.zeros((8 - block_rows, block_cols), F32)])
    spread = one_hot(iota((cols, block_cols), 0) // 2 == iota((cols, block_cols), 1))
    column_region = matmul_nt(spread, regions.astype(BF16)).astype(BF16)
    plane, lane = iota((planes * rows, LANES), 0), iota((planes * rows, LANES), 1)
    ones = jnp.where((iota((cols, LANES), 1) == ONE_LANE) | (iota((cols, LANES), 1) == ONE_LANE + 1), 1.0, 0.0)
    cells = []
    for r in range(rows):
        place = one_hot((plane == lane * rows + r) | (plane == (lane - LOW_LANE) * rows + r))
        region_place = one_hot((iota((8, LANES), 0) == r // 2) & (iota((8, LANES), 1) == REGION_LANE))
        flags = matmul(column_bits, place) + matmul(column_region, region_place) + ones
        cells.append(jnp.concatenate([state[r * cols : (r + 1) * cols].astype(F32), flags], axis=1))
    write_patch(outs, cells)


def fetch(sources, targets, sems):
    return [pltpu.make_async_copy(*pair, sems.at[i]) for i, pair in enumerate(zip(sources, targets))]


def prepare_kernel(candidate_bits, gate_bits, bias, embed, bit_weight, spread):
    by_bit = jnp.concatenate([candidate_bits[...], gate_bits[...]], axis=1)
    bias = jnp.concatenate([jnp.zeros_like(bias), bias[...]], axis=1)
    lane = iota((LANES, 1), 0)
    weight = jnp.zeros(bit_weight.shape, F32)
    for part in range(2):
        begin = (0, LOW_LANE)[part]
        for bit in range(2):
            row = two_parts(by_bit[bit : bit + 1])[part].astype(F32)
            here = (lane >= begin) & (lane < begin + 2 * ROUNDS) & (lane % 2 == bit)
            weight = jnp.where(here, row, weight)
        weight = jnp.where(lane == ONE_LANE + part, two_parts(bias)[part].astype(F32), weight)
    bit_weight[...] = weight.astype(BF16)
    for at in range(0, spread.shape[0], embed.shape[0]):
        spread[at : at + embed.shape[0]] = embed[...]


class Patch:
    def __init__(self, cols, state, taps, bits, mask):
        self.cols, self.span, self.width = cols, cols + 2 * HALF, HALF
        self.state, self.taps, self.bits, self.mask = state, taps, bits, mask
        self.groups, self.count = state.shape[:2]
        self.rows, self.channels = self.count // self.span, self.groups * LANES

    def get(self, at):
        return jnp.concatenate([self.state[j, at] for j in range(self.groups)], axis=1)

    def put(self, at, values):
        for j in range(self.groups):
            self.state[j, at] = values[:, j * LANES : (j + 1) * LANES]

    def fill(self, parts, halo, put):
        above, below, left, right = halo
        r = 0
        for part, part_rows in (
            (above, self.width), *((part, part.shape[0] // self.cols) for part in parts), (below, self.width)
        ):
            length = part.shape[0] // part_rows
            for at in range(0, part.shape[0], length):
                put(pl.ds(r * self.span + (self.span - length) // 2, length), part[at : at + length].astype(F32))
                r += 1
        for part, first in ((left, 0), (right, self.width + self.cols)):
            values = part[...].astype(F32)
            side_rows = values.shape[0] // self.width
            for r in range(side_rows):
                at = (r + (self.rows - side_rows) // 2) * self.span + first
                put(pl.ds(at, self.width), values[r * self.width : (r + 1) * self.width])

    def keep(self, slot, first, values):
        size = values.shape[0]
        mask = self.mask[first : first + size]
        values = jnp.concatenate([values[:, c : c + LANES] * mask for c in range(0, self.channels, LANES)], axis=1)
        for b in range(3):
            moved = values if b == 1 else pltpu.roll(values, 1 if b == 0 else size - 1, 0)
            self.taps[slot, first : first + size, b * self.channels : (b + 1) * self.channels] = moved.astype(BF16)

    def begin(self):
        part = self.count // 2
        for first in range(0, self.count, part):
            self.keep(0, first, self.get(pl.ds(first, part)))

    def advance(self, first_round, flags, conv, gate_weight, bit_weight, waits):
        span, channels, rows = self.span, self.channels, self.rows
        lane = iota((1, LANES), 1)
        for step in range(HALF):
            t, slot = first_round + step, step % 2
            now = (lane == 2 * t) | (lane == 2 * t + 1) | (lane == LOW_LANE + 2 * t) | (lane == LOW_LANE + 2 * t + 1)
            self.bits[...] = flags[...] * one_hot(now | (lane >= ONE_LANE))
            total = rows - 2 * (step + 1)
            for begin, part_rows in ((step + 1, total),):
                first, size = begin * span, part_rows * span
                parts = [self.taps[slot, first + a * span : first + a * span + size] for a in (-1, 0, 1)]
                flag = self.bits[first : first + size]
                rounded = self.taps[slot, first : first + size, channels : 2 * channels]
                candidate = matmul(flag, bit_weight[:, :channels])
                if step == 0:
                    third = conv.shape[0] // 3
                    for a in range(3):
                        waits[a].wait()
                        candidate = candidate + matmul(parts[a], conv[a * third : (a + 1) * third])
                    waits[3].wait()
                else:
                    candidate = candidate + matmul(jnp.concatenate(parts, axis=1), conv[...])
                gate = matmul(rounded, gate_weight[...]) + matmul(flag, bit_weight[:, channels:])
                before = self.get(pl.ds(first, size))
                after = before + (0.5 * jnp.tanh(0.5 * gate) + 0.5) * (jnp.tanh(candidate) - before)
                self.put(pl.ds(first, size), after)
                if step < HALF - 1:
                    self.keep(1 - slot, first, after)

    def own(self, r):
        return self.get(pl.ds((self.width + r) * self.span + self.width, self.cols))


def patch_scratch(rows, cols, channels):
    count = (rows + 2 * HALF) * (cols + 2 * HALF)
    return [
        pltpu.VMEM((channels // LANES, count, LANES), F32),
        pltpu.VMEM((2, count, 3 * channels), BF16),
        pltpu.VMEM((count, LANES), BF16),
        pltpu.VMEM((count, LANES), F32),
    ]


def mask_of(flags):
    return matmul(flags, one_hot(iota((LANES, LANES), 0) == ONE_LANE))


def thirds(ref):
    size = ref.shape[0] // 3
    return [ref.at[a * size : (a + 1) * size] for a in range(3)]


def first_kernel(cols, tiles, top, bottom, *refs):
    halo, (region, bit_weight, conv_hbm, gate_hbm) = refs[:4], refs[4:8]
    (exact, partial, flags), new_patch = refs[8:11], refs[11:15]
    state, taps, bits, mask, flags_wide, conv, gate_weight, sems = refs[15:]
    copies = fetch((*thirds(conv_hbm), gate_hbm), (*thirds(conv), gate_weight), sems)
    for copy in copies:
        copy.start()
    patch = Patch(cols, state, taps, bits, mask)
    channels = patch.channels

    def put(at, values):
        patch.put(at, values[:, :channels])
        flags_wide[at] = values[:, channels:]

    patch.fill((top, bottom), halo, put)
    flags[...] = flags_wide[...].astype(BF16)
    mask[...] = mask_of(flags[...])
    patch.begin()
    patch.advance(0, flags, conv, gate_weight, bit_weight, copies)

    own = patch.rows - 2 * patch.width
    cells = [patch.own(r) for r in range(own)]
    for r in range(own):
        exact[r * cols : (r + 1) * cols] = cells[r]
    write_patch(new_patch, cells)
    block_cols = cols // 2
    total = jnp.zeros(partial.shape, F32)
    for r in range(0, own, 2):
        begin = (patch.width + r) * patch.span + patch.width
        parts = [
            patch.get(pl.ds(begin + a * patch.span + b, block_cols, stride=2)) for a in range(2) for b in range(2)
        ]
        pooled = (sum(parts[1:], parts[0]) * 0.25).astype(BF16)
        member = one_hot(iota((partial.shape[0], block_cols), 0) == region[r // 2 : r // 2 + 1])
        total = total + matmul(member, pooled)
    chunk = total.shape[0] // tiles
    for tile in range(tiles):
        at = (tile % 2 * (tiles // 2) + tile // 2) * chunk
        partial[tile * chunk : (tile + 1) * chunk] = total[at : at + chunk].astype(BF16)


def chunk_kernel(tiles, pieces, out):
    values = pieces[...].astype(F32)
    chunk = values.shape[0] // tiles
    total = values[:chunk]
    for p in range(1, tiles):
        total = total + values[p * chunk : (p + 1) * chunk]
    total = total.astype(BF16)
    for p in range(out.shape[0] // chunk):
        out[p * chunk : (p + 1) * chunk] = total


def member_of(flags):
    region = matmul(flags, one_hot(iota((LANES, LANES), 0) == REGION_LANE))
    return jnp.where(region == iota(region.shape, 1).astype(F32), 1.0, 0.0)


def layer_rooms(cols):
    blocks = (cols + 2 * HALF) // 2
    return blocks, (blocks + 7) // 8 * 8, HALF // 2


def context_kernel(cols, bands, place, sums, other_sums, attn_gain, mlp_gain, flags, *refs):
    sources, (context_out, returned_out), targets, refs = refs[:9], refs[9:11], refs[11:20], refs[20:]
    sums_all, tokens_all, normed_all, keys, values, member, tokens, normed, attention, hidden, context, sems = refs
    embed, pool_weight, key_weight, value_weight, query_weight, out_weight, up_weight, down_weight, return_weight = targets
    copies = fetch(sources, targets, sems)
    for copy in copies[:4]:
        copy.start()
    g, own_half = place[0], place[1]

    half_tokens = sums.shape[0] // bands
    band_tokens = 2 * half_tokens
    for band in range(bands):
        at = pl.ds(band * half_tokens, half_tokens)
        pair = sums[at].astype(F32), other_sums[at].astype(F32)
        for half in range(2):
            part = jnp.where(own_half == half, *pair).astype(BF16)
            sums_all[pl.ds(band * band_tokens + half * half_tokens, half_tokens)] = part
    member[...] = member_of(flags[...])
    copies[0].wait()
    copies[1].wait()
    for copy in copies[4:7]:
        copy.start()
    total = embed[...].astype(F32) + matmul(sums_all[...], pool_weight[...])
    tokens_all[...] = total
    normed_all[...] = rms_norm(total, attn_gain[...]).astype(BF16)

    own = pl.ds(pl.multiple_of(g * band_tokens, band_tokens), band_tokens)
    tokens[:band_tokens] = tokens_all[own]
    normed[:band_tokens] = normed_all[own]
    _, room, block_rows = layer_rooms(cols)
    side, span = room * block_rows, cols + 2 * HALF
    for number, (band, row) in enumerate(
        ((jnp.maximum(g - 1, 0), 0), (jnp.minimum(g + 1, bands - 1), flags.shape[0] // span - HALF))
    ):
        pick = jnp.concatenate([member[pl.ds((row + 2 * r) * span, room, stride=2)] for r in range(block_rows)])
        pick = pick.astype(BF16)
        at = pl.ds(pl.multiple_of(band * band_tokens, band_tokens), band_tokens)
        into = pl.ds(band_tokens + number * side, side)
        tokens[into] = select(pick, tokens_all[at])
        normed[into] = matmul(pick, normed_all[at]).astype(BF16)

    copies[2].wait()
    keys[...] = matmul(normed_all[...], key_weight[...]).astype(BF16)
    copies[3].wait()
    for copy in copies[7:]:
        copy.start()
    values[...] = matmul(normed_all[...], value_weight[...]).astype(BF16)
    copies[4].wait()
    queries = matmul(normed[...], query_weight[...]).astype(BF16)
    for head in range(HEADS):
        at = slice(head * HDIM, (head + 1) * HDIM)
        scores = matmul_nt(queries[:, at], keys[:, at]) * (1.0 / math.sqrt(HDIM))
        weights = jnp.exp(scores - jnp.max(scores, axis=-1, keepdims=True))
        denominator = jnp.sum(weights, axis=-1, keepdims=True)
        attention[:, at] = (matmul(weights.astype(BF16), values[:, at]) / denominator).astype(BF16)
    copies[5].wait()
    attended = tokens[...] + matmul(attention[...], out_weight[...])
    tokens[...] = attended
    normed[...] = rms_norm(attended, mlp_gain[...]).astype(BF16)
    copies[6].wait()
    part = 512
    for at in range(0, up_weight.shape[1], part):
        hidden[:, at : at + part] = jax.nn.gelu(matmul(normed[...], up_weight[:, at : at + part])).astype(BF16)
    copies[7].wait()
    context[...] = (tokens[...] + matmul(hidden[...], down_weight[...])).astype(BF16)
    context_out[...] = context[:band_tokens]
    copies[8].wait()
    returned_out[...] = matmul(context[...], return_weight[...])


def second_kernel(
    cols, exact, above, below, left, right, flags, returned, bit_weight, conv_hbm, gate_hbm, state_out,
    state, taps, bits, mask, conv, gate_weight, sems,
):
    copies = fetch((*thirds(conv_hbm), gate_hbm), (*thirds(conv), gate_weight), sems)
    for copy in copies:
        copy.start()
    patch = Patch(cols, state, taps, bits, mask)
    patch.fill((exact,), (above, below, left, right), patch.put)
    mask[...] = mask_of(flags[...])
    blocks, room, block_rows = layer_rooms(cols)
    side = room * block_rows
    band_tokens = returned.shape[0] - 2 * side
    first, last = patch.width * patch.span, (patch.rows - patch.width) * patch.span
    middle = pl.ds(first, last - first)
    member = member_of(flags[middle]).astype(BF16)
    patch.put(middle, patch.get(middle) + select(member, returned[:band_tokens]))
    for number, row in enumerate((0, patch.rows - patch.width)):
        for r in range(patch.width):
            start = band_tokens + number * side + r // 2 * room
            share = returned[start : start + blocks]
            for c in range(2):
                at = pl.ds((row + r) * patch.span + c, blocks, stride=2)
                patch.put(at, patch.get(at) + share)
    patch.begin()
    patch.advance(HALF, flags, conv, gate_weight, bit_weight, copies)
    for r in range(patch.rows - 2 * patch.width):
        state_out[r * cols : (r + 1) * cols] = patch.own(r).astype(BF16)


def local(
    syndrome_bits, region_assign, state_in, bit_to_candidate, bit_to_gate, conv_weight, gate_weight, gate_bias,
    pool_weight, region_embed, attn_norm_gain, query_weight, key_weight, value_weight, out_weight, mlp_norm_gain,
    mlp_up, mlp_down, return_weight,
):
    rows, cols, channels = state_in.shape
    band_tokens, embed_width = region_embed.shape
    bands, tiles = lax.axis_size("ctx"), math.prod(lax.axis_size(name) for name in TILE)
    conv = conv_weight.reshape(9 * channels, channels)
    half = HALF * cols

    top, bottom, first, last = call(
        message_kernel,
        "message",
        (syndrome_bits.reshape(2 * ROUNDS, rows, cols), region_assign, state_in.reshape(rows * cols, channels)),
        patch_outputs(half, channels + LANES),
        grant=8,
    )
    above, below = row_halo(top, bottom)
    embed, _ = lax.optimization_barrier((region_embed, top))
    bit_weight, embed = call(
        prepare_kernel,
        "prepare",
        (bit_to_candidate, bit_to_gate, gate_bias[None], embed),
        [array(LANES, 2 * channels, BF16), array(bands * band_tokens, embed_width, BF16)],
        moved=8 * MIB,
    )
    embed, bit_weight, above, below = lax.optimization_barrier((embed, bit_weight, above, below))
    left, right = col_halo(cols, above, first, last, below)
    embed = lax.all_to_all(embed.reshape(bands, band_tokens, -1), "ctx", 0, 0).reshape(-1, embed_width)

    count = (rows + 2 * HALF) * (cols + 2 * HALF)
    flops = 15 * rows * cols * HALF * 2 * channels * channels
    exact, partial, flags, top, bottom, first, last = call(
        functools.partial(first_kernel, cols, tiles),
        "rounds",
        (top, bottom, above, below, left, right, region_assign, bit_weight, conv, gate_weight),
        [array(rows * cols, channels, F32), array(band_tokens, channels, BF16), array(count, LANES, BF16)]
        + patch_outputs(half, channels),
        patch_scratch(rows, cols, channels)
        + [
            pltpu.VMEM((count, LANES), F32), pltpu.VMEM(conv.shape, BF16), pltpu.VMEM(gate_weight.shape, BF16),
            pltpu.SemaphoreType.DMA((4,)),
        ],
        in_hbm=(8, 9),
        flops=flops,
    )

    partial, embed = lax.optimization_barrier((partial, embed))
    pieces = lax.all_to_all(partial.reshape(tiles, -1, channels), TILE, 0, 0)
    left, right = shifted(last, TILE, 1), shifted(first, TILE, -1)
    pieces, left, right = lax.optimization_barrier((pieces, left, right))
    up, down = call(
        rows_kernel,
        "rows",
        (top, bottom, left, right),
        [array(HALF * (cols + 2 * HALF), channels, BF16)] * 2,
        grant=8,
    )
    (chunks,) = call(
        functools.partial(chunk_kernel, tiles),
        "chunk",
        (pieces.reshape(band_tokens, channels),),
        [array(bands * band_tokens // 2, channels, BF16)],
        grant=8,
    )
    sums = lax.all_to_all(chunks.reshape(bands * tiles // 2, -1, channels), ("ctx", "chip"), 0, 0)
    sums, up, down = lax.optimization_barrier((sums.reshape(-1, channels), up, down))
    above, below = row_halo(up, down)
    other_sums = lax.ppermute(sums, "core", [(0, 1), (1, 0)])

    layer = (
        embed, pool_weight, key_weight, value_weight, query_weight, out_weight, mlp_up, mlp_down, return_weight,
    )
    _, room, block_rows = layer_rooms(cols)
    layer_rows = band_tokens + 2 * room * block_rows
    all_tokens = bands * band_tokens
    mlp = mlp_up.shape[1]
    place = jnp.stack([lax.axis_index("ctx"), lax.axis_index("core")]).astype(jnp.int32)
    context, returned = call(
        functools.partial(context_kernel, cols, bands),
        "context",
        (place, sums, other_sums, attn_norm_gain[None], mlp_norm_gain[None], flags, *layer),
        [array(band_tokens, embed_width, BF16), array(layer_rows, channels, F32)],
        [pltpu.VMEM(value.shape, value.dtype) for value in layer]
        + [
            pltpu.VMEM((all_tokens, channels), BF16),
            pltpu.VMEM((all_tokens, embed_width), F32), pltpu.VMEM((all_tokens, embed_width), BF16),
            pltpu.VMEM((all_tokens, embed_width), BF16), pltpu.VMEM((all_tokens, embed_width), BF16),
            pltpu.VMEM((count, LANES), F32),
            pltpu.VMEM((layer_rows, embed_width), F32), pltpu.VMEM((layer_rows, embed_width), BF16),
            pltpu.VMEM((layer_rows, embed_width), BF16), pltpu.VMEM((layer_rows, mlp), BF16),
            pltpu.VMEM((layer_rows, embed_width), BF16), pltpu.SemaphoreType.DMA((len(layer),)),
        ],
        in_hbm=range(6, 6 + len(layer)),
        scalars=(0,),
        flops=2 * embed_width * (all_tokens * (channels + 2 * embed_width) + layer_rows * (2 * embed_width + 2 * mlp)),
        moved=20 * MIB,
    )
    (state,) = call(
        functools.partial(second_kernel, cols),
        "rounds",
        (exact, above, below, left, right, flags, returned, bit_weight, conv, gate_weight),
        [array(rows * cols, channels, BF16)],
        patch_scratch(rows, cols, channels)
        + [pltpu.VMEM(conv.shape, BF16), pltpu.VMEM(gate_weight.shape, BF16), pltpu.SemaphoreType.DMA((4,))],
        in_hbm=(8, 9),
        flops=flops,
    )
    return (state.reshape(rows, cols, channels), context)


def solution(mesh):
    bands, tiles = mesh.devices.shape
    split = jax.sharding.Mesh(mesh.devices.reshape(bands, tiles // 2, 2), ("ctx", *TILE))
    return jax.shard_map(
        local,
        mesh=split,
        in_specs=(
            P(None, None, "ctx", TILE),
            P("ctx", TILE),
            P("ctx", TILE, None),
            P(), P(), P(), P(), P(), P(),
            P("ctx", None),
            P(), P(), P(), P(), P(), P(), P(), P(), P(),
        ),
        out_specs=(P("ctx", TILE, None), P("ctx", None)),
        check_vma=False,
    )
```

```python
import functools
import math

import jax
import jax.numpy as jnp
from jax import lax
from jax.experimental import pallas as pl
from jax.experimental.pallas import tpu as pltpu
from jax.sharding import PartitionSpec as P

HEADS = 8
HDIM = 128
ROUNDS = 8
HALF = ROUNDS // 2
LANES = 128
F32 = jnp.float32
BF16 = jnp.bfloat16
MIB = 2**20

TILE = ("chip", "core")

REGION_LANE, LOW_LANE, ONE_LANE = 2 * ROUNDS, 32, 64


def shifted(value, axis, step):
    size = math.prod(lax.axis_size(name) for name in axis)
    pairs = [(i, i + step) for i in range(size) if 0 <= i + step < size]
    return lax.ppermute(value, axis, pairs)


def row_halo(top, bottom):
    return shifted(bottom, ("ctx",), 1), shifted(top, ("ctx",), -1)


def col_halo(cols, above, first, last, below):
    count, lanes = first.shape
    first, last = call(
        functools.partial(edges_kernel, cols),
        "edges",
        (above, first, last, below),
        [array(2 * count, lanes, BF16)] * 2,
        grant=8,
    )
    return shifted(last, TILE, 1), shifted(first, TILE, -1)


def matmul(left, right):
    return jnp.dot(left, right, preferred_element_type=F32)


def matmul_nt(left, right):
    return lax.dot_general(left, right, (((1,), (1,)), ((), ())), preferred_element_type=F32)


def two_parts(values):
    high = values.astype(BF16)
    return high, (values - high.astype(F32)).astype(BF16)


def select(member, values):
    high, low = two_parts(values)
    return matmul(member, high) + matmul(member, low)


def rms_norm(values, gain):
    return values * lax.rsqrt(jnp.mean(values * values, axis=-1, keepdims=True) + 1e-05) * gain


def iota(shape, dim):
    return lax.broadcasted_iota(jnp.int32, shape, dim)


def one_hot(condition):
    return jnp.where(condition, 1.0, 0.0).astype(BF16)


def call(kernel, name, operands, outs, scratch=(), in_hbm=(), scalars=(), grant=60, flops=0, moved=MIB):
    def spec(index):
        if index in in_hbm:
            return pl.BlockSpec(memory_space=pltpu.HBM)
        return pl.BlockSpec(memory_space=pltpu.SMEM if index in scalars else pltpu.VMEM)

    return pl.pallas_call(
        kernel,
        out_shape=outs,
        in_specs=[spec(index) for index in range(len(operands))],
        out_specs=[pl.BlockSpec(memory_space=pltpu.VMEM)] * len(outs),
        scratch_shapes=scratch,
        compiler_params=pltpu.CompilerParams(vmem_limit_bytes=grant * MIB),
        cost_estimate=pl.CostEstimate(flops=flops, bytes_accessed=moved, transcendentals=0),
        name=name,
    )(*operands)


def array(count, lanes, dtype):
    return jax.ShapeDtypeStruct((count, lanes), dtype)


def first_columns(part, cols, begin):
    values = part[...].astype(F32)
    return [values[at + begin : at + begin + HALF] for at in range(0, part.shape[0], cols)]


def edges_kernel(cols, above, own_first, own_last, below, first, last):
    for own, begin, out in ((own_first, 0, first), (own_last, cols - HALF, last)):
        parts = first_columns(above, cols, begin) + [own[...].astype(F32)] + first_columns(below, cols, begin)
        out[...] = jnp.concatenate(parts).astype(BF16)


def patch_outputs(half, lanes):
    return [array(half, lanes, BF16)] * 2 + [array(2 * HALF * HALF, lanes, BF16)] * 2


def write_patch(outs, rows):
    top, bottom, first, last = outs
    cols = rows[0].shape[0]
    for r, values in enumerate(rows):
        half = (top, bottom)[r // HALF]
        half[r % HALF * cols : (r % HALF + 1) * cols] = values.astype(BF16)
    first[...] = jnp.concatenate([values[:HALF] for values in rows]).astype(BF16)
    last[...] = jnp.concatenate([values[cols - HALF :] for values in rows]).astype(BF16)


def message_kernel(syndrome, region, state, *outs):
    planes, rows, cols = syndrome.shape
    bits = syndrome[...].reshape(planes * rows, cols).astype(F32).astype(BF16)
    column_bits = matmul_nt(one_hot(iota((cols, cols), 0) == iota((cols, cols), 1)), bits).astype(BF16)
    block_rows, block_cols = region.shape
    regions = jnp.concatenate([region[...].astype(F32), jnp.zeros((8 - block_rows, block_cols), F32)])
    spread = one_hot(iota((cols, block_cols), 0) // 2 == iota((cols, block_cols), 1))
    column_region = matmul_nt(spread, regions.astype(BF16)).astype(BF16)
    plane, lane = iota((planes * rows, LANES), 0), iota((planes * rows, LANES), 1)
    ones = jnp.where((iota((cols, LANES), 1) == ONE_LANE) | (iota((cols, LANES), 1) == ONE_LANE + 1), 1.0, 0.0)
    cells = []
    for r in range(rows):
        place = one_hot((plane == lane * rows + r) | (plane == (lane - LOW_LANE) * rows + r))
        region_place = one_hot((iota((8, LANES), 0) == r // 2) & (iota((8, LANES), 1) == REGION_LANE))
        flags = matmul(column_bits, place) + matmul(column_region, region_place) + ones
        cells.append(jnp.concatenate([state[r * cols : (r + 1) * cols].astype(F32), flags], axis=1))
    write_patch(outs, cells)


def fetch(sources, targets, sems):
    return [pltpu.make_async_copy(*pair, sems.at[i]) for i, pair in enumerate(zip(sources, targets))]


def prepare_kernel(candidate_bits, gate_bits, bias, embed, bit_weight, spread):
    by_bit = jnp.concatenate([candidate_bits[...], gate_bits[...]], axis=1)
    bias = jnp.concatenate([jnp.zeros_like(bias), bias[...]], axis=1)
    lane = iota((LANES, 1), 0)
    weight = jnp.zeros(bit_weight.shape, F32)
    for part in range(2):
        begin = (0, LOW_LANE)[part]
        for bit in range(2):
            row = two_parts(by_bit[bit : bit + 1])[part].astype(F32)
            here = (lane >= begin) & (lane < begin + 2 * ROUNDS) & (lane % 2 == bit)
            weight = jnp.where(here, row, weight)
        weight = jnp.where(lane == ONE_LANE + part, two_parts(bias)[part].astype(F32), weight)
    bit_weight[...] = weight.astype(BF16)
    for at in range(0, spread.shape[0], embed.shape[0]):
        spread[at : at + embed.shape[0]] = embed[...]


class Patch:
    def __init__(self, cols, state, taps, bits, mask):
        self.cols, self.span, self.width = cols, cols + 2 * HALF, HALF
        self.state, self.taps, self.bits, self.mask = state, taps, bits, mask
        self.groups, self.count = state.shape[:2]
        self.rows, self.channels = self.count // self.span, self.groups * LANES

    def get(self, at):
        return jnp.concatenate([self.state[j, at] for j in range(self.groups)], axis=1)

    def put(self, at, values):
        for j in range(self.groups):
            self.state[j, at] = values[:, j * LANES : (j + 1) * LANES]

    def fill(self, parts, halo, put):
        above, below, left, right = halo
        r = 0
        for part, part_rows in (
            (above, self.width), *((part, part.shape[0] // self.cols) for part in parts), (below, self.width)
        ):
            length = part.shape[0] // part_rows
            for at in range(0, part.shape[0], length):
                put(pl.ds(r * self.span + (self.span - length) // 2, length), part[at : at + length].astype(F32))
                r += 1
        for part, first in ((left, 0), (right, self.width + self.cols)):
            values = part[...].astype(F32)
            side_rows = values.shape[0] // self.width
            for r in range(side_rows):
                at = (r + (self.rows - side_rows) // 2) * self.span + first
                put(pl.ds(at, self.width), values[r * self.width : (r + 1) * self.width])

    def keep(self, slot, first, values):
        size = values.shape[0]
        mask = self.mask[first : first + size]
        values = jnp.concatenate([values[:, c : c + LANES] * mask for c in range(0, self.channels, LANES)], axis=1)
        for b in range(3):
            moved = values if b == 1 else pltpu.roll(values, 1 if b == 0 else size - 1, 0)
            self.taps[slot, first : first + size, b * self.channels : (b + 1) * self.channels] = moved.astype(BF16)

    def begin(self):
        part = self.count // 2
        for first in range(0, self.count, part):
            self.keep(0, first, self.get(pl.ds(first, part)))

    def advance(self, first_round, flags, conv, gate_weight, bit_weight, waits):
        span, channels, rows = self.span, self.channels, self.rows
        lane = iota((1, LANES), 1)
        for step in range(HALF):
            t, slot = first_round + step, step % 2
            now = (lane == 2 * t) | (lane == 2 * t + 1) | (lane == LOW_LANE + 2 * t) | (lane == LOW_LANE + 2 * t + 1)
            self.bits[...] = flags[...] * one_hot(now | (lane >= ONE_LANE))
            total = rows - 2 * (step + 1)
            for begin, part_rows in ((step + 1, total),):
                first, size = begin * span, part_rows * span
                parts = [self.taps[slot, first + a * span : first + a * span + size] for a in (-1, 0, 1)]
                flag = self.bits[first : first + size]
                rounded = self.taps[slot, first : first + size, channels : 2 * channels]
                candidate = matmul(flag, bit_weight[:, :channels])
                if step == 0:
                    third = conv.shape[0] // 3
                    for a in range(3):
                        waits[a].wait()
                        candidate = candidate + matmul(parts[a], conv[a * third : (a + 1) * third])
                    waits[3].wait()
                else:
                    candidate = candidate + matmul(jnp.concatenate(parts, axis=1), conv[...])
                gate = matmul(rounded, gate_weight[...]) + matmul(flag, bit_weight[:, channels:])
                before = self.get(pl.ds(first, size))
                after = before + (0.5 * jnp.tanh(0.5 * gate) + 0.5) * (jnp.tanh(candidate) - before)
                self.put(pl.ds(first, size), after)
                if step < HALF - 1:
                    self.keep(1 - slot, first, after)

    def own(self, r):
        return self.get(pl.ds((self.width + r) * self.span + self.width, self.cols))


def patch_scratch(rows, cols, channels):
    count = (rows + 2 * HALF) * (cols + 2 * HALF)
    return [
        pltpu.VMEM((channels // LANES, count, LANES), F32),
        pltpu.VMEM((2, count, 3 * channels), BF16),
        pltpu.VMEM((count, LANES), BF16),
        pltpu.VMEM((count, LANES), F32),
    ]


def mask_of(flags):
    return matmul(flags, one_hot(iota((LANES, LANES), 0) == ONE_LANE))


def thirds(ref):
    size = ref.shape[0] // 3
    return [ref.at[a * size : (a + 1) * size] for a in range(3)]


def first_kernel(cols, place, top, bottom, *refs):
    halo, (region, bit_weight, conv_hbm, gate_hbm) = refs[:4], refs[4:8]
    (exact, kept, given, flags), new_patch = refs[8:12], refs[12:16]
    state, taps, bits, mask, flags_wide, conv, gate_weight, sems = refs[16:]
    copies = fetch((*thirds(conv_hbm), gate_hbm), (*thirds(conv), gate_weight), sems)
    for copy in copies:
        copy.start()
    patch = Patch(cols, state, taps, bits, mask)
    channels = patch.channels

    def put(at, values):
        patch.put(at, values[:, :channels])
        flags_wide[at] = values[:, channels:]

    patch.fill((top, bottom), halo, put)
    flags[...] = flags_wide[...].astype(BF16)
    mask[...] = mask_of(flags[...])
    patch.begin()
    patch.advance(0, flags, conv, gate_weight, bit_weight, copies)

    own = patch.rows - 2 * patch.width
    cells = [patch.own(r) for r in range(own)]
    for r in range(own):
        exact[r * cols : (r + 1) * cols] = cells[r]
    write_patch(new_patch, cells)
    block_cols = cols // 2
    half = kept.shape[0]
    total = jnp.zeros((2 * half, channels), F32)
    for r in range(0, own, 2):
        begin = (patch.width + r) * patch.span + patch.width
        parts = [
            patch.get(pl.ds(begin + a * patch.span + b, block_cols, stride=2)) for a in range(2) for b in range(2)
        ]
        pooled = (sum(parts[1:], parts[0]) * 0.25).astype(BF16)
        member = one_hot(iota((2 * half, block_cols), 0) == region[r // 2 : r // 2 + 1])
        total = total + matmul(member, pooled)
    is_first = place[1] == 0
    kept[...] = jnp.where(is_first, total[:half], total[half:])
    given[...] = jnp.where(is_first, total[half:], total[:half]).astype(BF16)


def repeat_into(out, values):
    count = values.shape[0]
    for at in range(0, out.shape[0], count):
        out[at : at + count] = values.astype(BF16)


def pair_kernel(kept, received, out):
    repeat_into(out, kept[...] + received[...].astype(F32))


def band_kernel(chips, pieces, out):
    values = pieces[...].astype(F32)
    count = values.shape[0] // chips
    parts = [values[p * count : (p + 1) * count] for p in range(chips)]
    repeat_into(out, sum(parts[1:], parts[0]))


def second_kernel(cols, bands, place, sums, other_sums, attn_gain, mlp_gain, *refs):
    sources, (state_out, context_out) = refs[:18], refs[18:20]
    state, taps, bits, mask, sums_all, tokens_all, normed_all, keys, values, member, tokens, normed = refs[20:32]
    attention, hidden, context, sems = refs[32:36]
    targets = refs[36:]
    embed, flags, exact, above, below, left, right, bit_weight = targets[1:9]
    pool_weight, key_weight, value_weight, query_weight = targets[0], *targets[9:12]
    out_weight, up_weight, down_weight, return_weight, gate_weight, conv = targets[12:]
    copies = fetch((*sources[:-1], *thirds(sources[-1])), (*targets[:-1], *thirds(conv)), sems)
    patch = Patch(cols, state, taps, bits, mask)
    own_half = place[1]

    def start(*numbers):
        for number in numbers:
            copies[number].start()

    start(0, 1, 2, 9)

    half_tokens = sums.shape[0] // bands
    band_tokens = 2 * half_tokens
    for band in range(bands):
        at = pl.ds(band * half_tokens, half_tokens)
        pair = sums[at].astype(F32), other_sums[at].astype(F32)
        for half in range(2):
            part = jnp.where(own_half == half, *pair).astype(BF16)
            sums_all[pl.ds(band * band_tokens + half * half_tokens, half_tokens)] = part
    copies[0].wait()
    copies[1].wait()
    start(10, 11)
    total = embed[...].astype(F32) + matmul(sums_all[...], pool_weight[...])
    tokens_all[...] = total
    normed_all[...] = rms_norm(total, attn_gain[...]).astype(BF16)

    copies[2].wait()
    mask[...] = mask_of(flags[...])
    region = matmul(flags[...], one_hot(iota((LANES, LANES), 0) == REGION_LANE))
    member[...] = jnp.where(region == iota(region.shape, 1).astype(F32), 1.0, 0.0)

    g = place[0]
    own = pl.ds(pl.multiple_of(g * band_tokens, band_tokens), band_tokens)
    tokens[:band_tokens] = tokens_all[own]
    normed[:band_tokens] = normed_all[own]
    blocks = patch.span // 2
    room = (blocks + 7) // 8 * 8
    block_rows = patch.width // 2
    side = room * block_rows
    for number, (band, row) in enumerate(
        ((jnp.maximum(g - 1, 0), 0), (jnp.minimum(g + 1, bands - 1), patch.rows - patch.width))
    ):
        pick = jnp.concatenate(
            [member[pl.ds((row + 2 * r) * patch.span, room, stride=2)] for r in range(block_rows)]
        ).astype(BF16)
        at = pl.ds(pl.multiple_of(band * band_tokens, band_tokens), band_tokens)
        into = pl.ds(band_tokens + number * side, side)
        tokens[into] = select(pick, tokens_all[at])
        normed[into] = matmul(pick, normed_all[at]).astype(BF16)

    copies[9].wait()
    start(12, 13)
    keys[...] = matmul(normed_all[...], key_weight[...]).astype(BF16)
    copies[10].wait()
    start(14, 15)
    values[...] = matmul(normed_all[...], value_weight[...]).astype(BF16)
    copies[11].wait()
    start(*range(3, 9))
    queries = matmul(normed[...], query_weight[...]).astype(BF16)
    for head in range(HEADS):
        at = slice(head * HDIM, (head + 1) * HDIM)
        scores = matmul_nt(queries[:, at], keys[:, at]) * (1.0 / math.sqrt(HDIM))
        weights = jnp.exp(scores - jnp.max(scores, axis=-1, keepdims=True))
        denominator = jnp.sum(weights, axis=-1, keepdims=True)
        attention[:, at] = (matmul(weights.astype(BF16), values[:, at]) / denominator).astype(BF16)
    copies[12].wait()
    start(*range(16, len(copies)))
    attended = tokens[...] + matmul(attention[...], out_weight[...])
    tokens[...] = attended
    normed[...] = rms_norm(attended, mlp_gain[...]).astype(BF16)
    copies[13].wait()
    part = 512
    for at in range(0, up_weight.shape[1], part):
        hidden[:, at : at + part] = jax.nn.gelu(matmul(normed[...], up_weight[:, at : at + part])).astype(BF16)
    copies[14].wait()
    context[...] = (tokens[...] + matmul(hidden[...], down_weight[...])).astype(BF16)
    context_out[...] = context[:band_tokens]
    copies[15].wait()
    returned = matmul(context[...], return_weight[...])

    for copy in copies[3:9]:
        copy.wait()
    patch.fill((exact,), (above, below, left, right), patch.put)
    first, last = patch.width * patch.span, (patch.rows - patch.width) * patch.span
    middle = pl.ds(first, last - first)
    patch.put(middle, patch.get(middle) + select(member[first:last].astype(BF16), returned[:band_tokens]))
    for number, row in enumerate((0, patch.rows - patch.width)):
        for r in range(patch.width):
            start = band_tokens + number * side + r // 2 * room
            share = returned[start : start + blocks]
            for c in range(2):
                at = pl.ds((row + r) * patch.span + c, blocks, stride=2)
                patch.put(at, patch.get(at) + share)

    patch.begin()
    patch.advance(HALF, flags, conv, gate_weight, bit_weight, (*copies[17:], copies[16]))
    for r in range(patch.rows - 2 * patch.width):
        state_out[r * cols : (r + 1) * cols] = patch.own(r).astype(BF16)


def local(
    syndrome_bits, region_assign, state_in, bit_to_candidate, bit_to_gate, conv_weight, gate_weight, gate_bias,
    pool_weight, region_embed, attn_norm_gain, query_weight, key_weight, value_weight, out_weight, mlp_norm_gain,
    mlp_up, mlp_down, return_weight,
):
    rows, cols, channels = state_in.shape
    band_tokens, embed_width = region_embed.shape
    bands, tiles = lax.axis_size("ctx"), math.prod(lax.axis_size(name) for name in TILE)
    conv = conv_weight.reshape(9 * channels, channels)
    place = jnp.stack([lax.axis_index("ctx"), lax.axis_index("core")]).astype(jnp.int32)
    swap = [(0, 1), (1, 0)]
    half = HALF * cols

    top, bottom, first, last = call(
        message_kernel,
        "message",
        (syndrome_bits.reshape(2 * ROUNDS, rows, cols), region_assign, state_in.reshape(rows * cols, channels)),
        patch_outputs(half, channels + LANES),
        grant=8,
    )
    above, below = row_halo(top, bottom)
    embed, _ = lax.optimization_barrier((region_embed, top))
    bit_weight, embed = call(
        prepare_kernel,
        "prepare",
        (bit_to_candidate, bit_to_gate, gate_bias[None], embed),
        [array(LANES, 2 * channels, BF16), array(bands * band_tokens, embed_width, BF16)],
        moved=8 * MIB,
    )
    embed, bit_weight, above, below = lax.optimization_barrier((embed, bit_weight, above, below))
    left, right = col_halo(cols, above, first, last, below)
    embed = lax.all_to_all(embed.reshape(bands, band_tokens, -1), "ctx", 0, 0).reshape(-1, embed_width)

    count = (rows + 2 * HALF) * (cols + 2 * HALF)
    flops = 15 * rows * cols * HALF * 2 * channels * channels
    exact, kept, given, flags, top, bottom, first, last = call(
        functools.partial(first_kernel, cols),
        "rounds",
        (place, top, bottom, above, below, left, right, region_assign, bit_weight, conv, gate_weight),
        [
            array(rows * cols, channels, F32), array(band_tokens // 2, channels, F32),
            array(band_tokens // 2, channels, BF16), array(count, LANES, BF16),
        ]
        + patch_outputs(half, channels),
        patch_scratch(rows, cols, channels)
        + [
            pltpu.VMEM((count, LANES), F32), pltpu.VMEM(conv.shape, BF16), pltpu.VMEM(gate_weight.shape, BF16),
            pltpu.SemaphoreType.DMA((4,)),
        ],
        in_hbm=(9, 10),
        scalars=(0,),
        flops=flops,
    )

    chips, half_tokens = tiles // 2, band_tokens // 2
    given, embed = lax.optimization_barrier((given, embed))
    received = lax.ppermute(given, "core", swap)
    (pieces,) = call(
        pair_kernel, "pair", (kept, received), [array(chips * half_tokens, channels, BF16)], grant=8
    )
    pieces = lax.all_to_all(pieces.reshape(chips, half_tokens, channels), "chip", 0, 0)
    above, below = row_halo(top, bottom)
    pieces, above, below = lax.optimization_barrier((pieces, above, below))
    (sums,) = call(
        functools.partial(band_kernel, chips),
        "band",
        (pieces.reshape(-1, channels),),
        [array(bands * half_tokens, channels, BF16)],
        grant=8,
    )
    above, below, sums = lax.optimization_barrier((above, below, sums))
    sums = lax.all_to_all(sums.reshape(bands, half_tokens, channels), "ctx", 0, 0)
    left, right = col_halo(cols, above, first, last, below)
    sums, left, right = lax.optimization_barrier((sums.reshape(-1, channels), left, right))
    other_sums = lax.ppermute(sums, "core", swap)

    fetched = (
        pool_weight, embed, flags, exact, above, below, left, right, bit_weight, key_weight, value_weight, query_weight,
        out_weight, mlp_up, mlp_down, return_weight, gate_weight, conv,
    )
    blocks = (cols + 2 * HALF) // 2
    layer_rows = band_tokens + HALF * ((blocks + 7) // 8 * 8)
    all_tokens = bands * band_tokens
    state, context = call(
        functools.partial(second_kernel, cols, bands),
        "context",
        (place, sums, other_sums, attn_norm_gain[None], mlp_norm_gain[None], *fetched),
        [array(rows * cols, channels, BF16), array(band_tokens, embed_width, BF16)],
        patch_scratch(rows, cols, channels)
        + [
            pltpu.VMEM((all_tokens, channels), BF16),
            pltpu.VMEM((all_tokens, embed_width), F32), pltpu.VMEM((all_tokens, embed_width), BF16),
            pltpu.VMEM((all_tokens, embed_width), BF16), pltpu.VMEM((all_tokens, embed_width), BF16),
            pltpu.VMEM((count, LANES), F32),
            pltpu.VMEM((layer_rows, embed_width), F32), pltpu.VMEM((layer_rows, embed_width), BF16),
            pltpu.VMEM((layer_rows, embed_width), BF16), pltpu.VMEM((layer_rows, mlp_up.shape[1]), BF16),
            pltpu.VMEM((layer_rows, embed_width), BF16), pltpu.SemaphoreType.DMA((len(fetched) + 2,)),
        ]
        + [pltpu.VMEM(value.shape, value.dtype) for value in fetched],
        in_hbm=range(5, 5 + len(fetched)),
        scalars=(0,),
        flops=2 * flops,
    )
    return (state.reshape(rows, cols, channels), context)


def solution(mesh):
    bands, tiles = mesh.devices.shape
    split = jax.sharding.Mesh(mesh.devices.reshape(bands, tiles // 2, 2), ("ctx", *TILE))
    return jax.shard_map(
        local,
        mesh=split,
        in_specs=(
            P(None, None, "ctx", TILE),
            P("ctx", TILE),
            P("ctx", TILE, None),
            P(), P(), P(), P(), P(), P(),
            P("ctx", None),
            P(), P(), P(), P(), P(), P(), P(), P(), P(),
        ),
        out_specs=(P("ctx", TILE, None), P("ctx", None)),
        check_vma=False,
    )
```

```python
import functools
import math

import jax
import jax.numpy as jnp
from jax import lax
from jax.experimental import pallas as pl
from jax.experimental.pallas import tpu as pltpu
from jax.sharding import PartitionSpec as P

HEADS = 8
HDIM = 128
ROUNDS = 8
HALF = ROUNDS // 2
LANES = 128
F32 = jnp.float32
BF16 = jnp.bfloat16
MIB = 2**20

TILE = ("chip", "core")

REGION_LANE, LOW_LANE, ONE_LANE = 2 * ROUNDS, 32, 64


def shifted(value, axis, step):
    size = math.prod(lax.axis_size(name) for name in axis)
    pairs = [(i, i + step) for i in range(size) if 0 <= i + step < size]
    return lax.ppermute(value, axis, pairs)


def row_halo(top, bottom):
    return shifted(bottom, ("ctx",), 1), shifted(top, ("ctx",), -1)


def col_halo(cols, above, first, last, below):
    count, lanes = first.shape
    first, last = call(
        functools.partial(edges_kernel, cols),
        "edges",
        (above, first, last, below),
        [array(2 * count, lanes, BF16)] * 2,
        grant=8,
    )
    return shifted(last, TILE, 1), shifted(first, TILE, -1)


def matmul(left, right):
    return jnp.dot(left, right, preferred_element_type=F32)


def matmul_nt(left, right):
    return lax.dot_general(left, right, (((1,), (1,)), ((), ())), preferred_element_type=F32)


def two_parts(values):
    high = values.astype(BF16)
    return high, (values - high.astype(F32)).astype(BF16)


def select(member, values):
    high, low = two_parts(values)
    return matmul(member, high) + matmul(member, low)


def rms_norm(values, gain):
    return values * lax.rsqrt(jnp.mean(values * values, axis=-1, keepdims=True) + 1e-05) * gain


def iota(shape, dim):
    return lax.broadcasted_iota(jnp.int32, shape, dim)


def one_hot(condition):
    return jnp.where(condition, 1.0, 0.0).astype(BF16)


def call(kernel, name, operands, outs, scratch=(), in_hbm=(), scalars=(), grant=60, flops=0, moved=MIB):
    def spec(index):
        if index in in_hbm:
            return pl.BlockSpec(memory_space=pltpu.HBM)
        return pl.BlockSpec(memory_space=pltpu.SMEM if index in scalars else pltpu.VMEM)

    return pl.pallas_call(
        kernel,
        out_shape=outs,
        in_specs=[spec(index) for index in range(len(operands))],
        out_specs=[pl.BlockSpec(memory_space=pltpu.VMEM)] * len(outs),
        scratch_shapes=scratch,
        compiler_params=pltpu.CompilerParams(vmem_limit_bytes=grant * MIB),
        cost_estimate=pl.CostEstimate(flops=flops, bytes_accessed=moved, transcendentals=0),
        name=name,
    )(*operands)


def array(count, lanes, dtype):
    return jax.ShapeDtypeStruct((count, lanes), dtype)


def first_columns(part, cols, begin):
    values = part[...].astype(F32)
    return [values[at + begin : at + begin + HALF] for at in range(0, part.shape[0], cols)]


def edges_kernel(cols, above, own_first, own_last, below, first, last):
    for own, begin, out in ((own_first, 0, first), (own_last, cols - HALF, last)):
        parts = first_columns(above, cols, begin) + [own[...].astype(F32)] + first_columns(below, cols, begin)
        out[...] = jnp.concatenate(parts).astype(BF16)


def rows_kernel(top, bottom, left, right, up, down):
    sides = left[...].astype(F32), right[...].astype(F32)
    cols = top.shape[0] // HALF
    for number, (part, out) in enumerate(((top, up), (bottom, down))):
        values, cells = part[...].astype(F32), []
        for r in range(HALF):
            at = (number * HALF + r) * HALF
            before, after = (side[at : at + HALF] for side in sides)
            cells += [before, values[r * cols : (r + 1) * cols], after]
        out[...] = jnp.concatenate(cells).astype(BF16)


def patch_outputs(half, lanes):
    return [array(half, lanes, BF16)] * 2 + [array(2 * HALF * HALF, lanes, BF16)] * 2


def write_patch(outs, rows):
    top, bottom, first, last = outs
    cols = rows[0].shape[0]
    for r, values in enumerate(rows):
        half = (top, bottom)[r // HALF]
        half[r % HALF * cols : (r % HALF + 1) * cols] = values.astype(BF16)
    first[...] = jnp.concatenate([values[:HALF] for values in rows]).astype(BF16)
    last[...] = jnp.concatenate([values[cols - HALF :] for values in rows]).astype(BF16)


def message_kernel(syndrome, region, state, *outs):
    planes, rows, cols = syndrome.shape
    bits = syndrome[...].reshape(planes * rows, cols).astype(F32).astype(BF16)
    column_bits = matmul_nt(one_hot(iota((cols, cols), 0) == iota((cols, cols), 1)), bits).astype(BF16)
    block_rows, block_cols = region.shape
    regions = jnp.concatenate([region[...].astype(F32), jnp.zeros((8 - block_rows, block_cols), F32)])
    spread = one_hot(iota((cols, block_cols), 0) // 2 == iota((cols, block_cols), 1))
    column_region = matmul_nt(spread, regions.astype(BF16)).astype(BF16)
    plane, lane = iota((planes * rows, LANES), 0), iota((planes * rows, LANES), 1)
    ones = jnp.where((iota((cols, LANES), 1) == ONE_LANE) | (iota((cols, LANES), 1) == ONE_LANE + 1), 1.0, 0.0)
    cells = []
    for r in range(rows):
        place = one_hot((plane == lane * rows + r) | (plane == (lane - LOW_LANE) * rows + r))
        region_place = one_hot((iota((8, LANES), 0) == r // 2) & (iota((8, LANES), 1) == REGION_LANE))
        flags = matmul(column_bits, place) + matmul(column_region, region_place) + ones
        cells.append(jnp.concatenate([state[r * cols : (r + 1) * cols].astype(F32), flags], axis=1))
    write_patch(outs, cells)


def fetch(sources, targets, sems):
    return [pltpu.make_async_copy(*pair, sems.at[i]) for i, pair in enumerate(zip(sources, targets))]


def prepare_kernel(candidate_bits, gate_bits, bias, embed, bit_weight, spread):
    by_bit = jnp.concatenate([candidate_bits[...], gate_bits[...]], axis=1)
    bias = jnp.concatenate([jnp.zeros_like(bias), bias[...]], axis=1)
    lane = iota((LANES, 1), 0)
    weight = jnp.zeros(bit_weight.shape, F32)
    for part in range(2):
        begin = (0, LOW_LANE)[part]
        for bit in range(2):
            row = two_parts(by_bit[bit : bit + 1])[part].astype(F32)
            here = (lane >= begin) & (lane < begin + 2 * ROUNDS) & (lane % 2 == bit)
            weight = jnp.where(here, row, weight)
        weight = jnp.where(lane == ONE_LANE + part, two_parts(bias)[part].astype(F32), weight)
    bit_weight[...] = weight.astype(BF16)
    for at in range(0, spread.shape[0], embed.shape[0]):
        spread[at : at + embed.shape[0]] = embed[...]


class Patch:
    def __init__(self, cols, state, taps, bits, mask):
        self.cols, self.span, self.width = cols, cols + 2 * HALF, HALF
        self.state, self.taps, self.bits, self.mask = state, taps, bits, mask
        self.groups, self.count = state.shape[:2]
        self.rows, self.channels = self.count // self.span, self.groups * LANES

    def get(self, at):
        return jnp.concatenate([self.state[j, at] for j in range(self.groups)], axis=1)

    def put(self, at, values):
        for j in range(self.groups):
            self.state[j, at] = values[:, j * LANES : (j + 1) * LANES]

    def fill(self, parts, halo, put):
        above, below, left, right = halo
        r = 0
        for part, part_rows in (
            (above, self.width), *((part, part.shape[0] // self.cols) for part in parts), (below, self.width)
        ):
            length = part.shape[0] // part_rows
            for at in range(0, part.shape[0], length):
                put(pl.ds(r * self.span + (self.span - length) // 2, length), part[at : at + length].astype(F32))
                r += 1
        for part, first in ((left, 0), (right, self.width + self.cols)):
            values = part[...].astype(F32)
            side_rows = values.shape[0] // self.width
            for r in range(side_rows):
                at = (r + (self.rows - side_rows) // 2) * self.span + first
                put(pl.ds(at, self.width), values[r * self.width : (r + 1) * self.width])

    def keep(self, slot, first, values):
        size = values.shape[0]
        mask = self.mask[first : first + size]
        values = jnp.concatenate([values[:, c : c + LANES] * mask for c in range(0, self.channels, LANES)], axis=1)
        for b in range(3):
            moved = values if b == 1 else pltpu.roll(values, 1 if b == 0 else size - 1, 0)
            self.taps[slot, first : first + size, b * self.channels : (b + 1) * self.channels] = moved.astype(BF16)

    def begin(self):
        part = self.count // 2
        for first in range(0, self.count, part):
            self.keep(0, first, self.get(pl.ds(first, part)))

    def advance(self, first_round, flags, conv, gate_weight, bit_weight, waits):
        span, channels, rows = self.span, self.channels, self.rows
        lane = iota((1, LANES), 1)
        for step in range(HALF):
            t, slot = first_round + step, step % 2
            now = (lane == 2 * t) | (lane == 2 * t + 1) | (lane == LOW_LANE + 2 * t) | (lane == LOW_LANE + 2 * t + 1)
            self.bits[...] = flags[...] * one_hot(now | (lane >= ONE_LANE))
            total = rows - 2 * (step + 1)
            for begin, part_rows in ((step + 1, total),):
                first, size = begin * span, part_rows * span
                parts = [self.taps[slot, first + a * span : first + a * span + size] for a in (-1, 0, 1)]
                flag = self.bits[first : first + size]
                rounded = self.taps[slot, first : first + size, channels : 2 * channels]
                candidate = matmul(flag, bit_weight[:, :channels])
                if step == 0:
                    third = conv.shape[0] // 3
                    for a in range(3):
                        waits[a].wait()
                        candidate = candidate + matmul(parts[a], conv[a * third : (a + 1) * third])
                    waits[3].wait()
                else:
                    candidate = candidate + matmul(jnp.concatenate(parts, axis=1), conv[...])
                gate = matmul(rounded, gate_weight[...]) + matmul(flag, bit_weight[:, channels:])
                before = self.get(pl.ds(first, size))
                after = before + (0.5 * jnp.tanh(0.5 * gate) + 0.5) * (jnp.tanh(candidate) - before)
                self.put(pl.ds(first, size), after)
                if step < HALF - 1:
                    self.keep(1 - slot, first, after)

    def own(self, r):
        return self.get(pl.ds((self.width + r) * self.span + self.width, self.cols))


def patch_scratch(rows, cols, channels):
    count = (rows + 2 * HALF) * (cols + 2 * HALF)
    return [
        pltpu.VMEM((channels // LANES, count, LANES), F32),
        pltpu.VMEM((2, count, 3 * channels), BF16),
        pltpu.VMEM((count, LANES), BF16),
        pltpu.VMEM((count, LANES), F32),
    ]


def mask_of(flags):
    return matmul(flags, one_hot(iota((LANES, LANES), 0) == ONE_LANE))


def thirds(ref):
    size = ref.shape[0] // 3
    return [ref.at[a * size : (a + 1) * size] for a in range(3)]


def first_kernel(cols, place, top, bottom, *refs):
    halo, (region, bit_weight, conv_hbm, gate_hbm) = refs[:4], refs[4:8]
    (exact, kept, given, flags), new_patch = refs[8:12], refs[12:16]
    state, taps, bits, mask, flags_wide, conv, gate_weight, sems = refs[16:]
    copies = fetch((*thirds(conv_hbm), gate_hbm), (*thirds(conv), gate_weight), sems)
    for copy in copies:
        copy.start()
    patch = Patch(cols, state, taps, bits, mask)
    channels = patch.channels

    def put(at, values):
        patch.put(at, values[:, :channels])
        flags_wide[at] = values[:, channels:]

    patch.fill((top, bottom), halo, put)
    flags[...] = flags_wide[...].astype(BF16)
    mask[...] = mask_of(flags[...])
    patch.begin()
    patch.advance(0, flags, conv, gate_weight, bit_weight, copies)

    own = patch.rows - 2 * patch.width
    cells = [patch.own(r) for r in range(own)]
    for r in range(own):
        exact[r * cols : (r + 1) * cols] = cells[r]
    write_patch(new_patch, cells)
    block_cols = cols // 2
    half = kept.shape[0]
    total = jnp.zeros((2 * half, channels), F32)
    for r in range(0, own, 2):
        begin = (patch.width + r) * patch.span + patch.width
        parts = [
            patch.get(pl.ds(begin + a * patch.span + b, block_cols, stride=2)) for a in range(2) for b in range(2)
        ]
        pooled = (sum(parts[1:], parts[0]) * 0.25).astype(BF16)
        member = one_hot(iota((2 * half, block_cols), 0) == region[r // 2 : r // 2 + 1])
        total = total + matmul(member, pooled)
    is_first = place[1] == 0
    kept[...] = jnp.where(is_first, total[:half], total[half:])
    given[...] = jnp.where(is_first, total[half:], total[:half]).astype(BF16)


def repeat_into(out, values):
    count = values.shape[0]
    for at in range(0, out.shape[0], count):
        out[at : at + count] = values.astype(BF16)


def pair_kernel(kept, received, out):
    repeat_into(out, kept[...] + received[...].astype(F32))


def band_kernel(chips, pieces, out):
    values = pieces[...].astype(F32)
    count = values.shape[0] // chips
    parts = [values[p * count : (p + 1) * count] for p in range(chips)]
    repeat_into(out, sum(parts[1:], parts[0]))


def second_kernel(
    cols, bands, place, sums, other_sums, embed, flags, exact, above, below, left, right, attn_gain, mlp_gain, bit_weight,
    *refs
):
    sources, (state_out, context_out), refs = refs[:10], refs[10:12], refs[12:]
    state, taps, bits, mask, sums_all, tokens_all, normed_all, keys, values, member, tokens, normed = refs[:12]
    attention, hidden, context, sems = refs[12:16]
    targets = refs[16:]
    pool_weight, key_weight, value_weight, query_weight, out_weight = targets[:5]
    up_weight, down_weight, return_weight, gate_weight, conv = targets[5:]
    copies = fetch((*sources[:-1], *thirds(sources[-1])), (*targets[:-1], *thirds(conv)), sems)
    for copy in copies:
        copy.start()
    patch = Patch(cols, state, taps, bits, mask)
    own_half = place[1]

    half_tokens = sums.shape[0] // bands
    band_tokens = 2 * half_tokens
    for band in range(bands):
        at = pl.ds(band * half_tokens, half_tokens)
        pair = sums[at].astype(F32), other_sums[at].astype(F32)
        for half in range(2):
            part = jnp.where(own_half == half, *pair).astype(BF16)
            sums_all[pl.ds(band * band_tokens + half * half_tokens, half_tokens)] = part
    copies[0].wait()
    total = embed[...].astype(F32) + matmul(sums_all[...], pool_weight[...])
    tokens_all[...] = total
    normed_all[...] = rms_norm(total, attn_gain[...]).astype(BF16)

    mask[...] = mask_of(flags[...])
    region = matmul(flags[...], one_hot(iota((LANES, LANES), 0) == REGION_LANE))
    member[...] = jnp.where(region == iota(region.shape, 1).astype(F32), 1.0, 0.0)

    g = place[0]
    own = pl.ds(pl.multiple_of(g * band_tokens, band_tokens), band_tokens)
    tokens[:band_tokens] = tokens_all[own]
    normed[:band_tokens] = normed_all[own]
    blocks = patch.span // 2
    room = (blocks + 7) // 8 * 8
    block_rows = patch.width // 2
    side = room * block_rows
    for number, (band, row) in enumerate(
        ((jnp.maximum(g - 1, 0), 0), (jnp.minimum(g + 1, bands - 1), patch.rows - patch.width))
    ):
        pick = jnp.concatenate(
            [member[pl.ds((row + 2 * r) * patch.span, room, stride=2)] for r in range(block_rows)]
        ).astype(BF16)
        at = pl.ds(pl.multiple_of(band * band_tokens, band_tokens), band_tokens)
        into = pl.ds(band_tokens + number * side, side)
        tokens[into] = select(pick, tokens_all[at])
        normed[into] = matmul(pick, normed_all[at]).astype(BF16)

    copies[1].wait()
    keys[...] = matmul(normed_all[...], key_weight[...]).astype(BF16)
    copies[2].wait()
    values[...] = matmul(normed_all[...], value_weight[...]).astype(BF16)
    copies[3].wait()
    queries = matmul(normed[...], query_weight[...]).astype(BF16)
    for head in range(HEADS):
        at = slice(head * HDIM, (head + 1) * HDIM)
        scores = matmul_nt(queries[:, at], keys[:, at]) * (1.0 / math.sqrt(HDIM))
        weights = jnp.exp(scores - jnp.max(scores, axis=-1, keepdims=True))
        denominator = jnp.sum(weights, axis=-1, keepdims=True)
        attention[:, at] = (matmul(weights.astype(BF16), values[:, at]) / denominator).astype(BF16)
    copies[4].wait()
    attended = tokens[...] + matmul(attention[...], out_weight[...])
    tokens[...] = attended
    normed[...] = rms_norm(attended, mlp_gain[...]).astype(BF16)
    copies[5].wait()
    part = 512
    for at in range(0, up_weight.shape[1], part):
        hidden[:, at : at + part] = jax.nn.gelu(matmul(normed[...], up_weight[:, at : at + part])).astype(BF16)
    copies[6].wait()
    context[...] = (tokens[...] + matmul(hidden[...], down_weight[...])).astype(BF16)
    context_out[...] = context[:band_tokens]
    copies[7].wait()
    returned = matmul(context[...], return_weight[...])

    patch.fill((exact,), (above, below, left, right), patch.put)
    first, last = patch.width * patch.span, (patch.rows - patch.width) * patch.span
    middle = pl.ds(first, last - first)
    patch.put(middle, patch.get(middle) + select(member[first:last].astype(BF16), returned[:band_tokens]))
    for number, row in enumerate((0, patch.rows - patch.width)):
        for r in range(patch.width):
            start = band_tokens + number * side + r // 2 * room
            share = returned[start : start + blocks]
            for c in range(2):
                at = pl.ds((row + r) * patch.span + c, blocks, stride=2)
                patch.put(at, patch.get(at) + share)

    patch.begin()
    patch.advance(HALF, flags, conv, gate_weight, bit_weight, (*copies[9:], copies[8]))
    for r in range(patch.rows - 2 * patch.width):
        state_out[r * cols : (r + 1) * cols] = patch.own(r).astype(BF16)


def local(
    syndrome_bits, region_assign, state_in, bit_to_candidate, bit_to_gate, conv_weight, gate_weight, gate_bias,
    pool_weight, region_embed, attn_norm_gain, query_weight, key_weight, value_weight, out_weight, mlp_norm_gain,
    mlp_up, mlp_down, return_weight,
):
    rows, cols, channels = state_in.shape
    band_tokens, embed_width = region_embed.shape
    bands, tiles = lax.axis_size("ctx"), math.prod(lax.axis_size(name) for name in TILE)
    conv = conv_weight.reshape(9 * channels, channels)
    place = jnp.stack([lax.axis_index("ctx"), lax.axis_index("core")]).astype(jnp.int32)
    swap = [(0, 1), (1, 0)]
    half = HALF * cols

    top, bottom, first, last = call(
        message_kernel,
        "message",
        (syndrome_bits.reshape(2 * ROUNDS, rows, cols), region_assign, state_in.reshape(rows * cols, channels)),
        patch_outputs(half, channels + LANES),
        grant=8,
    )
    above, below = row_halo(top, bottom)
    embed, _ = lax.optimization_barrier((region_embed, top))
    bit_weight, embed = call(
        prepare_kernel,
        "prepare",
        (bit_to_candidate, bit_to_gate, gate_bias[None], embed),
        [array(LANES, 2 * channels, BF16), array(bands * band_tokens, embed_width, BF16)],
        moved=8 * MIB,
    )
    embed, bit_weight, above, below, place = lax.optimization_barrier((embed, bit_weight, above, below, place))
    left, right = col_halo(cols, above, first, last, below)
    embed = lax.all_to_all(embed.reshape(bands, band_tokens, -1), "ctx", 0, 0).reshape(-1, embed_width)

    count = (rows + 2 * HALF) * (cols + 2 * HALF)
    flops = 15 * rows * cols * HALF * 2 * channels * channels
    exact, kept, given, flags, top, bottom, first, last = call(
        functools.partial(first_kernel, cols),
        "rounds",
        (place, top, bottom, above, below, left, right, region_assign, bit_weight, conv, gate_weight),
        [
            array(rows * cols, channels, F32), array(band_tokens // 2, channels, F32),
            array(band_tokens // 2, channels, BF16), array(count, LANES, BF16),
        ]
        + patch_outputs(half, channels),
        patch_scratch(rows, cols, channels)
        + [
            pltpu.VMEM((count, LANES), F32), pltpu.VMEM(conv.shape, BF16), pltpu.VMEM(gate_weight.shape, BF16),
            pltpu.SemaphoreType.DMA((4,)),
        ],
        in_hbm=(9, 10),
        scalars=(0,),
        flops=flops,
    )

    chips, half_tokens = tiles // 2, band_tokens // 2
    given, embed = lax.optimization_barrier((given, embed))
    received = lax.ppermute(given, "core", swap)
    (pieces,) = call(
        pair_kernel, "pair", (kept, received), [array(chips * half_tokens, channels, BF16)], grant=8
    )
    pieces = lax.all_to_all(pieces.reshape(chips, half_tokens, channels), "chip", 0, 0)
    left, right = shifted(last, TILE, 1), shifted(first, TILE, -1)
    up, down = call(
        rows_kernel,
        "rows",
        (top, bottom, left, right),
        [array(HALF * (cols + 2 * HALF), channels, BF16)] * 2,
        grant=8,
    )
    pieces, up, down = lax.optimization_barrier((pieces, up, down))
    (sums,) = call(
        functools.partial(band_kernel, chips),
        "band",
        (pieces.reshape(-1, channels),),
        [array(bands * half_tokens, channels, BF16)],
        grant=8,
    )
    up, down, sums = lax.optimization_barrier((up, down, sums))
    sums = lax.all_to_all(sums.reshape(bands, half_tokens, channels), "ctx", 0, 0)
    above, below = row_halo(up, down)
    sums, above, below = lax.optimization_barrier((sums.reshape(-1, channels), above, below))
    other_sums = lax.ppermute(sums, "core", swap)

    fetched = (
        pool_weight, key_weight, value_weight, query_weight, out_weight, mlp_up, mlp_down, return_weight, gate_weight,
        conv,
    )
    blocks = (cols + 2 * HALF) // 2
    layer_rows = band_tokens + HALF * ((blocks + 7) // 8 * 8)
    all_tokens = bands * band_tokens
    state, context = call(
        functools.partial(second_kernel, cols, bands),
        "context",
        (
            place, sums, other_sums, embed, flags, exact, above, below, left, right, attn_norm_gain[None],
            mlp_norm_gain[None], bit_weight, *fetched,
        ),
        [array(rows * cols, channels, BF16), array(band_tokens, embed_width, BF16)],
        patch_scratch(rows, cols, channels)
        + [
            pltpu.VMEM((all_tokens, channels), BF16),
            pltpu.VMEM((all_tokens, embed_width), F32), pltpu.VMEM((all_tokens, embed_width), BF16),
            pltpu.VMEM((all_tokens, embed_width), BF16), pltpu.VMEM((all_tokens, embed_width), BF16),
            pltpu.VMEM((count, LANES), F32),
            pltpu.VMEM((layer_rows, embed_width), F32), pltpu.VMEM((layer_rows, embed_width), BF16),
            pltpu.VMEM((layer_rows, embed_width), BF16), pltpu.VMEM((layer_rows, mlp_up.shape[1]), BF16),
            pltpu.VMEM((layer_rows, embed_width), BF16), pltpu.SemaphoreType.DMA((len(fetched) + 2,)),
        ]
        + [pltpu.VMEM(value.shape, value.dtype) for value in fetched],
        in_hbm=range(13, 13 + len(fetched)),
        scalars=(0,),
        flops=2 * flops,
    )
    return (state.reshape(rows, cols, channels), context)


def solution(mesh):
    bands, tiles = mesh.devices.shape
    split = jax.sharding.Mesh(mesh.devices.reshape(bands, tiles // 2, 2), ("ctx", *TILE))
    return jax.shard_map(
        local,
        mesh=split,
        in_specs=(
            P(None, None, "ctx", TILE),
            P("ctx", TILE),
            P("ctx", TILE, None),
            P(), P(), P(), P(), P(), P(),
            P("ctx", None),
            P(), P(), P(), P(), P(), P(), P(), P(), P(),
        ),
        out_specs=(P("ctx", TILE, None), P("ctx", None)),
        check_vma=False,
    )
```

```python
import functools
import math

import jax
import jax.numpy as jnp
from jax import lax
from jax.experimental import pallas as pl
from jax.experimental.pallas import tpu as pltpu
from jax.sharding import PartitionSpec as P

HEADS = 8
HDIM = 128
ROUNDS = 8
HALF = ROUNDS // 2
LANES = 128
F32 = jnp.float32
BF16 = jnp.bfloat16
MIB = 2**20

TILE = ("chip", "core")

REGION_LANE, LOW_LANE, ONE_LANE = 2 * ROUNDS, 32, 64


def shifted(value, axis, step):
    size = math.prod(lax.axis_size(name) for name in axis)
    pairs = [(i, i + step) for i in range(size) if 0 <= i + step < size]
    return lax.ppermute(value, axis, pairs)


def row_halo(top, bottom):
    return shifted(bottom, ("ctx",), 1), shifted(top, ("ctx",), -1)


def col_halo(cols, above, first, last, below):
    count, lanes = first.shape
    first, last = call(
        functools.partial(edges_kernel, cols),
        "edges",
        (above, first, last, below),
        [array(2 * count, lanes, BF16)] * 2,
        grant=8,
    )
    return shifted(last, TILE, 1), shifted(first, TILE, -1)


def matmul(left, right):
    return jnp.dot(left, right, preferred_element_type=F32)


def matmul_nt(left, right):
    return lax.dot_general(left, right, (((1,), (1,)), ((), ())), preferred_element_type=F32)


def two_parts(values):
    high = values.astype(BF16)
    return high, (values - high.astype(F32)).astype(BF16)


def select(member, values):
    high, low = two_parts(values)
    return matmul(member, high) + matmul(member, low)


def rms_norm(values, gain):
    return values * lax.rsqrt(jnp.mean(values * values, axis=-1, keepdims=True) + 1e-05) * gain


def iota(shape, dim):
    return lax.broadcasted_iota(jnp.int32, shape, dim)


def one_hot(condition):
    return jnp.where(condition, 1.0, 0.0).astype(BF16)


def call(kernel, name, operands, outs, scratch=(), in_hbm=(), scalars=(), grant=60, flops=0, moved=MIB):
    def spec(index):
        if index in in_hbm:
            return pl.BlockSpec(memory_space=pltpu.HBM)
        return pl.BlockSpec(memory_space=pltpu.SMEM if index in scalars else pltpu.VMEM)

    return pl.pallas_call(
        kernel,
        out_shape=outs,
        in_specs=[spec(index) for index in range(len(operands))],
        out_specs=[pl.BlockSpec(memory_space=pltpu.VMEM)] * len(outs),
        scratch_shapes=scratch,
        compiler_params=pltpu.CompilerParams(vmem_limit_bytes=grant * MIB),
        cost_estimate=pl.CostEstimate(flops=flops, bytes_accessed=moved, transcendentals=0),
        name=name,
    )(*operands)


def array(count, lanes, dtype):
    return jax.ShapeDtypeStruct((count, lanes), dtype)


def first_columns(part, cols, begin):
    values = part[...].astype(F32)
    return [values[at + begin : at + begin + HALF] for at in range(0, part.shape[0], cols)]


def edges_kernel(cols, above, own_first, own_last, below, first, last):
    for own, begin, out in ((own_first, 0, first), (own_last, cols - HALF, last)):
        parts = first_columns(above, cols, begin) + [own[...].astype(F32)] + first_columns(below, cols, begin)
        out[...] = jnp.concatenate(parts).astype(BF16)


def rows_kernel(top, bottom, left, right, up, down):
    sides = left[...].astype(F32), right[...].astype(F32)
    cols = top.shape[0] // HALF
    for number, (part, out) in enumerate(((top, up), (bottom, down))):
        values, cells = part[...].astype(F32), []
        for r in range(HALF):
            at = (number * HALF + r) * HALF
            before, after = (side[at : at + HALF] for side in sides)
            cells += [before, values[r * cols : (r + 1) * cols], after]
        out[...] = jnp.concatenate(cells).astype(BF16)


def patch_outputs(half, lanes):
    return [array(half, lanes, BF16)] * 2 + [array(2 * HALF * HALF, lanes, BF16)] * 2


def write_patch(outs, rows):
    top, bottom, first, last = outs
    cols = rows[0].shape[0]
    for r, values in enumerate(rows):
        half = (top, bottom)[r // HALF]
        half[r % HALF * cols : (r % HALF + 1) * cols] = values.astype(BF16)
    first[...] = jnp.concatenate([values[:HALF] for values in rows]).astype(BF16)
    last[...] = jnp.concatenate([values[cols - HALF :] for values in rows]).astype(BF16)


def message_kernel(syndrome, region, state, *outs):
    planes, rows, cols = syndrome.shape
    bits = syndrome[...].reshape(planes * rows, cols).astype(F32).astype(BF16)
    column_bits = matmul_nt(one_hot(iota((cols, cols), 0) == iota((cols, cols), 1)), bits).astype(BF16)
    block_rows, block_cols = region.shape
    regions = jnp.concatenate([region[...].astype(F32), jnp.zeros((8 - block_rows, block_cols), F32)])
    spread = one_hot(iota((cols, block_cols), 0) // 2 == iota((cols, block_cols), 1))
    column_region = matmul_nt(spread, regions.astype(BF16)).astype(BF16)
    plane, lane = iota((planes * rows, LANES), 0), iota((planes * rows, LANES), 1)
    ones = jnp.where((iota((cols, LANES), 1) == ONE_LANE) | (iota((cols, LANES), 1) == ONE_LANE + 1), 1.0, 0.0)
    cells = []
    for r in range(rows):
        place = one_hot((plane == lane * rows + r) | (plane == (lane - LOW_LANE) * rows + r))
        region_place = one_hot((iota((8, LANES), 0) == r // 2) & (iota((8, LANES), 1) == REGION_LANE))
        flags = matmul(column_bits, place) + matmul(column_region, region_place) + ones
        cells.append(jnp.concatenate([state[r * cols : (r + 1) * cols].astype(F32), flags], axis=1))
    write_patch(outs, cells)


def fetch(sources, targets, sems):
    return [pltpu.make_async_copy(*pair, sems.at[i]) for i, pair in enumerate(zip(sources, targets))]


def prepare_kernel(candidate_bits, gate_bits, bias, embed, bit_weight, spread):
    by_bit = jnp.concatenate([candidate_bits[...], gate_bits[...]], axis=1)
    bias = jnp.concatenate([jnp.zeros_like(bias), bias[...]], axis=1)
    lane = iota((LANES, 1), 0)
    weight = jnp.zeros(bit_weight.shape, F32)
    for part in range(2):
        begin = (0, LOW_LANE)[part]
        for bit in range(2):
            row = two_parts(by_bit[bit : bit + 1])[part].astype(F32)
            here = (lane >= begin) & (lane < begin + 2 * ROUNDS) & (lane % 2 == bit)
            weight = jnp.where(here, row, weight)
        weight = jnp.where(lane == ONE_LANE + part, two_parts(bias)[part].astype(F32), weight)
    bit_weight[...] = weight.astype(BF16)
    for at in range(0, spread.shape[0], embed.shape[0]):
        spread[at : at + embed.shape[0]] = embed[...]


class Patch:
    def __init__(self, cols, state, taps, bits, mask):
        self.cols, self.span, self.width = cols, cols + 2 * HALF, HALF
        self.state, self.taps, self.bits, self.mask = state, taps, bits, mask
        self.groups, self.count = state.shape[:2]
        self.rows, self.channels = self.count // self.span, self.groups * LANES

    def get(self, at):
        return jnp.concatenate([self.state[j, at] for j in range(self.groups)], axis=1)

    def put(self, at, values):
        for j in range(self.groups):
            self.state[j, at] = values[:, j * LANES : (j + 1) * LANES]

    def fill(self, parts, halo, put):
        above, below, left, right = halo
        r = 0
        for part, part_rows in (
            (above, self.width), *((part, part.shape[0] // self.cols) for part in parts), (below, self.width)
        ):
            length = part.shape[0] // part_rows
            for at in range(0, part.shape[0], length):
                put(pl.ds(r * self.span + (self.span - length) // 2, length), part[at : at + length].astype(F32))
                r += 1
        for part, first in ((left, 0), (right, self.width + self.cols)):
            values = part[...].astype(F32)
            side_rows = values.shape[0] // self.width
            for r in range(side_rows):
                at = (r + (self.rows - side_rows) // 2) * self.span + first
                put(pl.ds(at, self.width), values[r * self.width : (r + 1) * self.width])

    def keep(self, slot, first, values):
        size = values.shape[0]
        mask = self.mask[first : first + size]
        values = jnp.concatenate([values[:, c : c + LANES] * mask for c in range(0, self.channels, LANES)], axis=1)
        for b in range(3):
            moved = values if b == 1 else pltpu.roll(values, 1 if b == 0 else size - 1, 0)
            self.taps[slot, first : first + size, b * self.channels : (b + 1) * self.channels] = moved.astype(BF16)

    def begin(self):
        part = self.count // 2
        for first in range(0, self.count, part):
            self.keep(0, first, self.get(pl.ds(first, part)))

    def advance(self, first_round, flags, conv, gate_weight, bit_weight, waits):
        span, channels, rows = self.span, self.channels, self.rows
        lane = iota((1, LANES), 1)
        for step in range(HALF):
            t, slot = first_round + step, step % 2
            now = (lane == 2 * t) | (lane == 2 * t + 1) | (lane == LOW_LANE + 2 * t) | (lane == LOW_LANE + 2 * t + 1)
            self.bits[...] = flags[...] * one_hot(now | (lane >= ONE_LANE))
            total = rows - 2 * (step + 1)
            for begin, part_rows in ((step + 1, total),):
                first, size = begin * span, part_rows * span
                parts = [self.taps[slot, first + a * span : first + a * span + size] for a in (-1, 0, 1)]
                flag = self.bits[first : first + size]
                rounded = self.taps[slot, first : first + size, channels : 2 * channels]
                candidate = matmul(flag, bit_weight[:, :channels])
                if step == 0 and waits:
                    third = conv.shape[0] // 3
                    for a in range(3):
                        waits[a].wait()
                        candidate = candidate + matmul(parts[a], conv[a * third : (a + 1) * third])
                    waits[3].wait()
                else:
                    candidate = candidate + matmul(jnp.concatenate(parts, axis=1), conv[...])
                gate = matmul(rounded, gate_weight[...]) + matmul(flag, bit_weight[:, channels:])
                before = self.get(pl.ds(first, size))
                after = before + (0.5 * jnp.tanh(0.5 * gate) + 0.5) * (jnp.tanh(candidate) - before)
                self.put(pl.ds(first, size), after)
                if step < HALF - 1:
                    self.keep(1 - slot, first, after)

    def own(self, r):
        return self.get(pl.ds((self.width + r) * self.span + self.width, self.cols))


def patch_scratch(rows, cols, channels):
    count = (rows + 2 * HALF) * (cols + 2 * HALF)
    return [
        pltpu.VMEM((channels // LANES, count, LANES), F32),
        pltpu.VMEM((2, count, 3 * channels), BF16),
        pltpu.VMEM((count, LANES), BF16),
        pltpu.VMEM((count, LANES), F32),
    ]


def mask_of(flags):
    return matmul(flags, one_hot(iota((LANES, LANES), 0) == ONE_LANE))


def thirds(ref):
    size = ref.shape[0] // 3
    return [ref.at[a * size : (a + 1) * size] for a in range(3)]


def first_kernel(cols, place, top, bottom, *refs):
    halo, (region, bit_weight, conv_hbm, gate_hbm) = refs[:4], refs[4:8]
    (exact, kept, given, flags), new_patch = refs[8:12], refs[12:16]
    state, taps, bits, mask, flags_wide, conv, gate_weight, sems = refs[16:]
    copies = fetch((*thirds(conv_hbm), gate_hbm), (*thirds(conv), gate_weight), sems)
    for copy in copies:
        copy.start()
    patch = Patch(cols, state, taps, bits, mask)
    channels = patch.channels

    def put(at, values):
        patch.put(at, values[:, :channels])
        flags_wide[at] = values[:, channels:]

    patch.fill((top, bottom), halo, put)
    flags[...] = flags_wide[...].astype(BF16)
    mask[...] = mask_of(flags[...])
    patch.begin()
    patch.advance(0, flags, conv, gate_weight, bit_weight, copies)

    own = patch.rows - 2 * patch.width
    cells = [patch.own(r) for r in range(own)]
    for r in range(own):
        exact[r * cols : (r + 1) * cols] = cells[r]
    write_patch(new_patch, cells)
    block_cols = cols // 2
    half = kept.shape[0]
    total = jnp.zeros((2 * half, channels), F32)
    for r in range(0, own, 2):
        begin = (patch.width + r) * patch.span + patch.width
        parts = [
            patch.get(pl.ds(begin + a * patch.span + b, block_cols, stride=2)) for a in range(2) for b in range(2)
        ]
        pooled = (sum(parts[1:], parts[0]) * 0.25).astype(BF16)
        member = one_hot(iota((2 * half, block_cols), 0) == region[r // 2 : r // 2 + 1])
        total = total + matmul(member, pooled)
    is_first = place[1] == 0
    kept[...] = jnp.where(is_first, total[:half], total[half:])
    given[...] = jnp.where(is_first, total[half:], total[:half]).astype(BF16)


def repeat_into(out, values):
    count = values.shape[0]
    for at in range(0, out.shape[0], count):
        out[at : at + count] = values.astype(BF16)


def pair_kernel(kept, received, out):
    repeat_into(out, kept[...] + received[...].astype(F32))


def band_kernel(chips, pieces, out):
    values = pieces[...].astype(F32)
    count = values.shape[0] // chips
    parts = [values[p * count : (p + 1) * count] for p in range(chips)]
    repeat_into(out, sum(parts[1:], parts[0]))


def second_kernel(
    cols, bands, place, sums, other_sums, embed, flags, exact, above, below, left, right, attn_gain, mlp_gain, bit_weight,
    *refs
):
    sources, (state_out, context_out), refs = refs[:10], refs[10:12], refs[12:]
    state, taps, bits, mask, sums_all, tokens_all, normed_all, keys, values, member, tokens, normed = refs[:12]
    attention, hidden, context, sems = refs[12:16]
    targets = refs[16:]
    pool_weight, key_weight, value_weight, query_weight, out_weight = targets[:5]
    up_weight, down_weight, return_weight, gate_weight, conv = targets[5:]
    copies = fetch(sources, targets, sems)
    for copy in copies[:2]:
        copy.start()
    patch = Patch(cols, state, taps, bits, mask)
    own_half = place[1]

    half_tokens = sums.shape[0] // bands
    band_tokens = 2 * half_tokens
    for band in range(bands):
        at = pl.ds(band * half_tokens, half_tokens)
        pair = sums[at].astype(F32), other_sums[at].astype(F32)
        for half in range(2):
            part = jnp.where(own_half == half, *pair).astype(BF16)
            sums_all[pl.ds(band * band_tokens + half * half_tokens, half_tokens)] = part
    copies[0].wait()
    for copy in copies[2:4]:
        copy.start()
    for band in range(bands):
        at = pl.ds(band * band_tokens, band_tokens)
        total = embed[at].astype(F32) + matmul(sums_all[at], pool_weight[...])
        tokens_all[at] = total
        normed_all[at] = rms_norm(total, attn_gain[...]).astype(BF16)

    mask[...] = mask_of(flags[...])
    region = matmul(flags[...], one_hot(iota((LANES, LANES), 0) == REGION_LANE))
    member[...] = jnp.where(region == iota(region.shape, 1).astype(F32), 1.0, 0.0)

    g = place[0]
    own = pl.ds(pl.multiple_of(g * band_tokens, band_tokens), band_tokens)
    tokens[:band_tokens] = tokens_all[own]
    normed[:band_tokens] = normed_all[own]
    blocks = patch.span // 2
    room = (blocks + 7) // 8 * 8
    block_rows = patch.width // 2
    side = room * block_rows
    for number, (band, row) in enumerate(
        ((jnp.maximum(g - 1, 0), 0), (jnp.minimum(g + 1, bands - 1), patch.rows - patch.width))
    ):
        pick = jnp.concatenate(
            [member[pl.ds((row + 2 * r) * patch.span, room, stride=2)] for r in range(block_rows)]
        ).astype(BF16)
        at = pl.ds(pl.multiple_of(band * band_tokens, band_tokens), band_tokens)
        into = pl.ds(band_tokens + number * side, side)
        tokens[into] = select(pick, tokens_all[at])
        normed[into] = matmul(pick, normed_all[at]).astype(BF16)

    copies[1].wait()
    for copy in copies[4:6]:
        copy.start()
    keys[...] = matmul(normed_all[...], key_weight[...]).astype(BF16)
    copies[2].wait()
    for copy in copies[6:8]:
        copy.start()
    values[...] = matmul(normed_all[...], value_weight[...]).astype(BF16)
    copies[3].wait()
    queries = matmul(normed[...], query_weight[...]).astype(BF16)
    for head in range(HEADS):
        at = slice(head * HDIM, (head + 1) * HDIM)
        scores = matmul_nt(queries[:, at], keys[:, at]) * (1.0 / math.sqrt(HDIM))
        weights = jnp.exp(scores - jnp.max(scores, axis=-1, keepdims=True))
        denominator = jnp.sum(weights, axis=-1, keepdims=True)
        attention[:, at] = (matmul(weights.astype(BF16), values[:, at]) / denominator).astype(BF16)
    copies[4].wait()
    for copy in copies[8:]:
        copy.start()
    attended = tokens[...] + matmul(attention[...], out_weight[...])
    tokens[...] = attended
    normed[...] = rms_norm(attended, mlp_gain[...]).astype(BF16)
    copies[5].wait()
    part = 512
    for at in range(0, up_weight.shape[1], part):
        hidden[:, at : at + part] = jax.nn.gelu(matmul(normed[...], up_weight[:, at : at + part])).astype(BF16)
    copies[6].wait()
    context[...] = (tokens[...] + matmul(hidden[...], down_weight[...])).astype(BF16)
    context_out[...] = context[:band_tokens]
    copies[7].wait()
    returned = matmul(context[...], return_weight[...])

    patch.fill((exact,), (above, below, left, right), patch.put)
    first, last = patch.width * patch.span, (patch.rows - patch.width) * patch.span
    middle = pl.ds(first, last - first)
    patch.put(middle, patch.get(middle) + select(member[first:last].astype(BF16), returned[:band_tokens]))
    for number, row in enumerate((0, patch.rows - patch.width)):
        for r in range(patch.width):
            start = band_tokens + number * side + r // 2 * room
            share = returned[start : start + blocks]
            for c in range(2):
                at = pl.ds((row + r) * patch.span + c, blocks, stride=2)
                patch.put(at, patch.get(at) + share)

    patch.begin()
    copies[8].wait()
    copies[9].wait()
    patch.advance(HALF, flags, conv, gate_weight, bit_weight, ())
    for r in range(patch.rows - 2 * patch.width):
        state_out[r * cols : (r + 1) * cols] = patch.own(r).astype(BF16)


def local(
    syndrome_bits, region_assign, state_in, bit_to_candidate, bit_to_gate, conv_weight, gate_weight, gate_bias,
    pool_weight, region_embed, attn_norm_gain, query_weight, key_weight, value_weight, out_weight, mlp_norm_gain,
    mlp_up, mlp_down, return_weight,
):
    rows, cols, channels = state_in.shape
    band_tokens, embed_width = region_embed.shape
    bands, tiles = lax.axis_size("ctx"), math.prod(lax.axis_size(name) for name in TILE)
    conv = conv_weight.reshape(9 * channels, channels)
    place = jnp.stack([lax.axis_index("ctx"), lax.axis_index("core")]).astype(jnp.int32)
    swap = [(0, 1), (1, 0)]
    half = HALF * cols

    top, bottom, first, last = call(
        message_kernel,
        "message",
        (syndrome_bits.reshape(2 * ROUNDS, rows, cols), region_assign, state_in.reshape(rows * cols, channels)),
        patch_outputs(half, channels + LANES),
        grant=8,
    )
    above, below = row_halo(top, bottom)
    embed, _ = lax.optimization_barrier((region_embed, top))
    bit_weight, embed = call(
        prepare_kernel,
        "prepare",
        (bit_to_candidate, bit_to_gate, gate_bias[None], embed),
        [array(LANES, 2 * channels, BF16), array(bands * band_tokens, embed_width, BF16)],
        moved=8 * MIB,
    )
    embed, bit_weight, above, below, place = lax.optimization_barrier((embed, bit_weight, above, below, place))
    left, right = col_halo(cols, above, first, last, below)
    embed = lax.all_to_all(embed.reshape(bands, band_tokens, -1), "ctx", 0, 0).reshape(-1, embed_width)

    count = (rows + 2 * HALF) * (cols + 2 * HALF)
    flops = 15 * rows * cols * HALF * 2 * channels * channels
    exact, kept, given, flags, top, bottom, first, last = call(
        functools.partial(first_kernel, cols),
        "rounds",
        (place, top, bottom, above, below, left, right, region_assign, bit_weight, conv, gate_weight),
        [
            array(rows * cols, channels, F32), array(band_tokens // 2, channels, F32),
            array(band_tokens // 2, channels, BF16), array(count, LANES, BF16),
        ]
        + patch_outputs(half, channels),
        patch_scratch(rows, cols, channels)
        + [
            pltpu.VMEM((count, LANES), F32), pltpu.VMEM(conv.shape, BF16), pltpu.VMEM(gate_weight.shape, BF16),
            pltpu.SemaphoreType.DMA((4,)),
        ],
        in_hbm=(9, 10),
        scalars=(0,),
        flops=flops,
    )

    chips, half_tokens = tiles // 2, band_tokens // 2
    given, embed = lax.optimization_barrier((given, embed))
    received = lax.ppermute(given, "core", swap)
    (pieces,) = call(
        pair_kernel, "pair", (kept, received), [array(chips * half_tokens, channels, BF16)], grant=8
    )
    pieces = lax.all_to_all(pieces.reshape(chips, half_tokens, channels), "chip", 0, 0)
    left, right = shifted(last, TILE, 1), shifted(first, TILE, -1)
    up, down = call(
        rows_kernel,
        "rows",
        (top, bottom, left, right),
        [array(HALF * (cols + 2 * HALF), channels, BF16)] * 2,
        grant=8,
    )
    pieces, up, down = lax.optimization_barrier((pieces, up, down))
    (sums,) = call(
        functools.partial(band_kernel, chips),
        "band",
        (pieces.reshape(-1, channels),),
        [array(bands * half_tokens, channels, BF16)],
        grant=8,
    )
    up, down, sums = lax.optimization_barrier((up, down, sums))
    sums = lax.all_to_all(sums.reshape(bands, half_tokens, channels), "ctx", 0, 0)
    above, below = row_halo(up, down)
    sums, above, below = lax.optimization_barrier((sums.reshape(-1, channels), above, below))
    other_sums = lax.ppermute(sums, "core", swap)

    fetched = (
        pool_weight, key_weight, value_weight, query_weight, out_weight, mlp_up, mlp_down, return_weight, gate_weight,
        conv,
    )
    blocks = (cols + 2 * HALF) // 2
    layer_rows = band_tokens + HALF * ((blocks + 7) // 8 * 8)
    all_tokens = bands * band_tokens
    state, context = call(
        functools.partial(second_kernel, cols, bands),
        "context",
        (
            place, sums, other_sums, embed, flags, exact, above, below, left, right, attn_norm_gain[None],
            mlp_norm_gain[None], bit_weight, *fetched,
        ),
        [array(rows * cols, channels, BF16), array(band_tokens, embed_width, BF16)],
        patch_scratch(rows, cols, channels)
        + [
            pltpu.VMEM((all_tokens, channels), BF16),
            pltpu.VMEM((all_tokens, embed_width), F32), pltpu.VMEM((all_tokens, embed_width), BF16),
            pltpu.VMEM((all_tokens, embed_width), BF16), pltpu.VMEM((all_tokens, embed_width), BF16),
            pltpu.VMEM((count, LANES), F32),
            pltpu.VMEM((layer_rows, embed_width), F32), pltpu.VMEM((layer_rows, embed_width), BF16),
            pltpu.VMEM((layer_rows, embed_width), BF16), pltpu.VMEM((layer_rows, mlp_up.shape[1]), BF16),
            pltpu.VMEM((layer_rows, embed_width), BF16), pltpu.SemaphoreType.DMA((len(fetched),)),
        ]
        + [pltpu.VMEM(value.shape, value.dtype) for value in fetched],
        in_hbm=range(13, 13 + len(fetched)),
        scalars=(0,),
        flops=2 * flops,
    )
    return (state.reshape(rows, cols, channels), context)


def solution(mesh):
    bands, tiles = mesh.devices.shape
    split = jax.sharding.Mesh(mesh.devices.reshape(bands, tiles // 2, 2), ("ctx", *TILE))
    return jax.shard_map(
        local,
        mesh=split,
        in_specs=(
            P(None, None, "ctx", TILE),
            P("ctx", TILE),
            P("ctx", TILE, None),
            P(), P(), P(), P(), P(), P(),
            P("ctx", None),
            P(), P(), P(), P(), P(), P(), P(), P(), P(),
        ),
        out_specs=(P("ctx", TILE, None), P("ctx", None)),
        check_vma=False,
    )
```

```python
import functools
import math

import jax
import jax.numpy as jnp
from jax import lax
from jax.experimental import pallas as pl
from jax.experimental.pallas import tpu as pltpu
from jax.sharding import PartitionSpec as P

HEADS = 8
HDIM = 128
ROUNDS = 8
HALF = ROUNDS // 2
LANES = 128
F32 = jnp.float32
BF16 = jnp.bfloat16
MIB = 2**20

TILE = ("chip", "core")

REGION_LANE, LOW_LANE, ONE_LANE = 2 * ROUNDS, 32, 64


def shifted(value, axis, step):
    size = math.prod(lax.axis_size(name) for name in axis)
    pairs = [(i, i + step) for i in range(size) if 0 <= i + step < size]
    return lax.ppermute(value, axis, pairs)


def row_halo(top, bottom):
    return shifted(bottom, ("ctx",), 1), shifted(top, ("ctx",), -1)


def col_halo(cols, above, first, last, below):
    count, lanes = first.shape
    first, last = call(
        functools.partial(edges_kernel, cols),
        "edges",
        (above, first, last, below),
        [array(2 * count, lanes, BF16)] * 2,
        grant=8,
    )
    return shifted(last, TILE, 1), shifted(first, TILE, -1)


def matmul(left, right):
    return jnp.dot(left, right, preferred_element_type=F32)


def matmul_nt(left, right):
    return lax.dot_general(left, right, (((1,), (1,)), ((), ())), preferred_element_type=F32)


def two_parts(values):
    high = values.astype(BF16)
    return high, (values - high.astype(F32)).astype(BF16)


def select(member, values):
    high, low = two_parts(values)
    return matmul(member, high) + matmul(member, low)


def rms_norm(values, gain):
    return values * lax.rsqrt(jnp.mean(values * values, axis=-1, keepdims=True) + 1e-05) * gain


def iota(shape, dim):
    return lax.broadcasted_iota(jnp.int32, shape, dim)


def one_hot(condition):
    return jnp.where(condition, 1.0, 0.0).astype(BF16)


def call(kernel, name, operands, outs, scratch=(), in_hbm=(), scalars=(), grant=60, flops=0, moved=MIB):
    def spec(index):
        if index in in_hbm:
            return pl.BlockSpec(memory_space=pltpu.HBM)
        return pl.BlockSpec(memory_space=pltpu.SMEM if index in scalars else pltpu.VMEM)

    return pl.pallas_call(
        kernel,
        out_shape=outs,
        in_specs=[spec(index) for index in range(len(operands))],
        out_specs=[pl.BlockSpec(memory_space=pltpu.VMEM)] * len(outs),
        scratch_shapes=scratch,
        compiler_params=pltpu.CompilerParams(vmem_limit_bytes=grant * MIB),
        cost_estimate=pl.CostEstimate(flops=flops, bytes_accessed=moved, transcendentals=0),
        name=name,
    )(*operands)


def array(count, lanes, dtype):
    return jax.ShapeDtypeStruct((count, lanes), dtype)


def first_columns(part, cols, begin):
    values = part[...].astype(F32)
    return [values[at + begin : at + begin + HALF] for at in range(0, part.shape[0], cols)]


def edges_kernel(cols, above, own_first, own_last, below, first, last):
    for own, begin, out in ((own_first, 0, first), (own_last, cols - HALF, last)):
        parts = first_columns(above, cols, begin) + [own[...].astype(F32)] + first_columns(below, cols, begin)
        out[...] = jnp.concatenate(parts).astype(BF16)


def rows_kernel(top, bottom, left, right, up, down):
    sides = left[...].astype(F32), right[...].astype(F32)
    cols = top.shape[0] // HALF
    for number, (part, out) in enumerate(((top, up), (bottom, down))):
        values, cells = part[...].astype(F32), []
        for r in range(HALF):
            at = (number * HALF + r) * HALF
            before, after = (side[at : at + HALF] for side in sides)
            cells += [before, values[r * cols : (r + 1) * cols], after]
        out[...] = jnp.concatenate(cells).astype(BF16)


def patch_outputs(half, lanes):
    return [array(half, lanes, BF16)] * 2 + [array(2 * HALF * HALF, lanes, BF16)] * 2


def write_patch(outs, rows):
    top, bottom, first, last = outs
    cols = rows[0].shape[0]
    for r, values in enumerate(rows):
        half = (top, bottom)[r // HALF]
        half[r % HALF * cols : (r % HALF + 1) * cols] = values.astype(BF16)
    first[...] = jnp.concatenate([values[:HALF] for values in rows]).astype(BF16)
    last[...] = jnp.concatenate([values[cols - HALF :] for values in rows]).astype(BF16)


def message_kernel(syndrome, region, state, *outs):
    planes, rows, cols = syndrome.shape
    bits = syndrome[...].reshape(planes * rows, cols).astype(F32).astype(BF16)
    column_bits = matmul_nt(one_hot(iota((cols, cols), 0) == iota((cols, cols), 1)), bits).astype(BF16)
    block_rows, block_cols = region.shape
    regions = jnp.concatenate([region[...].astype(F32), jnp.zeros((8 - block_rows, block_cols), F32)])
    spread = one_hot(iota((cols, block_cols), 0) // 2 == iota((cols, block_cols), 1))
    column_region = matmul_nt(spread, regions.astype(BF16)).astype(BF16)
    plane, lane = iota((planes * rows, LANES), 0), iota((planes * rows, LANES), 1)
    ones = jnp.where((iota((cols, LANES), 1) == ONE_LANE) | (iota((cols, LANES), 1) == ONE_LANE + 1), 1.0, 0.0)
    cells = []
    for r in range(rows):
        place = one_hot((plane == lane * rows + r) | (plane == (lane - LOW_LANE) * rows + r))
        region_place = one_hot((iota((8, LANES), 0) == r // 2) & (iota((8, LANES), 1) == REGION_LANE))
        flags = matmul(column_bits, place) + matmul(column_region, region_place) + ones
        cells.append(jnp.concatenate([state[r * cols : (r + 1) * cols].astype(F32), flags], axis=1))
    write_patch(outs, cells)


def fetch(sources, targets, sems):
    return [pltpu.make_async_copy(*pair, sems.at[i]) for i, pair in enumerate(zip(sources, targets))]


def prepare_kernel(candidate_bits, gate_bits, bias, embed, bit_weight, spread):
    by_bit = jnp.concatenate([candidate_bits[...], gate_bits[...]], axis=1)
    bias = jnp.concatenate([jnp.zeros_like(bias), bias[...]], axis=1)
    lane = iota((LANES, 1), 0)
    weight = jnp.zeros(bit_weight.shape, F32)
    for part in range(2):
        begin = (0, LOW_LANE)[part]
        for bit in range(2):
            row = two_parts(by_bit[bit : bit + 1])[part].astype(F32)
            here = (lane >= begin) & (lane < begin + 2 * ROUNDS) & (lane % 2 == bit)
            weight = jnp.where(here, row, weight)
        weight = jnp.where(lane == ONE_LANE + part, two_parts(bias)[part].astype(F32), weight)
    bit_weight[...] = weight.astype(BF16)
    for at in range(0, spread.shape[0], embed.shape[0]):
        spread[at : at + embed.shape[0]] = embed[...]


class Patch:
    def __init__(self, cols, state, taps, bits, mask):
        self.cols, self.span, self.width = cols, cols + 2 * HALF, HALF
        self.state, self.taps, self.bits, self.mask = state, taps, bits, mask
        self.groups, self.count = state.shape[:2]
        self.rows, self.channels = self.count // self.span, self.groups * LANES

    def get(self, at):
        return jnp.concatenate([self.state[j, at] for j in range(self.groups)], axis=1)

    def put(self, at, values):
        for j in range(self.groups):
            self.state[j, at] = values[:, j * LANES : (j + 1) * LANES]

    def fill(self, parts, halo, put):
        above, below, left, right = halo
        r = 0
        for part, part_rows in (
            (above, self.width), *((part, part.shape[0] // self.cols) for part in parts), (below, self.width)
        ):
            length = part.shape[0] // part_rows
            for at in range(0, part.shape[0], length):
                put(pl.ds(r * self.span + (self.span - length) // 2, length), part[at : at + length].astype(F32))
                r += 1
        for part, first in ((left, 0), (right, self.width + self.cols)):
            values = part[...].astype(F32)
            side_rows = values.shape[0] // self.width
            for r in range(side_rows):
                at = (r + (self.rows - side_rows) // 2) * self.span + first
                put(pl.ds(at, self.width), values[r * self.width : (r + 1) * self.width])

    def keep(self, slot, first, values):
        size = values.shape[0]
        mask = self.mask[first : first + size]
        values = jnp.concatenate([values[:, c : c + LANES] * mask for c in range(0, self.channels, LANES)], axis=1)
        for b in range(3):
            moved = values if b == 1 else pltpu.roll(values, 1 if b == 0 else size - 1, 0)
            self.taps[slot, first : first + size, b * self.channels : (b + 1) * self.channels] = moved.astype(BF16)

    def begin(self):
        part = self.count // 2
        for first in range(0, self.count, part):
            self.keep(0, first, self.get(pl.ds(first, part)))

    def advance(self, first_round, flags, conv, gate_weight, bit_weight, waits):
        span, channels, rows = self.span, self.channels, self.rows
        lane = iota((1, LANES), 1)
        for step in range(HALF):
            t, slot = first_round + step, step % 2
            now = (lane == 2 * t) | (lane == 2 * t + 1) | (lane == LOW_LANE + 2 * t) | (lane == LOW_LANE + 2 * t + 1)
            self.bits[...] = flags[...] * one_hot(now | (lane >= ONE_LANE))
            total = rows - 2 * (step + 1)
            for begin, part_rows in ((step + 1, total),):
                first, size = begin * span, part_rows * span
                parts = [self.taps[slot, first + a * span : first + a * span + size] for a in (-1, 0, 1)]
                flag = self.bits[first : first + size]
                rounded = self.taps[slot, first : first + size, channels : 2 * channels]
                candidate = matmul(flag, bit_weight[:, :channels])
                if step == 0 and waits:
                    third = conv.shape[0] // 3
                    for a in range(3):
                        waits[a].wait()
                        candidate = candidate + matmul(parts[a], conv[a * third : (a + 1) * third])
                    waits[3].wait()
                else:
                    candidate = candidate + matmul(jnp.concatenate(parts, axis=1), conv[...])
                gate = matmul(rounded, gate_weight[...]) + matmul(flag, bit_weight[:, channels:])
                before = self.get(pl.ds(first, size))
                after = before + (0.5 * jnp.tanh(0.5 * gate) + 0.5) * (jnp.tanh(candidate) - before)
                self.put(pl.ds(first, size), after)
                if step < HALF - 1:
                    self.keep(1 - slot, first, after)

    def own(self, r):
        return self.get(pl.ds((self.width + r) * self.span + self.width, self.cols))


def patch_scratch(rows, cols, channels):
    count = (rows + 2 * HALF) * (cols + 2 * HALF)
    return [
        pltpu.VMEM((channels // LANES, count, LANES), F32),
        pltpu.VMEM((2, count, 3 * channels), BF16),
        pltpu.VMEM((count, LANES), BF16),
        pltpu.VMEM((count, LANES), F32),
    ]


def mask_of(flags):
    return matmul(flags, one_hot(iota((LANES, LANES), 0) == ONE_LANE))


def thirds(ref):
    size = ref.shape[0] // 3
    return [ref.at[a * size : (a + 1) * size] for a in range(3)]


def first_kernel(cols, place, top, bottom, *refs):
    halo, (region, bit_weight, conv_hbm, gate_hbm) = refs[:4], refs[4:8]
    (exact, kept, given, flags), new_patch = refs[8:12], refs[12:16]
    state, taps, bits, mask, flags_wide, conv, gate_weight, sems = refs[16:]
    copies = fetch((*thirds(conv_hbm), gate_hbm), (*thirds(conv), gate_weight), sems)
    for copy in copies:
        copy.start()
    patch = Patch(cols, state, taps, bits, mask)
    channels = patch.channels

    def put(at, values):
        patch.put(at, values[:, :channels])
        flags_wide[at] = values[:, channels:]

    patch.fill((top, bottom), halo, put)
    flags[...] = flags_wide[...].astype(BF16)
    mask[...] = mask_of(flags[...])
    patch.begin()
    patch.advance(0, flags, conv, gate_weight, bit_weight, copies)

    own = patch.rows - 2 * patch.width
    cells = [patch.own(r) for r in range(own)]
    for r in range(own):
        exact[r * cols : (r + 1) * cols] = cells[r]
    write_patch(new_patch, cells)
    block_cols = cols // 2
    half = kept.shape[0]
    total = jnp.zeros((2 * half, channels), F32)
    for r in range(0, own, 2):
        begin = (patch.width + r) * patch.span + patch.width
        parts = [
            patch.get(pl.ds(begin + a * patch.span + b, block_cols, stride=2)) for a in range(2) for b in range(2)
        ]
        pooled = (sum(parts[1:], parts[0]) * 0.25).astype(BF16)
        member = one_hot(iota((2 * half, block_cols), 0) == region[r // 2 : r // 2 + 1])
        total = total + matmul(member, pooled)
    is_first = place[1] == 0
    kept[...] = jnp.where(is_first, total[:half], total[half:])
    given[...] = jnp.where(is_first, total[half:], total[:half]).astype(BF16)


def repeat_into(out, values):
    count = values.shape[0]
    for at in range(0, out.shape[0], count):
        out[at : at + count] = values.astype(BF16)


def pair_kernel(kept, received, out):
    repeat_into(out, kept[...] + received[...].astype(F32))


def band_kernel(chips, pieces, out):
    values = pieces[...].astype(F32)
    count = values.shape[0] // chips
    parts = [values[p * count : (p + 1) * count] for p in range(chips)]
    repeat_into(out, sum(parts[1:], parts[0]))


def member_of(flags):
    region = matmul(flags, one_hot(iota((LANES, LANES), 0) == REGION_LANE))
    return jnp.where(region == iota(region.shape, 1).astype(F32), 1.0, 0.0)


def layer_rooms(cols):
    blocks = (cols + 2 * HALF) // 2
    return blocks, (blocks + 7) // 8 * 8, HALF // 2


def context_kernel(cols, bands, place, sums, other_sums, attn_gain, mlp_gain, flags, *refs):
    sources, (context_out, returned_out), targets, refs = refs[:9], refs[9:11], refs[11:20], refs[20:]
    sums_all, tokens_all, normed_all, keys, values, member, tokens, normed, attention, hidden, context, sems = refs
    embed, pool_weight, key_weight, value_weight, query_weight, out_weight, up_weight, down_weight, return_weight = targets
    copies = fetch(sources, targets, sems)
    for copy in copies[:4]:
        copy.start()
    g, own_half = place[0], place[1]

    half_tokens = sums.shape[0] // bands
    band_tokens = 2 * half_tokens
    for band in range(bands):
        at = pl.ds(band * half_tokens, half_tokens)
        pair = sums[at].astype(F32), other_sums[at].astype(F32)
        for half in range(2):
            part = jnp.where(own_half == half, *pair).astype(BF16)
            sums_all[pl.ds(band * band_tokens + half * half_tokens, half_tokens)] = part
    member[...] = member_of(flags[...])
    copies[0].wait()
    copies[1].wait()
    for copy in copies[4:7]:
        copy.start()
    total = embed[...].astype(F32) + matmul(sums_all[...], pool_weight[...])
    tokens_all[...] = total
    normed_all[...] = rms_norm(total, attn_gain[...]).astype(BF16)

    own = pl.ds(pl.multiple_of(g * band_tokens, band_tokens), band_tokens)
    tokens[:band_tokens] = tokens_all[own]
    normed[:band_tokens] = normed_all[own]
    _, room, block_rows = layer_rooms(cols)
    side, span = room * block_rows, cols + 2 * HALF
    for number, (band, row) in enumerate(
        ((jnp.maximum(g - 1, 0), 0), (jnp.minimum(g + 1, bands - 1), flags.shape[0] // span - HALF))
    ):
        pick = jnp.concatenate([member[pl.ds((row + 2 * r) * span, room, stride=2)] for r in range(block_rows)])
        pick = pick.astype(BF16)
        at = pl.ds(pl.multiple_of(band * band_tokens, band_tokens), band_tokens)
        into = pl.ds(band_tokens + number * side, side)
        tokens[into] = select(pick, tokens_all[at])
        normed[into] = matmul(pick, normed_all[at]).astype(BF16)

    copies[2].wait()
    keys[...] = matmul(normed_all[...], key_weight[...]).astype(BF16)
    copies[3].wait()
    for copy in copies[7:]:
        copy.start()
    values[...] = matmul(normed_all[...], value_weight[...]).astype(BF16)
    copies[4].wait()
    queries = matmul(normed[...], query_weight[...]).astype(BF16)
    for head in range(HEADS):
        at = slice(head * HDIM, (head + 1) * HDIM)
        scores = matmul_nt(queries[:, at], keys[:, at]) * (1.0 / math.sqrt(HDIM))
        weights = jnp.exp(scores - jnp.max(scores, axis=-1, keepdims=True))
        denominator = jnp.sum(weights, axis=-1, keepdims=True)
        attention[:, at] = (matmul(weights.astype(BF16), values[:, at]) / denominator).astype(BF16)
    copies[5].wait()
    attended = tokens[...] + matmul(attention[...], out_weight[...])
    tokens[...] = attended
    normed[...] = rms_norm(attended, mlp_gain[...]).astype(BF16)
    copies[6].wait()
    part = 512
    for at in range(0, up_weight.shape[1], part):
        hidden[:, at : at + part] = jax.nn.gelu(matmul(normed[...], up_weight[:, at : at + part])).astype(BF16)
    copies[7].wait()
    context[...] = (tokens[...] + matmul(hidden[...], down_weight[...])).astype(BF16)
    context_out[...] = context[:band_tokens]
    copies[8].wait()
    returned_out[...] = matmul(context[...], return_weight[...])


def second_kernel(
    cols, exact, above, below, left, right, flags, returned, bit_weight, conv_hbm, gate_hbm, state_out,
    state, taps, bits, mask, conv, gate_weight, sems,
):
    copies = fetch((*thirds(conv_hbm), gate_hbm), (*thirds(conv), gate_weight), sems)
    for copy in copies:
        copy.start()
    patch = Patch(cols, state, taps, bits, mask)
    patch.fill((exact,), (above, below, left, right), patch.put)
    mask[...] = mask_of(flags[...])
    blocks, room, block_rows = layer_rooms(cols)
    side = room * block_rows
    band_tokens = returned.shape[0] - 2 * side
    first, last = patch.width * patch.span, (patch.rows - patch.width) * patch.span
    middle = pl.ds(first, last - first)
    member = member_of(flags[middle]).astype(BF16)
    patch.put(middle, patch.get(middle) + select(member, returned[:band_tokens]))
    for number, row in enumerate((0, patch.rows - patch.width)):
        for r in range(patch.width):
            start = band_tokens + number * side + r // 2 * room
            share = returned[start : start + blocks]
            for c in range(2):
                at = pl.ds((row + r) * patch.span + c, blocks, stride=2)
                patch.put(at, patch.get(at) + share)
    patch.begin()
    patch.advance(HALF, flags, conv, gate_weight, bit_weight, copies)
    for r in range(patch.rows - 2 * patch.width):
        state_out[r * cols : (r + 1) * cols] = patch.own(r).astype(BF16)


def local(
    syndrome_bits, region_assign, state_in, bit_to_candidate, bit_to_gate, conv_weight, gate_weight, gate_bias,
    pool_weight, region_embed, attn_norm_gain, query_weight, key_weight, value_weight, out_weight, mlp_norm_gain,
    mlp_up, mlp_down, return_weight,
):
    rows, cols, channels = state_in.shape
    band_tokens, embed_width = region_embed.shape
    bands, tiles = lax.axis_size("ctx"), math.prod(lax.axis_size(name) for name in TILE)
    conv = conv_weight.reshape(9 * channels, channels)
    place = jnp.stack([lax.axis_index("ctx"), lax.axis_index("core")]).astype(jnp.int32)
    swap = [(0, 1), (1, 0)]
    half = HALF * cols

    top, bottom, first, last = call(
        message_kernel,
        "message",
        (syndrome_bits.reshape(2 * ROUNDS, rows, cols), region_assign, state_in.reshape(rows * cols, channels)),
        patch_outputs(half, channels + LANES),
        grant=8,
    )
    above, below = row_halo(top, bottom)
    embed, _ = lax.optimization_barrier((region_embed, top))
    bit_weight, embed = call(
        prepare_kernel,
        "prepare",
        (bit_to_candidate, bit_to_gate, gate_bias[None], embed),
        [array(LANES, 2 * channels, BF16), array(bands * band_tokens, embed_width, BF16)],
        moved=8 * MIB,
    )
    embed, bit_weight, above, below, place = lax.optimization_barrier((embed, bit_weight, above, below, place))
    left, right = col_halo(cols, above, first, last, below)
    embed = lax.all_to_all(embed.reshape(bands, band_tokens, -1), "ctx", 0, 0).reshape(-1, embed_width)

    count = (rows + 2 * HALF) * (cols + 2 * HALF)
    flops = 15 * rows * cols * HALF * 2 * channels * channels
    exact, kept, given, flags, top, bottom, first, last = call(
        functools.partial(first_kernel, cols),
        "rounds",
        (place, top, bottom, above, below, left, right, region_assign, bit_weight, conv, gate_weight),
        [
            array(rows * cols, channels, F32), array(band_tokens // 2, channels, F32),
            array(band_tokens // 2, channels, BF16), array(count, LANES, BF16),
        ]
        + patch_outputs(half, channels),
        patch_scratch(rows, cols, channels)
        + [
            pltpu.VMEM((count, LANES), F32), pltpu.VMEM(conv.shape, BF16), pltpu.VMEM(gate_weight.shape, BF16),
            pltpu.SemaphoreType.DMA((4,)),
        ],
        in_hbm=(9, 10),
        scalars=(0,),
        flops=flops,
    )

    chips, half_tokens = tiles // 2, band_tokens // 2
    given, embed = lax.optimization_barrier((given, embed))
    received = lax.ppermute(given, "core", swap)
    (pieces,) = call(
        pair_kernel, "pair", (kept, received), [array(chips * half_tokens, channels, BF16)], grant=8
    )
    pieces = lax.all_to_all(pieces.reshape(chips, half_tokens, channels), "chip", 0, 0)
    left, right = shifted(last, TILE, 1), shifted(first, TILE, -1)
    up, down = call(
        rows_kernel,
        "rows",
        (top, bottom, left, right),
        [array(HALF * (cols + 2 * HALF), channels, BF16)] * 2,
        grant=8,
    )
    pieces, up, down = lax.optimization_barrier((pieces, up, down))
    (sums,) = call(
        functools.partial(band_kernel, chips),
        "band",
        (pieces.reshape(-1, channels),),
        [array(bands * half_tokens, channels, BF16)],
        grant=8,
    )
    up, down, sums = lax.optimization_barrier((up, down, sums))
    sums = lax.all_to_all(sums.reshape(bands, half_tokens, channels), "ctx", 0, 0)
    above, below = row_halo(up, down)
    sums = sums.reshape(-1, channels)
    other_sums = lax.ppermute(sums, "core", swap)

    layer = (
        embed, pool_weight, key_weight, value_weight, query_weight, out_weight, mlp_up, mlp_down, return_weight,
    )
    _, room, block_rows = layer_rooms(cols)
    layer_rows = band_tokens + 2 * room * block_rows
    all_tokens = bands * band_tokens
    mlp = mlp_up.shape[1]
    context, returned = call(
        functools.partial(context_kernel, cols, bands),
        "context",
        (place, sums, other_sums, attn_norm_gain[None], mlp_norm_gain[None], flags, *layer),
        [array(band_tokens, embed_width, BF16), array(layer_rows, channels, F32)],
        [pltpu.VMEM(value.shape, value.dtype) for value in layer]
        + [
            pltpu.VMEM((all_tokens, channels), BF16),
            pltpu.VMEM((all_tokens, embed_width), F32), pltpu.VMEM((all_tokens, embed_width), BF16),
            pltpu.VMEM((all_tokens, embed_width), BF16), pltpu.VMEM((all_tokens, embed_width), BF16),
            pltpu.VMEM((count, LANES), F32),
            pltpu.VMEM((layer_rows, embed_width), F32), pltpu.VMEM((layer_rows, embed_width), BF16),
            pltpu.VMEM((layer_rows, embed_width), BF16), pltpu.VMEM((layer_rows, mlp), BF16),
            pltpu.VMEM((layer_rows, embed_width), BF16), pltpu.SemaphoreType.DMA((len(layer),)),
        ],
        in_hbm=range(6, 6 + len(layer)),
        scalars=(0,),
        flops=2 * embed_width * (all_tokens * (channels + 2 * embed_width) + layer_rows * (2 * embed_width + 2 * mlp)),
        moved=20 * MIB,
    )
    (state,) = call(
        functools.partial(second_kernel, cols),
        "rounds",
        (exact, above, below, left, right, flags, returned, bit_weight, conv, gate_weight),
        [array(rows * cols, channels, BF16)],
        patch_scratch(rows, cols, channels)
        + [pltpu.VMEM(conv.shape, BF16), pltpu.VMEM(gate_weight.shape, BF16), pltpu.SemaphoreType.DMA((4,))],
        in_hbm=(8, 9),
        flops=flops,
    )
    return (state.reshape(rows, cols, channels), context)


def solution(mesh):
    bands, tiles = mesh.devices.shape
    split = jax.sharding.Mesh(mesh.devices.reshape(bands, tiles // 2, 2), ("ctx", *TILE))
    return jax.shard_map(
        local,
        mesh=split,
        in_specs=(
            P(None, None, "ctx", TILE),
            P("ctx", TILE),
            P("ctx", TILE, None),
            P(), P(), P(), P(), P(), P(),
            P("ctx", None),
            P(), P(), P(), P(), P(), P(), P(), P(), P(),
        ),
        out_specs=(P("ctx", TILE, None), P("ctx", None)),
        check_vma=False,
    )
```

```python
import functools
import math

import jax
import jax.numpy as jnp
from jax import lax
from jax.experimental import pallas as pl
from jax.experimental.pallas import tpu as pltpu
from jax.sharding import PartitionSpec as P

HEADS = 8
HDIM = 128
ROUNDS = 8
HALF = ROUNDS // 2
LANES = 128
F32 = jnp.float32
BF16 = jnp.bfloat16
MIB = 2**20

TILE = ("chip", "core")

REGION_LANE, LOW_LANE, ONE_LANE = 2 * ROUNDS, 32, 64


def shifted(value, axis, step):
    size = math.prod(lax.axis_size(name) for name in axis)
    pairs = [(i, i + step) for i in range(size) if 0 <= i + step < size]
    return lax.ppermute(value, axis, pairs)


def row_halo(top, bottom):
    return shifted(bottom, ("ctx",), 1), shifted(top, ("ctx",), -1)


def col_halo(cols, above, first, last, below):
    count, lanes = first.shape
    first, last = call(
        functools.partial(edges_kernel, cols),
        "edges",
        (above, first, last, below),
        [array(2 * count, lanes, BF16)] * 2,
        grant=8,
    )
    return shifted(last, TILE, 1), shifted(first, TILE, -1)


def matmul(left, right):
    return jnp.dot(left, right, preferred_element_type=F32)


def matmul_nt(left, right):
    return lax.dot_general(left, right, (((1,), (1,)), ((), ())), preferred_element_type=F32)


def two_parts(values):
    high = values.astype(BF16)
    return high, (values - high.astype(F32)).astype(BF16)


def select(member, values):
    high, low = two_parts(values)
    return matmul(member, high) + matmul(member, low)


def rms_norm(values, gain):
    return values * lax.rsqrt(jnp.mean(values * values, axis=-1, keepdims=True) + 1e-05) * gain


def iota(shape, dim):
    return lax.broadcasted_iota(jnp.int32, shape, dim)


def one_hot(condition):
    return jnp.where(condition, 1.0, 0.0).astype(BF16)


def call(kernel, name, operands, outs, scratch=(), in_hbm=(), scalars=(), grant=60, flops=0, moved=MIB):
    def spec(index):
        if index in in_hbm:
            return pl.BlockSpec(memory_space=pltpu.HBM)
        return pl.BlockSpec(memory_space=pltpu.SMEM if index in scalars else pltpu.VMEM)

    return pl.pallas_call(
        kernel,
        out_shape=outs,
        in_specs=[spec(index) for index in range(len(operands))],
        out_specs=[pl.BlockSpec(memory_space=pltpu.VMEM)] * len(outs),
        scratch_shapes=scratch,
        compiler_params=pltpu.CompilerParams(vmem_limit_bytes=grant * MIB),
        cost_estimate=pl.CostEstimate(flops=flops, bytes_accessed=moved, transcendentals=0),
        name=name,
    )(*operands)


def array(count, lanes, dtype):
    return jax.ShapeDtypeStruct((count, lanes), dtype)


def first_columns(part, cols, begin):
    values = part[...].astype(F32)
    return [values[at + begin : at + begin + HALF] for at in range(0, part.shape[0], cols)]


def edges_kernel(cols, above, own_first, own_last, below, first, last):
    for own, begin, out in ((own_first, 0, first), (own_last, cols - HALF, last)):
        parts = first_columns(above, cols, begin) + [own[...].astype(F32)] + first_columns(below, cols, begin)
        out[...] = jnp.concatenate(parts).astype(BF16)


def rows_kernel(top, bottom, left, right, up, down):
    sides = left[...].astype(F32), right[...].astype(F32)
    cols = top.shape[0] // HALF
    for number, (part, out) in enumerate(((top, up), (bottom, down))):
        values, cells = part[...].astype(F32), []
        for r in range(HALF):
            at = (number * HALF + r) * HALF
            before, after = (side[at : at + HALF] for side in sides)
            cells += [before, values[r * cols : (r + 1) * cols], after]
        out[...] = jnp.concatenate(cells).astype(BF16)


def patch_outputs(half, lanes):
    return [array(half, lanes, BF16)] * 2 + [array(2 * HALF * HALF, lanes, BF16)] * 2


def write_patch(outs, rows):
    top, bottom, first, last = outs
    cols = rows[0].shape[0]
    for r, values in enumerate(rows):
        half = (top, bottom)[r // HALF]
        half[r % HALF * cols : (r % HALF + 1) * cols] = values.astype(BF16)
    first[...] = jnp.concatenate([values[:HALF] for values in rows]).astype(BF16)
    last[...] = jnp.concatenate([values[cols - HALF :] for values in rows]).astype(BF16)


def message_kernel(syndrome, region, state, *outs):
    planes, rows, cols = syndrome.shape
    bits = syndrome[...].reshape(planes * rows, cols).astype(F32).astype(BF16)
    column_bits = matmul_nt(one_hot(iota((cols, cols), 0) == iota((cols, cols), 1)), bits).astype(BF16)
    block_rows, block_cols = region.shape
    regions = jnp.concatenate([region[...].astype(F32), jnp.zeros((8 - block_rows, block_cols), F32)])
    spread = one_hot(iota((cols, block_cols), 0) // 2 == iota((cols, block_cols), 1))
    column_region = matmul_nt(spread, regions.astype(BF16)).astype(BF16)
    plane, lane = iota((planes * rows, LANES), 0), iota((planes * rows, LANES), 1)
    ones = jnp.where((iota((cols, LANES), 1) == ONE_LANE) | (iota((cols, LANES), 1) == ONE_LANE + 1), 1.0, 0.0)
    cells = []
    for r in range(rows):
        place = one_hot((plane == lane * rows + r) | (plane == (lane - LOW_LANE) * rows + r))
        region_place = one_hot((iota((8, LANES), 0) == r // 2) & (iota((8, LANES), 1) == REGION_LANE))
        flags = matmul(column_bits, place) + matmul(column_region, region_place) + ones
        cells.append(jnp.concatenate([state[r * cols : (r + 1) * cols].astype(F32), flags], axis=1))
    write_patch(outs, cells)


def fetch(sources, targets, sems):
    return [pltpu.make_async_copy(*pair, sems.at[i]) for i, pair in enumerate(zip(sources, targets))]


def prepare_kernel(candidate_bits, gate_bits, bias, embed, bit_weight, spread):
    by_bit = jnp.concatenate([candidate_bits[...], gate_bits[...]], axis=1)
    bias = jnp.concatenate([jnp.zeros_like(bias), bias[...]], axis=1)
    lane = iota((LANES, 1), 0)
    weight = jnp.zeros(bit_weight.shape, F32)
    for part in range(2):
        begin = (0, LOW_LANE)[part]
        for bit in range(2):
            row = two_parts(by_bit[bit : bit + 1])[part].astype(F32)
            here = (lane >= begin) & (lane < begin + 2 * ROUNDS) & (lane % 2 == bit)
            weight = jnp.where(here, row, weight)
        weight = jnp.where(lane == ONE_LANE + part, two_parts(bias)[part].astype(F32), weight)
    bit_weight[...] = weight.astype(BF16)
    for at in range(0, spread.shape[0], embed.shape[0]):
        spread[at : at + embed.shape[0]] = embed[...]


class Patch:
    def __init__(self, cols, state, taps, bits, mask):
        self.cols, self.span, self.width = cols, cols + 2 * HALF, HALF
        self.state, self.taps, self.bits, self.mask = state, taps, bits, mask
        self.groups, self.count = state.shape[:2]
        self.rows, self.channels = self.count // self.span, self.groups * LANES

    def get(self, at):
        return jnp.concatenate([self.state[j, at] for j in range(self.groups)], axis=1)

    def put(self, at, values):
        for j in range(self.groups):
            self.state[j, at] = values[:, j * LANES : (j + 1) * LANES]

    def fill(self, parts, halo, put):
        above, below, left, right = halo
        r = 0
        for part, part_rows in (
            (above, self.width), *((part, part.shape[0] // self.cols) for part in parts), (below, self.width)
        ):
            length = part.shape[0] // part_rows
            for at in range(0, part.shape[0], length):
                put(pl.ds(r * self.span + (self.span - length) // 2, length), part[at : at + length].astype(F32))
                r += 1
        for part, first in ((left, 0), (right, self.width + self.cols)):
            values = part[...].astype(F32)
            side_rows = values.shape[0] // self.width
            for r in range(side_rows):
                at = (r + (self.rows - side_rows) // 2) * self.span + first
                put(pl.ds(at, self.width), values[r * self.width : (r + 1) * self.width])

    def keep(self, slot, first, values):
        size = values.shape[0]
        mask = self.mask[first : first + size]
        values = jnp.concatenate([values[:, c : c + LANES] * mask for c in range(0, self.channels, LANES)], axis=1)
        for b in range(3):
            moved = values if b == 1 else pltpu.roll(values, 1 if b == 0 else size - 1, 0)
            self.taps[slot, first : first + size, b * self.channels : (b + 1) * self.channels] = moved.astype(BF16)

    def begin(self):
        part = self.count // 2
        for first in range(0, self.count, part):
            self.keep(0, first, self.get(pl.ds(first, part)))

    def advance(self, first_round, flags, conv, gate_weight, bit_weight, waits):
        span, channels, rows = self.span, self.channels, self.rows
        lane = iota((1, LANES), 1)
        for step in range(HALF):
            t, slot = first_round + step, step % 2
            now = (lane == 2 * t) | (lane == 2 * t + 1) | (lane == LOW_LANE + 2 * t) | (lane == LOW_LANE + 2 * t + 1)
            self.bits[...] = flags[...] * one_hot(now | (lane >= ONE_LANE))
            total = rows - 2 * (step + 1)
            for begin, part_rows in ((step + 1, total),):
                first, size = begin * span, part_rows * span
                parts = [self.taps[slot, first + a * span : first + a * span + size] for a in (-1, 0, 1)]
                flag = self.bits[first : first + size]
                rounded = self.taps[slot, first : first + size, channels : 2 * channels]
                candidate = matmul(flag, bit_weight[:, :channels])
                if step == 0 and waits:
                    third = conv.shape[0] // 3
                    for a in range(3):
                        waits[a].wait()
                        candidate = candidate + matmul(parts[a], conv[a * third : (a + 1) * third])
                    waits[3].wait()
                else:
                    candidate = candidate + matmul(jnp.concatenate(parts, axis=1), conv[...])
                gate = matmul(rounded, gate_weight[...]) + matmul(flag, bit_weight[:, channels:])
                before = self.get(pl.ds(first, size))
                after = before + (0.5 * jnp.tanh(0.5 * gate) + 0.5) * (jnp.tanh(candidate) - before)
                self.put(pl.ds(first, size), after)
                if step < HALF - 1:
                    self.keep(1 - slot, first, after)

    def own(self, r):
        return self.get(pl.ds((self.width + r) * self.span + self.width, self.cols))


def patch_scratch(rows, cols, channels):
    count = (rows + 2 * HALF) * (cols + 2 * HALF)
    return [
        pltpu.VMEM((channels // LANES, count, LANES), F32),
        pltpu.VMEM((2, count, 3 * channels), BF16),
        pltpu.VMEM((count, LANES), BF16),
        pltpu.VMEM((count, LANES), F32),
    ]


def mask_of(flags):
    return matmul(flags, one_hot(iota((LANES, LANES), 0) == ONE_LANE))


def thirds(ref):
    size = ref.shape[0] // 3
    return [ref.at[a * size : (a + 1) * size] for a in range(3)]


def first_kernel(cols, place, top, bottom, *refs):
    halo, (region, bit_weight, conv_hbm, gate_hbm) = refs[:4], refs[4:8]
    (exact, kept, given, flags), new_patch = refs[8:12], refs[12:16]
    state, taps, bits, mask, flags_wide, conv, gate_weight, sems = refs[16:]
    copies = fetch((*thirds(conv_hbm), gate_hbm), (*thirds(conv), gate_weight), sems)
    for copy in copies:
        copy.start()
    patch = Patch(cols, state, taps, bits, mask)
    channels = patch.channels

    def put(at, values):
        patch.put(at, values[:, :channels])
        flags_wide[at] = values[:, channels:]

    patch.fill((top, bottom), halo, put)
    flags[...] = flags_wide[...].astype(BF16)
    mask[...] = mask_of(flags[...])
    patch.begin()
    patch.advance(0, flags, conv, gate_weight, bit_weight, copies)

    own = patch.rows - 2 * patch.width
    cells = [patch.own(r) for r in range(own)]
    for r in range(own):
        exact[r * cols : (r + 1) * cols] = cells[r]
    write_patch(new_patch, cells)
    block_cols = cols // 2
    half = kept.shape[0]
    total = jnp.zeros((2 * half, channels), F32)
    for r in range(0, own, 2):
        begin = (patch.width + r) * patch.span + patch.width
        parts = [
            patch.get(pl.ds(begin + a * patch.span + b, block_cols, stride=2)) for a in range(2) for b in range(2)
        ]
        pooled = (sum(parts[1:], parts[0]) * 0.25).astype(BF16)
        member = one_hot(iota((2 * half, block_cols), 0) == region[r // 2 : r // 2 + 1])
        total = total + matmul(member, pooled)
    is_first = place[1] == 0
    kept[...] = jnp.where(is_first, total[:half], total[half:])
    given[...] = jnp.where(is_first, total[half:], total[:half]).astype(BF16)


def repeat_into(out, values):
    count = values.shape[0]
    for at in range(0, out.shape[0], count):
        out[at : at + count] = values.astype(BF16)


def pair_kernel(kept, received, out):
    repeat_into(out, kept[...] + received[...].astype(F32))


def band_kernel(chips, pieces, out):
    values = pieces[...].astype(F32)
    count = values.shape[0] // chips
    parts = [values[p * count : (p + 1) * count] for p in range(chips)]
    repeat_into(out, sum(parts[1:], parts[0]))


def member_of(flags):
    region = matmul(flags, one_hot(iota((LANES, LANES), 0) == REGION_LANE))
    return jnp.where(region == iota(region.shape, 1).astype(F32), 1.0, 0.0)


def layer_rooms(cols):
    blocks = (cols + 2 * HALF) // 2
    return blocks, (blocks + 7) // 8 * 8, HALF // 2


def context_kernel(cols, bands, place, sums, other_sums, attn_gain, mlp_gain, flags, *refs):
    sources, (context_out, returned_out), targets, refs = refs[:9], refs[9:11], refs[11:20], refs[20:]
    sums_all, tokens_all, normed_all, keys, values, member, tokens, normed, attention, hidden, context, sems = refs
    embed, pool_weight, key_weight, value_weight, query_weight, out_weight, up_weight, down_weight, return_weight = targets
    copies = fetch(sources, targets, sems)
    for copy in copies[:4]:
        copy.start()
    g, own_half = place[0], place[1]

    half_tokens = sums.shape[0] // bands
    band_tokens = 2 * half_tokens
    for band in range(bands):
        at = pl.ds(band * half_tokens, half_tokens)
        pair = sums[at].astype(F32), other_sums[at].astype(F32)
        for half in range(2):
            part = jnp.where(own_half == half, *pair).astype(BF16)
            sums_all[pl.ds(band * band_tokens + half * half_tokens, half_tokens)] = part
    member[...] = member_of(flags[...])
    copies[0].wait()
    copies[1].wait()
    for copy in copies[4:7]:
        copy.start()
    total = embed[...].astype(F32) + matmul(sums_all[...], pool_weight[...])
    tokens_all[...] = total
    normed_all[...] = rms_norm(total, attn_gain[...]).astype(BF16)

    own = pl.ds(pl.multiple_of(g * band_tokens, band_tokens), band_tokens)
    tokens[:band_tokens] = tokens_all[own]
    normed[:band_tokens] = normed_all[own]
    _, room, block_rows = layer_rooms(cols)
    side, span = room * block_rows, cols + 2 * HALF
    for number, (band, row) in enumerate(
        ((jnp.maximum(g - 1, 0), 0), (jnp.minimum(g + 1, bands - 1), flags.shape[0] // span - HALF))
    ):
        pick = jnp.concatenate([member[pl.ds((row + 2 * r) * span, room, stride=2)] for r in range(block_rows)])
        pick = pick.astype(BF16)
        at = pl.ds(pl.multiple_of(band * band_tokens, band_tokens), band_tokens)
        into = pl.ds(band_tokens + number * side, side)
        tokens[into] = select(pick, tokens_all[at])
        normed[into] = matmul(pick, normed_all[at]).astype(BF16)

    copies[2].wait()
    keys[...] = matmul(normed_all[...], key_weight[...]).astype(BF16)
    copies[3].wait()
    for copy in copies[7:]:
        copy.start()
    values[...] = matmul(normed_all[...], value_weight[...]).astype(BF16)
    copies[4].wait()
    queries = matmul(normed[...], query_weight[...]).astype(BF16)
    for head in range(HEADS):
        at = slice(head * HDIM, (head + 1) * HDIM)
        scores = matmul_nt(queries[:, at], keys[:, at]) * (1.0 / math.sqrt(HDIM))
        weights = jnp.exp(scores - jnp.max(scores, axis=-1, keepdims=True))
        denominator = jnp.sum(weights, axis=-1, keepdims=True)
        attention[:, at] = (matmul(weights.astype(BF16), values[:, at]) / denominator).astype(BF16)
    copies[5].wait()
    attended = tokens[...] + matmul(attention[...], out_weight[...])
    tokens[...] = attended
    normed[...] = rms_norm(attended, mlp_gain[...]).astype(BF16)
    copies[6].wait()
    part = 512
    for at in range(0, up_weight.shape[1], part):
        hidden[:, at : at + part] = jax.nn.gelu(matmul(normed[...], up_weight[:, at : at + part])).astype(BF16)
    copies[7].wait()
    context[...] = (tokens[...] + matmul(hidden[...], down_weight[...])).astype(BF16)
    context_out[...] = context[:band_tokens]
    copies[8].wait()
    returned_out[...] = matmul(context[...], return_weight[...])


def second_kernel(
    cols, exact, above, below, left, right, flags, returned, bit_weight, conv_hbm, gate_hbm, state_out,
    state, taps, bits, mask, conv, gate_weight, sems,
):
    copies = fetch((*thirds(conv_hbm), gate_hbm), (*thirds(conv), gate_weight), sems)
    for copy in copies:
        copy.start()
    patch = Patch(cols, state, taps, bits, mask)
    patch.fill((exact,), (above, below, left, right), patch.put)
    mask[...] = mask_of(flags[...])
    blocks, room, block_rows = layer_rooms(cols)
    side = room * block_rows
    band_tokens = returned.shape[0] - 2 * side
    first, last = patch.width * patch.span, (patch.rows - patch.width) * patch.span
    middle = pl.ds(first, last - first)
    member = member_of(flags[middle]).astype(BF16)
    patch.put(middle, patch.get(middle) + select(member, returned[:band_tokens]))
    for number, row in enumerate((0, patch.rows - patch.width)):
        for r in range(patch.width):
            start = band_tokens + number * side + r // 2 * room
            share = returned[start : start + blocks]
            for c in range(2):
                at = pl.ds((row + r) * patch.span + c, blocks, stride=2)
                patch.put(at, patch.get(at) + share)
    patch.begin()
    patch.advance(HALF, flags, conv, gate_weight, bit_weight, copies)
    for r in range(patch.rows - 2 * patch.width):
        state_out[r * cols : (r + 1) * cols] = patch.own(r).astype(BF16)


def local(
    syndrome_bits, region_assign, state_in, bit_to_candidate, bit_to_gate, conv_weight, gate_weight, gate_bias,
    pool_weight, region_embed, attn_norm_gain, query_weight, key_weight, value_weight, out_weight, mlp_norm_gain,
    mlp_up, mlp_down, return_weight,
):
    rows, cols, channels = state_in.shape
    band_tokens, embed_width = region_embed.shape
    bands, tiles = lax.axis_size("ctx"), math.prod(lax.axis_size(name) for name in TILE)
    conv = conv_weight.reshape(9 * channels, channels)
    place = jnp.stack([lax.axis_index("ctx"), lax.axis_index("core")]).astype(jnp.int32)
    swap = [(0, 1), (1, 0)]
    half = HALF * cols

    top, bottom, first, last = call(
        message_kernel,
        "message",
        (syndrome_bits.reshape(2 * ROUNDS, rows, cols), region_assign, state_in.reshape(rows * cols, channels)),
        patch_outputs(half, channels + LANES),
        grant=8,
    )
    above, below = row_halo(top, bottom)
    embed, _ = lax.optimization_barrier((region_embed, top))
    bit_weight, embed = call(
        prepare_kernel,
        "prepare",
        (bit_to_candidate, bit_to_gate, gate_bias[None], embed),
        [array(LANES, 2 * channels, BF16), array(bands * band_tokens, embed_width, BF16)],
        moved=8 * MIB,
    )
    embed, bit_weight, above, below, place = lax.optimization_barrier((embed, bit_weight, above, below, place))
    left, right = col_halo(cols, above, first, last, below)
    embed = lax.all_to_all(embed.reshape(bands, band_tokens, -1), "ctx", 0, 0).reshape(-1, embed_width)

    count = (rows + 2 * HALF) * (cols + 2 * HALF)
    flops = 15 * rows * cols * HALF * 2 * channels * channels
    exact, kept, given, flags, top, bottom, first, last = call(
        functools.partial(first_kernel, cols),
        "rounds",
        (place, top, bottom, above, below, left, right, region_assign, bit_weight, conv, gate_weight),
        [
            array(rows * cols, channels, F32), array(band_tokens // 2, channels, F32),
            array(band_tokens // 2, channels, BF16), array(count, LANES, BF16),
        ]
        + patch_outputs(half, channels),
        patch_scratch(rows, cols, channels)
        + [
            pltpu.VMEM((count, LANES), F32), pltpu.VMEM(conv.shape, BF16), pltpu.VMEM(gate_weight.shape, BF16),
            pltpu.SemaphoreType.DMA((4,)),
        ],
        in_hbm=(9, 10),
        scalars=(0,),
        flops=flops,
    )

    chips, half_tokens = tiles // 2, band_tokens // 2
    given, embed = lax.optimization_barrier((given, embed))
    received = lax.ppermute(given, "core", swap)
    (pieces,) = call(
        pair_kernel, "pair", (kept, received), [array(chips * half_tokens, channels, BF16)], grant=8
    )
    pieces = lax.all_to_all(pieces.reshape(chips, half_tokens, channels), "chip", 0, 0)
    left, right = shifted(last, TILE, 1), shifted(first, TILE, -1)
    up, down = call(
        rows_kernel,
        "rows",
        (top, bottom, left, right),
        [array(HALF * (cols + 2 * HALF), channels, BF16)] * 2,
        grant=8,
    )
    pieces, up, down = lax.optimization_barrier((pieces, up, down))
    (sums,) = call(
        functools.partial(band_kernel, chips),
        "band",
        (pieces.reshape(-1, channels),),
        [array(bands * half_tokens, channels, BF16)],
        grant=8,
    )
    up, down, sums = lax.optimization_barrier((up, down, sums))
    sums = lax.all_to_all(sums.reshape(bands, half_tokens, channels), "ctx", 0, 0)
    above, below = row_halo(up, down)
    sums, above = lax.optimization_barrier((sums.reshape(-1, channels), above))
    other_sums = lax.ppermute(sums, "core", swap)

    layer = (
        embed, pool_weight, key_weight, value_weight, query_weight, out_weight, mlp_up, mlp_down, return_weight,
    )
    _, room, block_rows = layer_rooms(cols)
    layer_rows = band_tokens + 2 * room * block_rows
    all_tokens = bands * band_tokens
    mlp = mlp_up.shape[1]
    context, returned = call(
        functools.partial(context_kernel, cols, bands),
        "context",
        (place, sums, other_sums, attn_norm_gain[None], mlp_norm_gain[None], flags, *layer),
        [array(band_tokens, embed_width, BF16), array(layer_rows, channels, F32)],
        [pltpu.VMEM(value.shape, value.dtype) for value in layer]
        + [
            pltpu.VMEM((all_tokens, channels), BF16),
            pltpu.VMEM((all_tokens, embed_width), F32), pltpu.VMEM((all_tokens, embed_width), BF16),
            pltpu.VMEM((all_tokens, embed_width), BF16), pltpu.VMEM((all_tokens, embed_width), BF16),
            pltpu.VMEM((count, LANES), F32),
            pltpu.VMEM((layer_rows, embed_width), F32), pltpu.VMEM((layer_rows, embed_width), BF16),
            pltpu.VMEM((layer_rows, embed_width), BF16), pltpu.VMEM((layer_rows, mlp), BF16),
            pltpu.VMEM((layer_rows, embed_width), BF16), pltpu.SemaphoreType.DMA((len(layer),)),
        ],
        in_hbm=range(6, 6 + len(layer)),
        scalars=(0,),
        flops=2 * embed_width * (all_tokens * (channels + 2 * embed_width) + layer_rows * (2 * embed_width + 2 * mlp)),
        moved=20 * MIB,
    )
    (state,) = call(
        functools.partial(second_kernel, cols),
        "rounds",
        (exact, above, below, left, right, flags, returned, bit_weight, conv, gate_weight),
        [array(rows * cols, channels, BF16)],
        patch_scratch(rows, cols, channels)
        + [pltpu.VMEM(conv.shape, BF16), pltpu.VMEM(gate_weight.shape, BF16), pltpu.SemaphoreType.DMA((4,))],
        in_hbm=(8, 9),
        flops=flops,
    )
    return (state.reshape(rows, cols, channels), context)


def solution(mesh):
    bands, tiles = mesh.devices.shape
    split = jax.sharding.Mesh(mesh.devices.reshape(bands, tiles // 2, 2), ("ctx", *TILE))
    return jax.shard_map(
        local,
        mesh=split,
        in_specs=(
            P(None, None, "ctx", TILE),
            P("ctx", TILE),
            P("ctx", TILE, None),
            P(), P(), P(), P(), P(), P(),
            P("ctx", None),
            P(), P(), P(), P(), P(), P(), P(), P(), P(),
        ),
        out_specs=(P("ctx", TILE, None), P("ctx", None)),
        check_vma=False,
    )
```
